32 devices in a mesh: dp: 16 (over z, y, core), rep: 2 (over x).
Axes of the slice: x: 2, y: 2, z: 4, core: 2. Of those that a mesh axis runs over, the one named last changes fastest.
Arguments:
- passages: bfloat16 [2, 128, 128, 768], P(None, ('dp', 'rep')), may hold values from -6 to 6
- lengths: int32 [2, 128], P(None, ('dp', 'rep')), may hold values from 20 to 128, as said below
- queries: bfloat16 [2, 128, 768], P(None, ('dp', 'rep')), may hold values from -12 to 12
- positives: int32 [2, 128], P(None, ('dp', 'rep')), may hold values from 0 to 127
- out_grad: bfloat16 [2, 128, 128, 768], P(None, ('dp', 'rep')), may hold values from -6 to 6
- w_query: bfloat16 [768, 768], P('dp'), may hold values from -0.21875 to 0.21875
- b_query: bfloat16 [768], P('dp'), may hold values from -3 to 3
- w_key: bfloat16 [768, 768], P('dp'), may hold values from -0.21875 to 0.21875
- w_value: bfloat16 [768, 768], P('dp'), may hold values from -0.21875 to 0.21875
- b_value: bfloat16 [768], P('dp'), may hold values from -3 to 3
- w_out: bfloat16 [768, 768], P('dp'), may hold values from -0.625 to 0.625
- b_out: bfloat16 [768], P('dp'), may hold values from -3 to 3
- norm1_gain: bfloat16 [768], P('dp'), may hold values from 0.5 to 1.5
- norm1_bias: bfloat16 [768], P('dp'), may hold values from -3 to 3
- w_up: bfloat16 [768, 3072], P('dp'), may hold values from -0.21875 to 0.21875
- b_up: bfloat16 [3072], P('dp'), may hold values from -3 to 3
- w_down: bfloat16 [3072, 768], P('dp'), may hold values from -0.109375 to 0.109375
- b_down: bfloat16 [768], P('dp'), may hold values from -3 to 3
- norm2_gain: bfloat16 [768], P('dp'), may hold values from 0.5 to 1.5
- norm2_bias: bfloat16 [768], P('dp'), may hold values from -3 to 3
Outputs:
- output: bfloat16 [2, 128, 128, 768], P(None, ('dp', 'rep'))
- query_loss: float32 [2, 128], P(None, ('dp', 'rep'))
- passages_grad: float32 [2, 128, 128, 768], P(None, ('dp', 'rep'))
- queries_grad: float32 [2, 128, 768], P(None, ('dp', 'rep'))
- passage_cls_grad: float32 [2, 128, 768], P(None, ('dp', 'rep'))
- grad_w_query: float32 [768, 768], P('dp')
- grad_b_query: float32 [768], P('dp')
- grad_w_key: float32 [768, 768], P('dp')
- grad_w_value: float32 [768, 768], P('dp')
- grad_b_value: float32 [768], P('dp')
- grad_w_out: float32 [768, 768], P('dp')
- grad_b_out: float32 [768], P('dp')
- grad_norm1_gain: float32 [768], P('dp')
- grad_norm1_bias: float32 [768], P('dp')
- grad_w_up: float32 [768, 3072], P('dp')
- grad_b_up: float32 [3072], P('dp')
- grad_w_down: float32 [3072, 768], P('dp')
- grad_b_down: float32 [768], P('dp')
- grad_norm2_gain: float32 [768], P('dp')
- grad_norm2_bias: float32 [768], P('dp')
The draws below stay inside these ranges and needn't reach their ends.
Inputs may be any that keep to these rules, and one draw needn't show every extreme that they name: `lengths`: in every micro-batch some passage has length 128 and some has 20.
All inputs are finite; a program needn't handle non-finite values.
Results may differ from the reference program's by a relative error of at most 0.014.
Values may be sent and summed in bfloat16 or wider, within the bound.
No kernel may reach another device: no remote copies, remote signals or barrier semaphores. Data moves between devices by JAX's collectives and lax.ppermute only.
A program may use at most 192 MiB of HBM per device.

```python
import math
import jax
import jax.numpy as jnp
from jax import lax

D = 768
H = 12
HD = 64
FF = 3072
LEN = 128
MINLEN = 20
MB = 2
PASSAGES = 128
QUERIES = 128


def draw_lengths(key, part):
    key = jax.random.fold_in(key, 11)
    key_vals, key_top, key_bottom = jax.random.split(key, 3)
    values = jax.random.randint(key_vals, (MB, PASSAGES), MINLEN, LEN + 1)
    top_place = jax.random.randint(key_top, (MB, 1), 0, PASSAGES)
    bottom_place = jax.random.randint(key_bottom, (MB, 1), 0, PASSAGES)
    columns = jnp.arange(PASSAGES)[None, :]
    values = jnp.where(columns == bottom_place, MINLEN, values)
    values = jnp.where(columns == top_place, LEN, values)
    return values.astype(jnp.int32)


def set_ends(drawn, stream_key, least, top_value):
    longest = drawn.shape.index(max(drawn.shape))
    spots = []
    for shift in (0, 1):
        where = [jax.random.randint(jax.random.fold_in(stream_key, axis), (), 0, length) for axis, length in enumerate(drawn.shape)]
        where[longest] = (where[longest] + shift) % drawn.shape[longest]
        spots.append(tuple(where))
    return drawn.at[spots[0]].set(least).at[spots[1]].set(top_value)


def shard_levels(rng, shape, pieces, least, top_value):
    factor_of = 1.0
    for axis_at, parts in pieces:
        steps = jax.random.uniform(jax.random.fold_in(jax.random.fold_in(rng, 6), axis_at), (parts,), jnp.float32, least / len(pieces), top_value / len(pieces))
        factor_of = factor_of * jnp.repeat(jnp.exp(steps), shape[axis_at] // parts).reshape((-1,) + (1,) * (len(shape) - 1 - axis_at))
    return factor_of


def normal_values(own_key, shape, deviation, reach, pieces=(), kind=jnp.bfloat16):
    array = deviation * jax.random.normal(own_key, shape, jnp.float32)
    if pieces:
        array = array * shard_levels(own_key, shape, pieces, -0.22, 0.18)
    return jnp.clip(array, -reach, reach).astype(kind)


def setup_inputs(seed: int = 0) -> dict:
    keys = jax.random.split(jax.random.key(seed), 21)
    return {
        "passages": normal_values(keys[0], (MB, PASSAGES, LEN, D), 1.0, 6.0, ((1, 32),)),
        "lengths": draw_lengths(jax.random.fold_in(keys[20], 71), 0),
        "queries": normal_values(keys[2], (MB, QUERIES, D), 2.0, 12.0, ((1, 32),)),
        "positives": set_ends(jax.random.randint(keys[3], (MB, QUERIES), 0, PASSAGES), jax.random.fold_in(keys[3], 1), 0, PASSAGES - 1).astype(jnp.int32),
        "out_grad": normal_values(keys[4], (MB, PASSAGES, LEN, D), 1.0, 6.0, ((1, 32),)),
        "w_query": normal_values(keys[5], (D, D), D ** -0.5, 0.21875, ((0, 16),)),
        "b_query": normal_values(keys[6], (D,), 0.5, 3.0, ((0, 16),)),
        "w_key": normal_values(keys[7], (D, D), D ** -0.5, 0.21875, ((0, 16),)),
        "w_value": normal_values(keys[8], (D, D), D ** -0.5, 0.21875, ((0, 16),)),
        "b_value": normal_values(keys[9], (D,), 0.5, 3.0, ((0, 16),)),
        "w_out": normal_values(keys[10], (D, D), (D // 8) ** -0.5, 0.625, ((0, 16),)),
        "b_out": normal_values(keys[11], (D,), 0.5, 3.0, ((0, 16),)),
        "norm1_gain": jnp.clip(1.0 + 0.1 * jax.random.normal(keys[12], (D,), jnp.float32), 0.5, 1.5).astype(jnp.bfloat16),
        "norm1_bias": normal_values(keys[13], (D,), 0.5, 3.0, ((0, 16),)),
        "w_up": normal_values(keys[14], (D, FF), D ** -0.5, 0.21875, ((0, 16),)),
        "b_up": normal_values(keys[15], (FF,), 0.5, 3.0, ((0, 16),)),
        "w_down": normal_values(keys[16], (FF, D), FF ** -0.5, 0.109375, ((0, 16),)),
        "b_down": normal_values(keys[17], (D,), 0.5, 3.0, ((0, 16),)),
        "norm2_gain": jnp.clip(1.0 + 0.1 * jax.random.normal(keys[18], (D,), jnp.float32), 0.5, 1.5).astype(jnp.bfloat16),
        "norm2_bias": normal_values(keys[19], (D,), 0.5, 3.0, ((0, 16),)),
    }


HIGH = lax.Precision.HIGHEST

@jax.custom_vjp
def low(v):
    return lax.optimization_barrier(v.astype(jnp.bfloat16)).astype(jnp.float32)

@jax.custom_vjp
def low_back(v):
    return v

def low_keep(v):
    return (low(v), None)

def low_pass(kept, grad):
    return (grad,)

def back_keep(v):
    return (v, None)

def back_low(kept, grad):
    return (low(grad),)
low.defvjp(low_keep, low_pass)
low_back.defvjp(back_keep, back_low)

def layer_norm(v, gain, bias):
    mean_val = lax.optimization_barrier(jnp.mean(v, axis=-1, keepdims=True))
    centred = v - mean_val
    variance = lax.optimization_barrier(jnp.mean(centred * centred, axis=-1, keepdims=True))
    return centred * lax.rsqrt(variance + 1e-05) * gain + bias

def gelu_exact(v):
    return jax.nn.gelu(v, approximate=False)

def matmul(left, right):
    return jnp.dot(left, right, precision=HIGH)

def passage_block(layer_params, block_vals, block_lengths):
    weight_query, bias_query, weight_key, weight_value, bias_value, weight_out, bias_out, gain_one, shift_one, weight_up, bias_up, weight_down, bias_down, gain_two, shift_two = layer_params
    group = block_vals.shape[0]
    token_rows = block_vals.reshape(group * LEN, D)
    head_shape = (group, LEN, H, HD)
    query_heads = low(low_back(matmul(token_rows, weight_query) + bias_query)).reshape(head_shape)
    key_heads = low(low_back(matmul(token_rows, weight_key))).reshape(head_shape)
    value_heads = low(low_back(matmul(token_rows, weight_value) + bias_value)).reshape(head_shape)
    raw_scores = jnp.einsum('plhe,pmhe->phlm', query_heads, key_heads, precision=HIGH) * (1.0 / math.sqrt(HD))
    key_valid = (jnp.arange(LEN)[None, :] < block_lengths[:, None])[:, None, None, :]
    scores = low_back(jnp.where(key_valid, raw_scores, -1000000000.0))
    attn_probs = jax.nn.softmax(scores, axis=-1)
    context = jnp.einsum('phlm,pmhe->plhe', low(attn_probs), value_heads, precision=HIGH)
    context = low(low_back(context)).reshape(group * LEN, D)
    branch_one = low_back(matmul(context, weight_out) + bias_out)
    hidden_one = layer_norm(token_rows + branch_one, gain_one, shift_one)
    hidden_pre = low_back(matmul(low(hidden_one), weight_up) + bias_up)
    branch_two = low_back(matmul(low(gelu_exact(hidden_pre)), weight_down) + bias_down)
    return layer_norm(hidden_one + branch_two, gain_two, shift_two).reshape(group, LEN, D)

def reference(passages, lengths, queries, positives, out_grad, w_query, b_query, w_key, w_value, b_value, w_out, b_out, norm1_gain, norm1_bias, w_up, b_up, w_down, b_down, norm2_gain, norm2_bias):
    layer_params = tuple((t.astype(jnp.float32) for t in (w_query, b_query, w_key, w_value, b_value, w_out, b_out, norm1_gain, norm1_bias, w_up, b_up, w_down, b_down, norm2_gain, norm2_bias)))
    passage_vals = passages.astype(jnp.float32)
    query_vals = queries.astype(jnp.float32)
    cls_zero = jnp.zeros((MB, PASSAGES, D), jnp.float32)
    block_fn = jax.checkpoint(passage_block)

    def forward(params_in, passages_in, queries_in, cls_shift):
        outputs = []
        losses = []
        for micro_step in range(MB):
            blocks = passages_in[micro_step].reshape(PASSAGES // 32, 32, LEN, D)
            block_lens = lengths[micro_step].reshape(PASSAGES // 32, 32)
            result = lax.map(lambda item: block_fn(params_in, item[0], item[1]), (blocks, block_lens))
            result = result.reshape(PASSAGES, LEN, D)
            cls_vals = low(result[:, 0, :]) + cls_shift[micro_step]
            logits = matmul(queries_in[micro_step], cls_vals.T) * (1.0 / math.sqrt(D))
            log_total = jax.nn.logsumexp(logits, axis=-1)
            picked = jnp.take_along_axis(logits, positives[micro_step][:, None].astype(jnp.int32), axis=1)[:, 0]
            outputs.append(result)
            losses.append(log_total - picked)
        return (jnp.stack(outputs), jnp.stack(losses))
    (output_all, loss_all), pull = jax.vjp(forward, layer_params, passage_vals, query_vals, cls_zero)
    param_grads, passages_grad, queries_grad, cls_grad_all = pull((out_grad.astype(jnp.float32), jnp.ones_like(loss_all)))
    grad_w_query, grad_b_query, grad_w_key, grad_w_value, grad_b_value, grad_w_out, grad_b_out, grad_gain_one, grad_shift_one, grad_w_up, grad_b_up, grad_w_down, grad_b_down, grad_gain_two, grad_shift_two = param_grads
    return (output_all.astype(jnp.bfloat16), loss_all, passages_grad, queries_grad, cls_grad_all, grad_w_query, grad_b_query, grad_w_key, grad_w_value, grad_b_value, grad_w_out, grad_b_out, grad_gain_one, grad_shift_one, grad_w_up, grad_b_up, grad_w_down, grad_b_down, grad_gain_two, grad_shift_two)
```

```python
import functools
import math

import jax
import jax.numpy as jnp
from jax import lax
from jax.sharding import PartitionSpec as P

H = 12
F32 = jnp.float32
BF16 = jnp.bfloat16
INV_SQRT2 = 1.0 / math.sqrt(2.0)
INV_SQRT_2PI = 1.0 / math.sqrt(2.0 * math.pi)


class Grid:
    def __init__(self, dp, rep):
        self.dp, self.rep = dp, rep
        self.core = 2 if dp % 2 == 0 else 1
        rest = dp // self.core
        self.z = 4 if rest % 4 == 0 else 1
        self.y = rest // self.z
        self.stride = {"core": 1, "y": self.core, "z": self.core * self.y}
        self.size = {"core": self.core, "y": self.y, "z": self.z, "rep": rep}

    def positions(self):
        dp_index = lax.axis_index("dp")
        pos = {
            name: (dp_index // self.stride[name]) % self.size[name] for name in ("core", "y", "z")
        }
        pos["rep"] = lax.axis_index("rep")
        return pos

    def shift(self, name, by):
        if name == "rep":
            return [(i, i + by) for i in range(self.rep) if 0 <= i + by < self.rep]
        step, size = self.stride[name], self.size[name]
        return [
            (i, i + by * step) for i in range(self.dp) if 0 <= (i // step) % size + by < size
        ]

    def flip(self, name):
        return self.shift(name, 1) + self.shift(name, -1)

    def permute(self, value, name, pairs):
        return lax.ppermute(value, "rep" if name == "rep" else "dp", pairs)


def gather_remote(grid, pos, value, name):
    size = grid.size[name]
    if size == 2:
        return grid.permute(value, name, grid.flip(name))[None]
    ups, downs = [], []
    up = down = value
    for _ in range(size - 1):
        up = grid.permute(up, name, grid.shift(name, 1))
        down = grid.permute(down, name, grid.shift(name, -1))
        ups.append(up)
        downs.append(down)
    line = jnp.stack(ups[::-1] + downs)
    return lax.dynamic_slice_in_dim(line, size - 1 - pos[name], size - 1, axis=0)


def insert(own, remote, place):
    count = remote.shape[0] + 1
    rows = []
    for j in range(count):
        if j == 0:
            rows.append(jnp.where(place == 0, own, remote[0]))
        elif j == count - 1:
            rows.append(jnp.where(place == j, own, remote[j - 1]))
        else:
            rows.append(
                jnp.where(place == j, own, jnp.where(place < j, remote[j - 1], remote[j]))
            )
    return jnp.stack(rows)


def gather_axis(grid, pos, value, name):
    if grid.size[name] == 1:
        return value[None]
    return insert(value, gather_remote(grid, pos, value, name), pos[name])


def gather_weight(grid, pos, shard):
    rows, cols = shard.shape
    split = grid.rep == 2 and grid.z > 1 and grid.y == 2
    if not split:
        part = gather_axis(grid, pos, shard, "z")
        part = jnp.moveaxis(gather_axis(grid, pos, part, "y"), 0, 1)
    else:
        half = cols // 2
        mine = lax.dynamic_slice_in_dim(shard, pos["rep"] * half, half, axis=1)
        far = gather_remote(grid, pos, mine, "z")
        near = gather_axis(grid, pos, shard, "y")
        far = jnp.moveaxis(gather_axis(grid, pos, far, "y"), 0, 1)
        other = grid.permute(far, "rep", grid.flip("rep"))
        low = jnp.where(pos["rep"] == 0, far, other)
        high = jnp.where(pos["rep"] == 0, other, far)
        part = insert(near, jnp.concatenate([low, high], axis=-1), pos["z"])
    whole = gather_axis(grid, pos, part, "core")
    return jnp.moveaxis(whole, 0, 2).reshape(grid.dp * rows, cols)


def gather_small(grid, pos, value, names):
    for name in names:
        size = grid.size[name]
        if size & (size - 1) or size == 1:
            if size > 1:
                value = gather_axis(grid, pos, value, name).reshape((-1,) + value.shape[1:])
            continue
        bit = 1
        while bit < size:
            step = bit if name == "rep" else bit * grid.stride[name]
            count = grid.rep if name == "rep" else grid.dp
            other = grid.permute(value, name, [(i, i ^ step) for i in range(count)])
            upper = (pos[name] & bit) > 0
            value = jnp.concatenate(
                [jnp.where(upper, other, value), jnp.where(upper, value, other)], axis=0
            )
            bit *= 2
    return value


def scatter_axis(grid, pos, value, name, kind):
    size = grid.size[name]
    here = pos[name]
    if size == 1:
        return value[0].astype(F32)
    own = lax.dynamic_index_in_dim(value, here, 0, keepdims=False).astype(F32)
    if size == 2:
        out = lax.dynamic_index_in_dim(value, 1 - here, 0, keepdims=False)
        return own + grid.permute(out.astype(kind), name, grid.flip(name)).astype(F32)
    total = own
    for sign in (1, -1):
        arrived = None
        for step in range(1, size):
            target = jnp.clip(here + sign * (size - step), 0, size - 1)
            out = lax.dynamic_index_in_dim(value, target, 0, keepdims=False)
            if arrived is not None:
                out = out.astype(F32) + arrived.astype(F32)
            arrived = grid.permute(out.astype(kind), name, grid.shift(name, sign))
        total = total + arrived.astype(F32)
    return total


def scatter_weight(grid, pos, grad, kind=BF16):
    rows = grad.shape[0] // grid.dp
    cols = grad.shape[1]
    value = grad.astype(kind).reshape(grid.z, grid.y, grid.core, rows, cols)
    value = scatter_axis(grid, pos, jnp.moveaxis(value, 2, 0), "core", kind).astype(kind)
    if grid.rep == 2:
        half = cols // 2
        mine = lax.dynamic_slice_in_dim(value, pos["rep"] * half, half, axis=3)
        theirs = lax.dynamic_slice_in_dim(value, (1 - pos["rep"]) * half, half, axis=3)
        value = mine.astype(F32) + grid.permute(theirs, "rep", grid.flip("rep")).astype(F32)
        value = value.astype(kind)
    value = scatter_axis(grid, pos, jnp.moveaxis(value, 1, 0), "y", kind).astype(kind)
    value = scatter_axis(grid, pos, value, "z", kind)
    if grid.rep == 2:
        value = value.astype(kind)
        other = grid.permute(value, "rep", grid.flip("rep"))
        first = pos["rep"] == 0
        value = jnp.concatenate(
            [jnp.where(first, value, other), jnp.where(first, other, value)], axis=1
        ).astype(F32)
    elif grid.rep > 1:
        value = lax.psum(value, "rep")
    return value


def scatter_small(grid, pos, value):
    shape = value.shape[1:]
    value = value.reshape((grid.z, grid.y, grid.core) + shape)
    value = scatter_axis(grid, pos, jnp.moveaxis(value, 2, 0), "core", F32)
    value = scatter_axis(grid, pos, jnp.moveaxis(value, 1, 0), "y", F32)
    value = scatter_axis(grid, pos, value, "z", F32)
    if grid.rep == 2:
        value = value + grid.permute(value, "rep", grid.flip("rep"))
    elif grid.rep > 1:
        value = lax.psum(value, "rep")
    return value


def mm(left, right):
    return jnp.dot(left, right, preferred_element_type=F32)


def mm_left(left, right):
    return lax.dot_general(left, right, (((0,), (0,)), ((), ())), preferred_element_type=F32)


def mm_back(left, right):
    return lax.dot_general(left, right, (((1,), (1,)), ((), ())), preferred_element_type=F32)


def row_total(values):
    return jnp.sum(values.astype(F32), axis=0)


def norm_parts(v):
    mean_val = jnp.mean(v, axis=-1, keepdims=True)
    centred = v - mean_val
    variance = jnp.mean(centred * centred, axis=-1, keepdims=True)
    scale = lax.rsqrt(variance + 1e-05)
    return centred * scale, scale


def norm_back(grad, unit, scale, gain):
    inner = grad * gain
    mean_one = jnp.mean(inner, axis=-1, keepdims=True)
    mean_two = jnp.mean(inner * unit, axis=-1, keepdims=True)
    return (inner - mean_one - unit * mean_two) * scale


def per_device(
    grid,
    passages,
    lengths,
    queries,
    positives,
    out_grad,
    w_query,
    b_query,
    w_key,
    w_value,
    b_value,
    w_out,
    b_out,
    norm1_gain,
    norm1_bias,
    w_up,
    b_up,
    w_down,
    b_down,
    norm2_gain,
    norm2_bias,
):
    steps, count, length, width = passages.shape
    head = width // H
    total = steps * count
    rows = total * length
    heads = (total, length, H, head)
    score_scale = 1.0 / math.sqrt(head)
    inv_width = 1.0 / math.sqrt(width)
    pos = grid.positions()
    dp = grid.dp

    vectors = (b_query, b_value, b_out, norm1_gain, norm1_bias, b_down, norm2_gain, norm2_bias, b_up)
    small = gather_small(grid, pos, jnp.concatenate(vectors)[None], ("core", "y", "z"))
    spans, at = [], 0
    for vec in vectors:
        spans.append(small[:, at : at + vec.shape[0]].reshape(-1).astype(F32))
        at += vec.shape[0]
    (bias_q, bias_v, bias_out, gain_one, shift_one, bias_down, gain_two, shift_two, bias_up) = spans

    qkv = gather_weight(grid, pos, jnp.concatenate([w_query, w_key, w_value], axis=1))
    weight_q, weight_k, weight_v = qkv[:, :width], qkv[:, width : 2 * width], qkv[:, 2 * width :]
    weight_out = gather_weight(grid, pos, w_out)
    weight_up = gather_weight(grid, pos, w_up)
    weight_down = gather_weight(grid, pos, w_down)
    all_queries = gather_small(
        grid, pos, jnp.moveaxis(queries, 0, 1), ("rep", "core", "y", "z")
    )

    tokens = passages.reshape(rows, width)
    key_valid = (jnp.arange(length)[None, :] < lengths.reshape(total)[:, None])[:, None, None, :]
    q = (mm(tokens, weight_q) + bias_q).astype(BF16).reshape(heads)
    k = mm(tokens, weight_k).astype(BF16).reshape(heads)
    v = (mm(tokens, weight_v) + bias_v).astype(BF16).reshape(heads)

    def scores_of():
        raw = jnp.einsum("plhe,pmhe->phlm", q, k, preferred_element_type=F32) * score_scale
        return jnp.where(key_valid, raw, -1000000000.0)

    scores = scores_of()
    log_total = jax.nn.logsumexp(scores, axis=-1, keepdims=True)
    probs_low = jnp.exp(scores - log_total).astype(BF16)
    context = jnp.einsum("phlm,pmhe->plhe", probs_low, v, preferred_element_type=F32)
    context = context.astype(BF16).reshape(rows, width)
    sum_one = tokens.astype(F32) + mm(context, weight_out) + bias_out
    unit_one, scale_one = norm_parts(sum_one)
    hidden = unit_one * gain_one + shift_one
    hidden_low = hidden.astype(BF16)
    pre = mm(hidden_low, weight_up) + bias_up
    phi = 0.5 * lax.erfc(-pre * INV_SQRT2)
    gelu_low = (pre * phi).astype(BF16)
    slope = (phi + pre * (jnp.exp(-0.5 * pre * pre) * INV_SQRT_2PI)).astype(BF16)
    sum_two = hidden + mm(gelu_low, weight_down) + bias_down
    unit_two, scale_two = norm_parts(sum_two)
    result = (unit_two * gain_two + shift_two).reshape(steps, count, length, width)
    output = result.astype(BF16)

    all_cls = gather_small(
        grid, pos, jnp.moveaxis(output[:, :, 0, :], 0, 1), ("rep", "core", "y", "z")
    )
    first = (pos["z"] * grid.stride["z"] + pos["y"] * grid.stride["y"] + pos["core"]) * grid.rep
    first = (first + pos["rep"]) * count
    logits = jnp.einsum("qmd,pmd->mqp", all_queries, all_cls, preferred_element_type=F32)
    logits = logits * inv_width
    query_total = jax.nn.logsumexp(logits, axis=-1)
    passages_all = all_cls.shape[0]
    mine = lax.dynamic_slice_in_dim(logits, first, count, axis=1)
    mine_total = lax.dynamic_slice_in_dim(query_total, first, count, axis=1)
    onehot = (positives[:, :, None] == jnp.arange(passages_all)[None, None, :]).astype(F32)
    query_loss = mine_total - jnp.sum(mine * onehot, axis=-1)
    mine_grad = (jnp.exp(mine - mine_total[:, :, None]) - onehot) * inv_width
    queries_grad = jnp.einsum(
        "mqp,pmd->mqd", mine_grad.astype(BF16), all_cls, preferred_element_type=F32
    )
    all_positives = gather_small(
        grid, pos, jnp.moveaxis(positives, 0, 1), ("rep", "core", "y", "z")
    )
    column = lax.dynamic_slice_in_dim(logits, first, count, axis=2)
    hit = (all_positives.T[:, :, None] == (first + jnp.arange(count))[None, None, :]).astype(F32)
    column_grad = (jnp.exp(column - query_total[:, :, None]) - hit) * inv_width
    cls_grad = jnp.einsum(
        "mqp,qmd->mpd", column_grad.astype(BF16), all_queries, preferred_element_type=F32
    )

    grad_out = out_grad.astype(F32).at[:, :, 0, :].add(cls_grad).reshape(rows, width)
    grad_gain_two = jnp.sum(grad_out * unit_two, axis=0)
    grad_shift_two = jnp.sum(grad_out, axis=0)
    grad_two = norm_back(grad_out, unit_two, scale_two, gain_two)
    down_low = grad_two.astype(BF16)
    grad_b_down = row_total(down_low)
    shard_w_down = scatter_weight(grid, pos, mm_left(gelu_low, down_low))
    up_low = (mm_back(down_low, weight_down) * slope.astype(F32)).astype(BF16)
    grad_b_up = row_total(up_low)
    shard_w_up = scatter_weight(grid, pos, mm_left(hidden_low, up_low))
    grad_hidden = grad_two + mm_back(up_low, weight_up)
    grad_gain_one = jnp.sum(grad_hidden * unit_one, axis=0)
    grad_shift_one = jnp.sum(grad_hidden, axis=0)
    grad_one = norm_back(grad_hidden, unit_one, scale_one, gain_one)
    attn_low = grad_one.astype(BF16)
    grad_b_out = row_total(attn_low)
    shard_w_out = scatter_weight(grid, pos, mm_left(context, attn_low))
    context_grad = mm_back(attn_low, weight_out).astype(BF16).reshape(heads)
    attn_probs = jnp.exp(scores_of() - log_total)
    probs_grad = jnp.einsum("plhe,pmhe->phlm", context_grad, v, preferred_element_type=F32)
    inner = jnp.sum(probs_grad * attn_probs, axis=-1, keepdims=True)
    score_low = (attn_probs * (probs_grad - inner)).astype(BF16)
    q_low = jnp.einsum("phlm,pmhe->plhe", score_low, k, preferred_element_type=F32) * score_scale
    q_low = q_low.astype(BF16).reshape(rows, width)
    k_low = jnp.einsum("phlm,plhe->pmhe", score_low, q, preferred_element_type=F32) * score_scale
    k_low = k_low.astype(BF16).reshape(rows, width)
    v_low = jnp.einsum("phlm,plhe->pmhe", probs_low, context_grad, preferred_element_type=F32)
    v_low = v_low.astype(BF16).reshape(rows, width)
    shard_w_query = scatter_weight(grid, pos, mm_left(tokens, q_low))
    shard_w_key = scatter_weight(grid, pos, mm_left(tokens, k_low))
    shard_w_value = scatter_weight(grid, pos, mm_left(tokens, v_low))
    grad_b_query = row_total(q_low)
    grad_b_value = row_total(v_low)
    input_grad = (
        grad_one + mm_back(q_low, weight_q) + mm_back(k_low, weight_k) + mm_back(v_low, weight_v)
    )

    grads = (
        grad_b_query,
        grad_b_value,
        grad_b_out,
        grad_gain_one,
        grad_shift_one,
        grad_b_down,
        grad_gain_two,
        grad_shift_two,
        grad_b_up,
    )
    sums = scatter_small(
        grid, pos, jnp.concatenate([g.reshape(dp, -1) for g in grads], axis=1)
    )
    parts, at = [], 0
    for vec in vectors:
        parts.append(sums[at : at + vec.shape[0]])
        at += vec.shape[0]
    (s_b_q, s_b_v, s_b_out, s_gain1, s_shift1, s_b_down, s_gain2, s_shift2, s_b_up) = parts
    return (
        output,
        query_loss,
        input_grad.reshape(steps, count, length, width),
        queries_grad,
        cls_grad,
        shard_w_query,
        s_b_q,
        shard_w_key,
        shard_w_value,
        s_b_v,
        shard_w_out,
        s_b_out,
        s_gain1,
        s_shift1,
        shard_w_up,
        s_b_up,
        shard_w_down,
        s_b_down,
        s_gain2,
        s_shift2,
    )


def solution(mesh):
    both = ("dp", "rep")
    matrix, vector = P("dp", None), P("dp")
    weights = (
        matrix, vector, matrix, matrix, vector, matrix, vector, vector, vector,
        matrix, vector, matrix, vector, vector, vector,
    )
    grid = Grid(mesh.shape["dp"], mesh.shape["rep"])
    wide = P(None, both, None, None)
    return jax.shard_map(
        functools.partial(per_device, grid),
        mesh=mesh,
        in_specs=(wide, P(None, both), P(None, both, None), P(None, both), wide) + weights,
        out_specs=(wide, P(None, both), wide, P(None, both, None), P(None, both, None)) + weights,
        check_vma=False,
    )
```

```python
import functools
import math

import jax
import jax.numpy as jnp
from jax import lax
from jax.experimental import pallas as pl
from jax.experimental.pallas import tpu as pltpu
from jax.sharding import PartitionSpec as P

H = 12
F32 = jnp.float32
BF16 = jnp.bfloat16
INV_SQRT2 = 1.0 / math.sqrt(2.0)
INV_SQRT_2PI = 1.0 / math.sqrt(2.0 * math.pi)


ANY = pl.BlockSpec(memory_space=pl.ANY)
SMEM = pl.BlockSpec(memory_space=pltpu.SMEM)
VMEM = pl.BlockSpec(memory_space=pltpu.VMEM)
MIB = 2**20
LANES = 128


class Grid:
    def __init__(self, dp, rep, rows):
        self.dp, self.rep = dp, rep
        self.fast = dp == 16 and rep == 2 and rows % 16 == 0
        self.bits = {"core": 1, "y": 2, "z1": 4, "z2": 8}

    def flip(self, value, name):
        if name == "x":
            return lax.ppermute(value, "rep", [(i, i ^ 1) for i in range(self.rep)])
        bit = self.bits[name]
        return lax.ppermute(value, "dp", [(i, i ^ bit) for i in range(self.dp)])


def run_copies(copies):
    for copy in copies:
        copy.start()
    for copy in copies:
        copy.wait()


def place_of(here_ref, key, rows):
    core, y, z, half = key
    row = pl.multiple_of((here_ref[0] ^ (z * 4 + y * 2 + core)) * rows, 16)
    return pl.ds(row, rows), here_ref[1] ^ half


def join_kernel(here_ref, *refs, keys, widths, extra):
    count = len(keys)
    pieces, outs, sems = refs[:count], refs[count:-1], refs[-1]
    copies = []
    for piece, names in zip(pieces, keys):
        for i, key in enumerate(names):
            rows = piece.shape[1]
            where, half = place_of(here_ref, key, rows)
            at = 0
            for out, width in zip(outs, widths):
                column = pl.ds(pl.multiple_of(half * width, LANES), width)
                copies.append((piece.at[i, :, pl.ds(at, width)], out.at[where, column]))
                at += width
            if extra and key[3] == 0:
                copies.append((piece.at[i, :, pl.ds(at, extra)], outs[-1].at[where, :]))
    run_copies([pltpu.make_async_copy(a, b, sems.at[i]) for i, (a, b) in enumerate(copies)])


def join(bag, widths, extra, here):
    arrays, keys = zip(*bag)
    rows = arrays[0].shape[1]
    shapes = [(16 * rows, 2 * width) for width in widths] + ([(16 * rows, extra)] if extra else [])
    copies = 32 * len(widths) + (16 if extra else 0)
    size = sum(a * b for a, b in shapes)
    return pl.pallas_call(
        functools.partial(join_kernel, keys=keys, widths=widths, extra=extra),
        out_shape=[jax.ShapeDtypeStruct(shape, arrays[0].dtype) for shape in shapes],
        in_specs=[SMEM] + [ANY] * len(arrays),
        out_specs=[VMEM] * len(shapes),
        scratch_shapes=[pltpu.SemaphoreType.DMA((copies,))],
        compiler_params=pltpu.CompilerParams(vmem_limit_bytes=32 * MIB),
        cost_estimate=pl.CostEstimate(flops=0, bytes_accessed=4 * size, transcendentals=0),
        name="join",
    )(here, *arrays)


def split_kernel(here_ref, value_ref, *refs, keys):
    *pieces, sems = refs
    copies = []
    for piece, names in zip(pieces, keys):
        _, rows, width = piece.shape
        for i, key in enumerate(names):
            where, half = place_of(here_ref, key, rows)
            column = pl.ds(pl.multiple_of(half * width, LANES), width)
            copies.append((value_ref.at[where, column], piece.at[i]))
    run_copies([pltpu.make_async_copy(a, b, sems.at[i]) for i, (a, b) in enumerate(copies)])


def split(value, keys, here):
    rows, width = value.shape[0] // 16, value.shape[1] // 2
    return pl.pallas_call(
        functools.partial(split_kernel, keys=keys),
        out_shape=[jax.ShapeDtypeStruct((len(names), rows, width), value.dtype) for names in keys],
        in_specs=[SMEM, VMEM],
        out_specs=[ANY] * len(keys),
        scratch_shapes=[pltpu.SemaphoreType.DMA((32,))],
        compiler_params=pltpu.CompilerParams(vmem_limit_bytes=32 * MIB),
        cost_estimate=pl.CostEstimate(flops=0, bytes_accessed=4 * value.size, transcendentals=0),
        name="split",
    )(here, value)


def halves_of(parts, extra, x):
    out = []
    for place in (x, 1 - x):
        row = [
            lax.dynamic_slice_in_dim(p, place * (p.shape[1] // 2), p.shape[1] // 2, axis=1)
            for p in parts
        ]
        out.append(jnp.concatenate(row + ([extra] if extra is not None else []), axis=1))
    return out


def with_cores(grid, bag):
    return bag + [(grid.flip(a, "core"), [(1,) + k[1:] for k in keys]) for a, keys in bag]


def gather_first(grid, here, parts, extra):
    mine, twin = halves_of(parts, extra, here[1])
    own = jnp.stack([mine, twin])
    h0 = mine[None]
    across = grid.flip(own, "y")
    h1 = grid.flip(h0, "z1")
    h2 = grid.flip(h0, "z2")
    line = jnp.concatenate([h1, h2])
    h3 = grid.flip(h1, "z2")
    line_y = grid.flip(line, "y")
    line_x = grid.flip(line, "x")
    back_y = grid.flip(jnp.concatenate([h3, line_x[:1]]), "y")
    back_x = grid.flip(jnp.concatenate([h3, line_y[1:]]), "x")
    last = grid.flip(back_y[:1], "x")
    bag = [
        (own, [(0, 0, 0, 0), (0, 0, 0, 1)]),
        (across, [(0, 1, 0, 0), (0, 1, 0, 1)]),
        (line, [(0, 0, 1, 0), (0, 0, 2, 0)]),
        (line_y, [(0, 1, 1, 0), (0, 1, 2, 0)]),
        (line_x, [(0, 0, 1, 1), (0, 0, 2, 1)]),
        (h3, [(0, 0, 3, 0)]),
        (back_y, [(0, 1, 3, 0), (0, 1, 1, 1)]),
        (back_x, [(0, 0, 3, 1), (0, 1, 2, 1)]),
        (last, [(0, 1, 3, 1)]),
    ]
    widths = [p.shape[1] // 2 for p in parts]
    return join(with_cores(grid, bag), widths, extra.shape[1], here)


def gather_later(grid, here, parts):
    mine = halves_of(parts, None, here[1])[0][None]
    low = jnp.concatenate([mine, grid.flip(mine, "z1")])
    line = jnp.concatenate([low, grid.flip(low, "z2")])
    line_y = grid.flip(line, "y")
    line_x = grid.flip(line, "x")
    cross_x = grid.flip(line_y[:2], "x")
    cross_y = grid.flip(line_x[2:], "y")
    bag = [
        (line, [(0, 0, z, 0) for z in range(4)]),
        (line_y, [(0, 1, z, 0) for z in range(4)]),
        (line_x, [(0, 0, z, 1) for z in range(4)]),
        (cross_x, [(0, 1, z, 1) for z in range(2)]),
        (cross_y, [(0, 1, z, 1) for z in range(2, 4)]),
    ]
    return join(with_cores(grid, bag), [p.shape[1] // 2 for p in parts], 0, here)


def gather_small(grid, value):
    if not grid.fast:
        return lax.all_gather(value, ("dp", "rep"), axis=0, tiled=True)
    for name in ("x", "core", "y", "z1", "z2"):
        other = grid.flip(value, name)
        if name == "x":
            upper = lax.axis_index("rep") > 0
        else:
            upper = (lax.axis_index("dp") & grid.bits[name]) > 0
        value = jnp.concatenate(
            [jnp.where(upper, other, value), jnp.where(upper, value, other)], axis=0
        )
    return value


def added(kind, *terms):
    total = terms[0].astype(F32)
    for term in terms[1:]:
        total = total + term.astype(F32)
    return total.astype(kind)


def scatter_weight(grid, here, grad):
    if not grid.fast:
        part = lax.psum_scatter(grad.astype(F32), "dp", scatter_dimension=0, tiled=True)
        return lax.psum(part, "rep")
    low, high = (0, 1), (2, 3)
    names = [(1, 1, low), (1, 1, high), (0, 1, low), (0, 1, high), (1, 0, low), (1, 0, high)]
    names = names + [(0, 0, low + high)]
    keys = [[(c, y, z, h) for z in zs] for c in range(2) for y, h, zs in names]
    pieces = split(grad.astype(BF16), keys, here)
    count = len(names)
    far = [grid.flip(p, "core") for p in pieces[count:]]
    (cross_low, cross_high, x_low, x_high, y_low, y_high, own) = list(zip(pieces, far))
    got_y_low = grid.flip(added(BF16, *cross_low), "x")
    got_x_high = grid.flip(added(BF16, *cross_high), "y")
    to_x = jnp.concatenate([added(BF16, *x_low), added(BF16, *x_high, got_x_high)])
    to_y = jnp.concatenate([added(BF16, *y_low, got_y_low), added(BF16, *y_high)])
    value = added(BF16, *own, grid.flip(to_x, "x"), grid.flip(to_y, "y"))
    value = added(BF16, value[:2], grid.flip(value[2:], "z2"))
    value = added(BF16, value[0], grid.flip(value[1], "z1"))
    other = grid.flip(value, "x")
    first = here[1] == 0
    return jnp.concatenate(
        [jnp.where(first, value, other), jnp.where(first, other, value)], axis=1
    ).astype(F32)


def scatter_small(grid, value, mine):
    if not grid.fast:
        return mine(lax.psum(value, ("dp", "rep")))
    for name in ("x", "core", "y", "z1", "z2"):
        value = value + grid.flip(value, name)
    return mine(value)


def mm(left, right):
    return jnp.dot(left, right, preferred_element_type=F32)


def mm_left(left, right):
    return lax.dot_general(left, right, (((0,), (0,)), ((), ())), preferred_element_type=F32)


def mm_back(left, right):
    return lax.dot_general(left, right, (((1,), (1,)), ((), ())), preferred_element_type=F32)


def row_total(values):
    return jnp.sum(values.astype(F32), axis=0)


def normal_parts(v):
    phi = 0.5 + 0.5 * lax.erf(v * INV_SQRT2)
    return phi, jnp.exp(-0.5 * v * v) * INV_SQRT_2PI


def norm_parts(v):
    mean_val = jnp.mean(v, axis=-1, keepdims=True)
    centred = v - mean_val
    variance = jnp.mean(centred * centred, axis=-1, keepdims=True)
    scale = lax.rsqrt(variance + 1e-05)
    return centred * scale, scale


def norm_back(grad, unit, scale, gain):
    inner = grad * gain
    mean_one = jnp.mean(inner, axis=-1, keepdims=True)
    mean_two = jnp.mean(inner * unit, axis=-1, keepdims=True)
    return (inner - mean_one - unit * mean_two) * scale


def per_device(
    grid,
    passages,
    lengths,
    queries,
    positives,
    out_grad,
    w_query,
    b_query,
    w_key,
    w_value,
    b_value,
    w_out,
    b_out,
    norm1_gain,
    norm1_bias,
    w_up,
    b_up,
    w_down,
    b_down,
    norm2_gain,
    norm2_bias,
):
    steps, count, length, width = passages.shape
    head = width // H
    total = steps * count
    rows = total * length
    heads = (total, length, H, head)
    score_scale = 1.0 / math.sqrt(head)
    inv_width = 1.0 / math.sqrt(width)
    dp = grid.dp
    dp_index, rep_index = lax.axis_index("dp"), lax.axis_index("rep")
    here = jnp.stack([dp_index, rep_index]).astype(jnp.int32)

    block = w_query.shape[0]
    vectors = (b_query, b_value, b_out, norm1_gain, norm1_bias, b_down, norm2_gain, norm2_bias)
    spread = b_up.shape[0] // block
    columns = [v[:, None] for v in vectors] + [b_up.reshape(spread, block).T]
    columns = jnp.concatenate(columns, axis=1)
    columns = jnp.pad(columns, ((0, 0), (0, LANES - columns.shape[1])))
    if grid.fast:
        weight_q, weight_k, weight_v, table = gather_first(
            grid, here, (w_query, w_key, w_value), columns
        )
        weight_out, weight_up = gather_later(grid, here, (w_out, w_up))
        (weight_down,) = gather_later(grid, here, (w_down,))
    else:
        weight_q, weight_k, weight_v, table, weight_out, weight_up, weight_down = [
            lax.all_gather(w, "dp", axis=0, tiled=True)
            for w in (w_query, w_key, w_value, columns, w_out, w_up, w_down)
        ]
    table = table[:, :16].T.astype(F32)
    (bias_q, bias_v, bias_out, gain_one, shift_one, bias_down, gain_two, shift_two) = [
        table[i] for i in range(8)
    ]
    bias_up = jnp.transpose(
        table[8 : 8 + spread].reshape(spread, dp, block), (1, 0, 2)
    ).reshape(-1)
    digits = jnp.stack([positives.T // 256, positives.T % 256], axis=-1).astype(BF16)
    payload = jnp.concatenate(
        [
            jnp.moveaxis(queries, 0, 1),
            jnp.pad(digits, ((0, 0), (0, 0), (0, LANES - 2))),
        ],
        axis=-1,
    )
    payload = gather_small(grid, payload)
    all_queries = payload[:, :, :width]
    digits = payload[:, :, width : width + 2].astype(jnp.int32)
    all_positives = digits[:, :, 0] * 256 + digits[:, :, 1]

    tokens = passages.reshape(rows, width)
    key_valid = (jnp.arange(length)[None, :] < lengths.reshape(total)[:, None])[:, None, None, :]
    q = (mm(tokens, weight_q) + bias_q).astype(BF16).reshape(heads)
    k = mm(tokens, weight_k).astype(BF16).reshape(heads)
    v = (mm(tokens, weight_v) + bias_v).astype(BF16).reshape(heads)

    def scores_of():
        raw = jnp.einsum("plhe,pmhe->phlm", q, k, preferred_element_type=F32) * score_scale
        return jnp.where(key_valid, raw, -1000000000.0)

    scores = scores_of()
    log_total = jax.nn.logsumexp(scores, axis=-1, keepdims=True)
    probs_low = jnp.exp(scores - log_total).astype(BF16)
    context = jnp.einsum("phlm,pmhe->plhe", probs_low, v, preferred_element_type=F32)
    context = context.astype(BF16).reshape(rows, width)
    sum_one = tokens.astype(F32) + mm(context, weight_out) + bias_out
    unit_one, scale_one = norm_parts(sum_one)
    hidden = unit_one * gain_one + shift_one
    hidden_low = hidden.astype(BF16)
    pre = mm(hidden_low, weight_up) + bias_up
    phi, density = normal_parts(pre)
    gelu_low = (pre * phi).astype(BF16)
    slope = (phi + pre * density).astype(BF16)
    sum_two = hidden + mm(gelu_low, weight_down) + bias_down
    unit_two, scale_two = norm_parts(sum_two)
    result = (unit_two * gain_two + shift_two).reshape(steps, count, length, width)
    output = result.astype(BF16)

    all_cls = gather_small(grid, jnp.moveaxis(output[:, :, 0, :], 0, 1))
    first = (dp_index * grid.rep + rep_index) * count
    logits = jnp.einsum("qmd,pmd->mqp", all_queries, all_cls, preferred_element_type=F32)
    logits = logits * inv_width
    query_total = jax.nn.logsumexp(logits, axis=-1)
    passages_all = all_cls.shape[0]
    mine = lax.dynamic_slice_in_dim(logits, first, count, axis=1)
    mine_total = lax.dynamic_slice_in_dim(query_total, first, count, axis=1)
    onehot = (positives[:, :, None] == jnp.arange(passages_all)[None, None, :]).astype(F32)
    query_loss = mine_total - jnp.sum(mine * onehot, axis=-1)
    mine_grad = (jnp.exp(mine - mine_total[:, :, None]) - onehot) * inv_width
    queries_grad = jnp.einsum(
        "mqp,pmd->mqd", mine_grad.astype(BF16), all_cls, preferred_element_type=F32
    )
    column = lax.dynamic_slice_in_dim(logits, first, count, axis=2)
    hit = (all_positives.T[:, :, None] == (first + jnp.arange(count))[None, None, :]).astype(F32)
    column_grad = (jnp.exp(column - query_total[:, :, None]) - hit) * inv_width
    cls_grad = jnp.einsum(
        "mqp,qmd->mpd", column_grad.astype(BF16), all_queries, preferred_element_type=F32
    )

    grad_out = out_grad.astype(F32).at[:, :, 0, :].add(cls_grad).reshape(rows, width)
    grad_gain_two = jnp.sum(grad_out * unit_two, axis=0)
    grad_shift_two = jnp.sum(grad_out, axis=0)
    grad_two = norm_back(grad_out, unit_two, scale_two, gain_two)
    down_low = grad_two.astype(BF16)
    grad_b_down = row_total(down_low)
    shard_w_down = scatter_weight(grid, here, mm_left(gelu_low, down_low))
    up_low = (mm_back(down_low, weight_down) * slope.astype(F32)).astype(BF16)
    grad_b_up = row_total(up_low)
    shard_w_up = scatter_weight(grid, here, mm_left(hidden_low, up_low))
    grad_hidden = grad_two + mm_back(up_low, weight_up)
    grad_gain_one = jnp.sum(grad_hidden * unit_one, axis=0)
    grad_shift_one = jnp.sum(grad_hidden, axis=0)
    grad_one = norm_back(grad_hidden, unit_one, scale_one, gain_one)
    attn_low = grad_one.astype(BF16)
    grad_b_out = row_total(attn_low)
    shard_w_out = scatter_weight(grid, here, mm_left(context, attn_low))
    context_grad = mm_back(attn_low, weight_out).astype(BF16).reshape(heads)
    attn_probs = jnp.exp(scores_of() - log_total)
    probs_grad = jnp.einsum("plhe,pmhe->phlm", context_grad, v, preferred_element_type=F32)
    inner = jnp.sum(probs_grad * attn_probs, axis=-1, keepdims=True)
    score_low = (attn_probs * (probs_grad - inner)).astype(BF16)
    q_low = jnp.einsum("phlm,pmhe->plhe", score_low, k, preferred_element_type=F32) * score_scale
    q_low = q_low.astype(BF16).reshape(rows, width)
    k_low = jnp.einsum("phlm,plhe->pmhe", score_low, q, preferred_element_type=F32) * score_scale
    k_low = k_low.astype(BF16).reshape(rows, width)
    v_low = jnp.einsum("phlm,plhe->pmhe", probs_low, context_grad, preferred_element_type=F32)
    v_low = v_low.astype(BF16).reshape(rows, width)
    shard_w_query = scatter_weight(grid, here, mm_left(tokens, q_low))
    shard_w_key = scatter_weight(grid, here, mm_left(tokens, k_low))
    shard_w_value = scatter_weight(grid, here, mm_left(tokens, v_low))
    grad_b_query = row_total(q_low)
    grad_b_value = row_total(v_low)
    input_grad = (
        grad_one + mm_back(q_low, weight_q) + mm_back(k_low, weight_k) + mm_back(v_low, weight_v)
    )

    grads = (
        grad_b_query,
        grad_b_value,
        grad_b_out,
        grad_gain_one,
        grad_shift_one,
        grad_b_down,
        grad_gain_two,
        grad_shift_two,
    )
    grads = jnp.concatenate([jnp.stack(grads), grad_b_up.reshape(spread, width)])

    def mine_of(sums):
        low = lax.dynamic_slice_in_dim(sums[:8], dp_index * block, block, axis=1)
        return low, lax.dynamic_slice_in_dim(
            sums[8:].reshape(-1), dp_index * spread * block, spread * block, axis=0
        )

    low, s_b_up = scatter_small(grid, grads, mine_of)
    (s_b_q, s_b_v, s_b_out, s_gain1, s_shift1, s_b_down, s_gain2, s_shift2) = [
        low[i] for i in range(8)
    ]
    return (
        output,
        query_loss,
        input_grad.reshape(steps, count, length, width),
        queries_grad,
        cls_grad,
        shard_w_query,
        s_b_q,
        shard_w_key,
        shard_w_value,
        s_b_v,
        shard_w_out,
        s_b_out,
        s_gain1,
        s_shift1,
        shard_w_up,
        s_b_up,
        shard_w_down,
        s_b_down,
        s_gain2,
        s_shift2,
    )


def solution(mesh):
    both = ("dp", "rep")
    matrix, vector = P("dp", None), P("dp")
    weights = (
        matrix, vector, matrix, matrix, vector, matrix, vector, vector, vector,
        matrix, vector, matrix, vector, vector, vector,
    )
    grid = Grid(mesh.shape["dp"], mesh.shape["rep"], 768 // mesh.shape["dp"])
    wide = P(None, both, None, None)
    return jax.shard_map(
        functools.partial(per_device, grid),
        mesh=mesh,
        in_specs=(wide, P(None, both), P(None, both, None), P(None, both), wide) + weights,
        out_specs=(wide, P(None, both), wide, P(None, both, None), P(None, both, None)) + weights,
        check_vma=False,
    )
```

```python
import functools
import math

import jax
import jax.numpy as jnp
from jax import lax
from jax.experimental import pallas as pl
from jax.experimental.pallas import tpu as pltpu
from jax.sharding import PartitionSpec as P

H = 12
F32 = jnp.float32
BF16 = jnp.bfloat16
INV_SQRT2 = 1.0 / math.sqrt(2.0)
INV_SQRT_2PI = 1.0 / math.sqrt(2.0 * math.pi)


ANY = pl.BlockSpec(memory_space=pl.ANY)
SMEM = pl.BlockSpec(memory_space=pltpu.SMEM)
VMEM = pl.BlockSpec(memory_space=pltpu.VMEM)
MIB = 2**20
LANES = 128


class Grid:
    def __init__(self, dp, rep, rows):
        self.dp, self.rep = dp, rep
        self.fast = dp == 16 and rep == 2 and rows % 16 == 0
        self.bits = {"core": 1, "y": 2, "z1": 4, "z2": 8}

    def flip(self, value, name):
        if name == "x":
            return lax.ppermute(value, "rep", [(i, i ^ 1) for i in range(self.rep)])
        bit = self.bits[name]
        return lax.ppermute(value, "dp", [(i, i ^ bit) for i in range(self.dp)])


def run_copies(copies):
    for copy in copies:
        copy.start()
    for copy in copies:
        copy.wait()


def place_of(here_ref, key, rows):
    core, y, z, half = key
    row = pl.multiple_of((here_ref[0] ^ (z * 4 + y * 2 + core)) * rows, 16)
    return pl.ds(row, rows), here_ref[1] ^ half


def join_kernel(here_ref, *refs, keys, widths, extra):
    count = len(keys)
    pieces, outs, sems = refs[:count], refs[count:-1], refs[-1]
    copies = []
    for piece, names in zip(pieces, keys):
        for i, key in enumerate(names):
            rows = piece.shape[1]
            where, half = place_of(here_ref, key, rows)
            at = 0
            for out, width in zip(outs, widths):
                column = pl.ds(pl.multiple_of(half * width, LANES), width)
                copies.append((piece.at[i, :, pl.ds(at, width)], out.at[where, column]))
                at += width
            if extra and key[3] == 0:
                copies.append((piece.at[i, :, pl.ds(at, extra)], outs[-1].at[where, :]))
    run_copies([pltpu.make_async_copy(a, b, sems.at[i]) for i, (a, b) in enumerate(copies)])


def join(bag, widths, extra, here):
    arrays, keys = zip(*bag)
    rows = arrays[0].shape[1]
    shapes = [(16 * rows, 2 * width) for width in widths] + ([(16 * rows, extra)] if extra else [])
    copies = 32 * len(widths) + (16 if extra else 0)
    size = sum(a * b for a, b in shapes)
    return pl.pallas_call(
        functools.partial(join_kernel, keys=keys, widths=widths, extra=extra),
        out_shape=[jax.ShapeDtypeStruct(shape, arrays[0].dtype) for shape in shapes],
        in_specs=[SMEM] + [ANY] * len(arrays),
        out_specs=[VMEM] * len(shapes),
        scratch_shapes=[pltpu.SemaphoreType.DMA((copies,))],
        compiler_params=pltpu.CompilerParams(vmem_limit_bytes=2 * MIB),
        cost_estimate=pl.CostEstimate(flops=0, bytes_accessed=4 * size, transcendentals=0),
        name="join",
    )(here, *arrays)


def split_kernel(here_ref, *refs, keys, count):
    values, pieces, sems = refs[:count], refs[count:-1], refs[-1]
    copies = []
    for piece, names in zip(pieces, keys):
        rows = piece.shape[1]
        for i, key in enumerate(names):
            where, half = place_of(here_ref, key, rows)
            at = 0
            for value in values:
                width = value.shape[1] // 2
                column = pl.ds(pl.multiple_of(half * width, LANES), width)
                copies.append((value.at[where, column], piece.at[i, :, pl.ds(at, width)]))
                at += width
    run_copies([pltpu.make_async_copy(a, b, sems.at[i]) for i, (a, b) in enumerate(copies)])


def split(values, keys, here):
    rows, width = values[0].shape[0] // 16, sum(v.shape[1] for v in values) // 2
    kind = values[0].dtype
    size = sum(v.size for v in values)
    return pl.pallas_call(
        functools.partial(split_kernel, keys=keys, count=len(values)),
        out_shape=[jax.ShapeDtypeStruct((len(names), rows, width), kind) for names in keys],
        in_specs=[SMEM] + [VMEM] * len(values),
        out_specs=[ANY] * len(keys),
        scratch_shapes=[pltpu.SemaphoreType.DMA((32 * len(values),))],
        compiler_params=pltpu.CompilerParams(vmem_limit_bytes=2 * MIB),
        cost_estimate=pl.CostEstimate(flops=0, bytes_accessed=4 * size, transcendentals=0),
        name="split",
    )(here, *values)


def order_kernel(*refs):
    refs[-1][0, 0] = 0.0


def after(grid, *trees):
    if not grid.fast:
        return 0.0
    leaves = jax.tree.leaves(trees)
    return pl.pallas_call(
        order_kernel,
        out_shape=jax.ShapeDtypeStruct((1, 1), F32),
        in_specs=[ANY] * len(leaves),
        out_specs=SMEM,
        compiler_params=pltpu.CompilerParams(vmem_limit_bytes=MIB // 4),
        name="order",
    )(*leaves).reshape(())


def halves_of(parts, extra, x):
    out = []
    for place in (x, 1 - x):
        row = [
            lax.dynamic_slice_in_dim(p, place * (p.shape[1] // 2), p.shape[1] // 2, axis=1)
            for p in parts
        ]
        out.append(jnp.concatenate(row + ([extra] if extra is not None else []), axis=1))
    return out


def core_keys(keys):
    return [(1,) + key[1:] for key in keys]


class Spread:
    def __init__(self, grid, value):
        self.grid, self.value, self.held = grid, value, []
        self.names = ["x", "core", "y", "z1", "z2"]
        self.other = None
        if not grid.fast:
            self.value = lax.all_gather(value, ("dp", "rep"), axis=0, tiled=True)
            self.names = []

    def absorb(self, order=0.0):
        if self.other is None:
            return
        name = self.names.pop(0)
        if name == "x":
            upper = lax.axis_index("rep") > 0
        else:
            upper = (lax.axis_index("dp") & self.grid.bits[name]) > 0
        low = jnp.where(upper, self.other, self.value)
        high = jnp.where(upper, self.value, self.other)
        self.value, self.other = jnp.concatenate([low, high], axis=0), None
        self.value = plus(self.value, order)

    def step(self, order=0.0):
        self.absorb(order)
        if self.names:
            self.other = self.grid.flip(self.value, self.names[0])
            self.held = [self.other]


class Total:
    def __init__(self, grid, value):
        self.grid, self.parts, self.held = grid, [value], []
        self.names = ["x", "core", "y", "z1", "z2"]
        if not grid.fast:
            self.parts, self.names = [lax.psum(value, ("dp", "rep"))], []

    def step(self, order=0.0):
        value = sum(self.parts[1:], self.parts[0])
        self.parts = [plus(value, order)]
        if self.names:
            self.parts.append(self.grid.flip(self.parts[0], self.names.pop(0)))
        self.held = self.parts[1:]

    def finish(self):
        while self.names:
            self.step()
        return sum(self.parts[1:], self.parts[0])


def plus(value, order):
    return value if isinstance(order, float) else (value.astype(F32) + order).astype(value.dtype)


def sums_kernel(order_ref, *refs, plan, count):
    zero = order_ref[0, 0]
    for out_ref, terms in zip(refs[count:], plan):
        at = 0
        for size, parts in terms:
            for i in range(size):
                total = zero
                for source, first in parts:
                    total = total + refs[source][first + i].astype(F32)
                out_ref[at + i] = total.astype(out_ref.dtype)
            at += size


def sums(order, arrays, plan):
    shapes = [(sum(size for size, _ in terms),) + arrays[0].shape[1:] for terms in plan]
    size = sum(a * b * c for a, b, c in shapes)
    return pl.pallas_call(
        functools.partial(sums_kernel, plan=plan, count=len(arrays)),
        out_shape=[jax.ShapeDtypeStruct(shape, BF16) for shape in shapes],
        in_specs=[SMEM] + [VMEM] * len(arrays),
        out_specs=[VMEM] * len(shapes),
        compiler_params=pltpu.CompilerParams(vmem_limit_bytes=8 * MIB),
        cost_estimate=pl.CostEstimate(flops=2 * size, bytes_accessed=6 * size, transcendentals=0),
        name="sums",
    )(jnp.full((1, 1), order, F32), *arrays)


class Scatter:
    def __init__(self, grid, here):
        self.grid, self.here, self.stage, self.held, self.sent = grid, here, 0, [], []

    def start(self, grads):
        self.widths = [g.shape[1] for g in grads]
        if not self.grid.fast:
            parts = [
                lax.psum_scatter(g.astype(F32), "dp", scatter_dimension=0, tiled=True)
                for g in grads
            ]
            self.result = [lax.psum(p, "rep") for p in parts]
            return
        keys = [
            [(c, y, z, h) for y, h in ((1, 1), (0, 1), (1, 0), (0, 0)) for z in range(4)]
            for c in range(2)
        ]
        self.near, self.far = split(grads, keys, self.here)
        self.held = [self.far]

    def step(self, order=0.0):
        if not self.grid.fast:
            return
        flip = self.grid.flip
        self.stage += 1
        if self.stage == 1:
            self.held = [flip(self.far, "core")]
        elif self.stage == 2:
            plan = [[(n, [(0, at), (1, at)])] for n, at in ((2, 0), (2, 2), (4, 4), (4, 8), (4, 12))]
            low, high, self.x, self.y, self.own = sums(order, [self.near, *self.held], plan)
            self.sent, self.held = [low, high], [flip(low, "x"), flip(high, "y")]
        elif self.stage == 3:
            plan = [[(2, [(0, 0)]), (2, [(0, 2), (3, 0)])], [(2, [(1, 0), (2, 0)]), (2, [(1, 2)])]]
            to_x, to_y = sums(order, [self.x, self.y, *self.held], plan)
            self.sent, self.held = [to_x, to_y], [flip(to_x, "x"), flip(to_y, "y")]
        elif self.stage == 4:
            plan = [[(2, [(0, at), (1, at), (2, at)])] for at in (0, 2)]
            self.low, high = sums(order, [self.own, *self.held], plan)
            self.sent, self.held = [high], [flip(high, "z2")]
        elif self.stage == 5:
            plan = [[(1, [(0, at), (1, at)])] for at in (0, 1)]
            self.low, high = sums(order, [self.low, *self.held], plan)
            self.sent, self.held = [high], [flip(high, "z1")]
        elif self.stage == 6:
            (self.low,) = sums(order, [self.low, *self.held], [[(1, [(0, 0), (1, 0)])]])
            self.sent, self.held = [self.low], [flip(self.low, "x")]

    def finish(self):
        if not self.grid.fast:
            return self.result
        while self.stage < 6:
            self.step()
        value, other = self.low[0], self.held[0][0]
        first = self.here[1] == 0
        left, right = jnp.where(first, value, other), jnp.where(first, other, value)
        out, at = [], 0
        for width in self.widths:
            cut = slice(at, at + width // 2)
            out.append(jnp.concatenate([left[:, cut], right[:, cut]], axis=1).astype(F32))
            at += width // 2
        return out


def mm(left, right):
    return jnp.dot(left, right, preferred_element_type=F32)


def mm_left(left, right):
    return lax.dot_general(left, right, (((0,), (0,)), ((), ())), preferred_element_type=F32)


def mm_back(left, right):
    return lax.dot_general(left, right, (((1,), (1,)), ((), ())), preferred_element_type=F32)


def row_total(values):
    return mm(jnp.ones((8, values.shape[0]), BF16), values)[0]


def normal_parts(v):
    phi = 0.5 + 0.5 * lax.erf(v * INV_SQRT2)
    return phi, jnp.exp(-0.5 * v * v) * INV_SQRT_2PI


def norm_parts(v):
    mean_val = jnp.mean(v, axis=-1, keepdims=True)
    centred = v - mean_val
    variance = jnp.mean(centred * centred, axis=-1, keepdims=True)
    scale = lax.rsqrt(variance + 1e-05)
    return centred * scale, scale


def norm_back(grad, unit, scale, gain):
    inner = grad * gain
    mean_one = jnp.mean(inner, axis=-1, keepdims=True)
    mean_two = jnp.mean(inner * unit, axis=-1, keepdims=True)
    return (inner - mean_one - unit * mean_two) * scale


def two_heads(t, first):
    zero = jnp.zeros_like(t)
    return jnp.concatenate([jnp.where(first, t, zero), jnp.where(first, zero, t)], axis=0)

def attn_kernel(len_ref, q_ref, k_ref, v_ref, *refs, scale, n, pairs, many):
    c_ref, total_ref = refs[-2:]
    lane = lax.broadcasted_iota(jnp.int32, (1, 2 * n), 1) % n
    first = lax.broadcasted_iota(jnp.int32, (n, LANES), 1) < LANES // 2
    spot = lax.broadcasted_iota(jnp.int32, (n, LANES), 1)
    for i in range(many):
        rows = slice(i * n, (i + 1) * n)
        length = len_ref[pl.program_id(0) * many + i]
        totals = jnp.zeros((n, LANES), F32)
        for pair in range(pairs):
            at = slice(pair * LANES, (pair + 1) * LANES)
            q = q_ref[rows, at] * scale
            s = mm_back(q, two_heads(k_ref[rows, at], first))
            s = jnp.where(lane < length, s, -1000000000.0)
            parts = []
            for h in range(2):
                part = s[:, h * n : (h + 1) * n]
                top = jnp.max(part, axis=-1, keepdims=True)
                part = jnp.exp(part - top)
                total = jnp.sum(part, axis=-1, keepdims=True)
                parts.append((part * (1.0 / total)).astype(BF16))
                totals = jnp.where(spot == 2 * pair + h, top + jnp.log(total), totals)
            p = jnp.concatenate(parts, axis=1)
            c_ref[rows, at] = mm(p, two_heads(v_ref[rows, at], first)).astype(BF16)
        total_ref[i] = totals.T[: total_ref.shape[1]]

def attention(q, k, v, lengths, deps, n, heads):
    rows, width = q.shape
    count, many = rows // n, 2
    scale = 1.0 / math.sqrt(width // heads)
    block = pl.BlockSpec((n * many, width), lambda i: (i, 0))
    lines = 16
    return pl.pallas_call(
        functools.partial(attn_kernel, scale=scale, n=n, pairs=heads // 2, many=many),
        grid=(count // many,),
        in_specs=[SMEM, block, block, block] + [ANY] * len(deps),
        out_specs=[block, pl.BlockSpec((many, lines, n), lambda i: (i, 0, 0))],
        out_shape=[jax.ShapeDtypeStruct((rows, width), BF16), jax.ShapeDtypeStruct((count, lines, n), F32)],
        compiler_params=pltpu.CompilerParams(vmem_limit_bytes=16 * MIB),
        cost_estimate=pl.CostEstimate(flops=8 * rows * n * width, bytes_accessed=8 * rows * width, transcendentals=rows * n * heads),
        name="attention",
    )(lengths, q, k, v, *deps)

def attn_back_kernel(len_ref, total_ref, q_ref, k_ref, v_ref, d_ref, *refs, scale, n, pairs, many):
    dq_ref, dk_ref, dv_ref = refs[-3:]
    row = lax.broadcasted_iota(jnp.int32, (2 * n, n), 0) % n
    first = lax.broadcasted_iota(jnp.int32, (n, LANES), 1) < LANES // 2
    for i in range(many):
        rows = slice(i * n, (i + 1) * n)
        length = len_ref[pl.program_id(0) * many + i]
        valid = row < length
        for pair in range(pairs):
            at = slice(pair * LANES, (pair + 1) * LANES)
            q, k, v, d = q_ref[rows, at] * scale, k_ref[rows, at] * scale, v_ref[rows, at], d_ref[rows, at]
            kk = two_heads(k_ref[rows, at], first)
            s = jnp.where(valid, mm_back(kk, q), -1000000000.0)
            dp = mm_back(two_heads(v, first), d)
            ps, ds = [], []
            for h in range(2):
                part = slice(h * n, (h + 1) * n)
                p = jnp.exp(s[part] - total_ref[i, 2 * pair + h : 2 * pair + h + 1, :])
                t = p * dp[part]
                ds.append((t - p * jnp.sum(t, axis=0, keepdims=True)).astype(BF16))
                ps.append(p.astype(BF16))
            dv_ref[rows, at] = mm(jnp.concatenate(ps, axis=1), two_heads(d, first)).astype(BF16)
            dk_ref[rows, at] = mm(jnp.concatenate(ds, axis=1), two_heads(q, first)).astype(BF16)
            dq_ref[rows, at] = mm_left(jnp.concatenate(ds, axis=0), two_heads(k, first)).astype(BF16)

def attention_back(q, k, v, d, totals, lengths, deps, n, heads):
    rows, width = q.shape
    count, many = rows // n, 2
    scale = 1.0 / math.sqrt(width // heads)
    block = pl.BlockSpec((n * many, width), lambda i: (i, 0))
    shape = jax.ShapeDtypeStruct((rows, width), BF16)
    return pl.pallas_call(
        functools.partial(attn_back_kernel, scale=scale, n=n, pairs=heads // 2, many=many),
        grid=(count // many,),
        in_specs=[SMEM, pl.BlockSpec((many,) + totals.shape[1:], lambda i: (i, 0, 0))] + [block] * 4 + [ANY] * len(deps),
        out_specs=[block] * 3,
        out_shape=[shape] * 3,
        compiler_params=pltpu.CompilerParams(vmem_limit_bytes=16 * MIB),
        cost_estimate=pl.CostEstimate(flops=20 * rows * n * width, bytes_accessed=14 * rows * width, transcendentals=rows * n * heads),
        name="attention_back",
    )(lengths, totals, q, k, v, d, *deps)


def per_device(
    grid,
    passages,
    lengths,
    queries,
    positives,
    out_grad,
    w_query,
    b_query,
    w_key,
    w_value,
    b_value,
    w_out,
    b_out,
    norm1_gain,
    norm1_bias,
    w_up,
    b_up,
    w_down,
    b_down,
    norm2_gain,
    norm2_bias,
):
    steps, count, length, width = passages.shape
    total = steps * count
    rows = total * length
    inv_width = 1.0 / math.sqrt(width)
    dp = grid.dp
    dp_index, rep_index = lax.axis_index("dp"), lax.axis_index("rep")
    here = jnp.stack([dp_index, rep_index]).astype(jnp.int32)

    block = w_query.shape[0]
    vectors = (b_query, b_value, b_out, norm1_gain, norm1_bias, b_down, norm2_gain, norm2_bias)
    spread = b_up.shape[0] // block
    columns = [v[:, None] for v in vectors] + [b_up.reshape(spread, block).T]
    columns = jnp.concatenate(columns, axis=1)
    columns = jnp.pad(columns, ((0, 0), (0, LANES - columns.shape[1])))
    tokens = passages.reshape(rows, width)
    digits = jnp.stack([positives.T // 256, positives.T % 256], axis=-1).astype(BF16)
    payload = Spread(
        grid,
        jnp.concatenate(
            [
                jnp.moveaxis(queries, 0, 1).reshape(total, width),
                jnp.pad(digits.reshape(total, 2), ((0, 0), (0, LANES - 2))),
            ],
            axis=-1,
        ),
    )
    weight_down = lax.all_gather(w_down, "dp", axis=0, tiled=True)
    spans = lengths.reshape(total)
    if grid.fast:
        flip = grid.flip
        mine, twin = halves_of((w_query, w_key, w_value), columns, here[1])
        own, mine = jnp.stack([mine, twin]), mine[None]
        second = halves_of((w_out, w_up), None, here[1])[0][None]
        across, h1, h2 = flip(own, "y"), flip(mine, "z1"), flip(mine, "z2")
        s1 = flip(second, "z1")
        order = after(grid, across, h1, h2)
        line = plus(jnp.concatenate([h1, h2]), order)
        h3, line_y, line_x = flip(h1, "z2"), flip(line, "y"), flip(line, "x")
        own_c, across_c = flip(own, "core"), flip(across, "core")
        second = plus(jnp.concatenate([second, s1]), order)
        second_far = flip(second, "z2")
        order = after(grid, h3, line_y, line_x, second)
        back_y = flip(plus(jnp.concatenate([h3, line_x[:1]]), order), "y")
        back_x = flip(plus(jnp.concatenate([h3, line_y[1:]]), order), "x")
        cores = [flip(v, "core") for v in (line, h3, line_y, line_x)]
        order = after(grid, back_y, back_x)
        end = flip(plus(back_y[:1], order), "x")
        cores = [own_c, across_c] + cores + [flip(v, "core") for v in (back_y, back_x)]
        cores.append(flip(end, "core"))
        bag = [
            (own, [(0, 0, 0, 0), (0, 0, 0, 1)]),
            (across, [(0, 1, 0, 0), (0, 1, 0, 1)]),
            (line, [(0, 0, 1, 0), (0, 0, 2, 0)]),
            (h3, [(0, 0, 3, 0)]),
            (line_y, [(0, 1, 1, 0), (0, 1, 2, 0)]),
            (line_x, [(0, 0, 1, 1), (0, 0, 2, 1)]),
            (back_y, [(0, 1, 3, 0), (0, 1, 1, 1)]),
            (back_x, [(0, 0, 3, 1), (0, 1, 2, 1)]),
            (end, [(0, 1, 3, 1)]),
        ]
        bag += [(v, core_keys(keys)) for v, (_, keys) in zip(cores, bag)]
        weight_q, weight_k, weight_v, table = join(bag, [width // 2] * 3, LANES, here)
        order = after(grid, table)
        second = plus(jnp.concatenate([second, second_far]), order)
        second_y, second_x = flip(second, "y"), flip(second, "x")
        payload.step(order)
        order = after(grid, second)
    else:
        weight_q, weight_k, weight_v, table, weight_out, weight_up = [
            lax.all_gather(w, "dp", axis=0, tiled=True)
            for w in (w_query, w_key, w_value, columns, w_out, w_up)
        ]
        order = 0.0
    table = table[:, :16].T.astype(F32)
    (bias_q, bias_v, bias_out, gain_one, shift_one, bias_down, gain_two, shift_two) = [
        table[i] for i in range(8)
    ]
    bias_up = jnp.transpose(
        table[8 : 8 + spread].reshape(spread, dp, block), (1, 0, 2)
    ).reshape(-1)
    q = plus(mm(tokens, weight_q) + bias_q, order).astype(BF16)
    k = plus(mm(tokens, weight_k), order).astype(BF16)
    v = plus(mm(tokens, weight_v) + bias_v, order).astype(BF16)
    context, log_total = attention(q, k, v, spans, [], length, H)
    z_keys = [[(0, y, z, h) for z in range(4)] for y, h in ((0, 0), (1, 0), (0, 1), (1, 1))]

    def cross(order, line, line_y, line_x):
        low, high = flip(plus(line_y[:2], order), "x"), flip(plus(line_x[2:], order), "y")
        cores = [flip(v, "core") for v in (line, line_y, line_x, low, high)]
        keys = z_keys[:3] + [z_keys[3][:2], z_keys[3][2:]]
        bag = list(zip((line, line_y, line_x, low, high), keys))
        return bag + [(v, core_keys(names)) for v, (_, names) in zip(cores, bag)]

    if grid.fast:
        order = after(grid, context, second_y, second_x, payload.held)
        bag = cross(order, second, second_y, second_x)
        payload.step(order)
        weight_out, weight_up = join(bag, [width // 2, w_up.shape[1] // 2], 0, here)
        order = after(grid, weight_out, payload.held)
        payload.step(order)
    sum_one = tokens.astype(F32) + mm(context, weight_out) + bias_out
    unit_one, scale_one = norm_parts(sum_one)
    hidden = unit_one * gain_one + shift_one
    hidden_low = hidden.astype(BF16)
    pre = mm(hidden_low, weight_up) + bias_up
    phi, density = normal_parts(pre)
    gelu_low = (pre * phi).astype(BF16)
    slope = (phi + pre * density).astype(BF16)
    order = after(grid, gelu_low, payload.held) if grid.fast else 0.0
    payload.step(order)
    sum_two = plus(hidden, order) + mm(gelu_low, weight_down) + bias_down
    unit_two, scale_two = norm_parts(sum_two)
    result = (unit_two * gain_two + shift_two).reshape(steps, count, length, width)
    output = result.astype(BF16)

    def starts(value):
        return value.reshape(total, length, -1)[:, 0]

    def put_starts(value, part):
        blocks = value.reshape(total, length, -1)
        return lax.dynamic_update_slice(blocks, part[:, None], (0, 0, 0)).reshape(value.shape)

    cls = Spread(grid, jnp.moveaxis(output[:, :, 0, :], 0, 1).reshape(total, width))
    cls.step()
    payload.step(after(grid, output, payload.held) if grid.fast else 0.0)
    grad_out = out_grad.reshape(rows, width).astype(F32)
    grad_two = norm_back(grad_out, unit_two, scale_two, gain_two)
    down_low = grad_two.astype(BF16)
    later = (jnp.arange(rows) % length > 0)[:, None]
    grad_gain_two = jnp.sum(grad_out * unit_two, axis=0)
    grad_shift_two = jnp.sum(grad_out, axis=0)
    grad_b_down = jnp.sum(jnp.where(later, down_low.astype(F32), 0.0), axis=0)
    order = after(grid, down_low, cls.held)
    cls.step(order)
    cls.step()
    parts = [slice(0, w_up.shape[1] // 2), slice(w_up.shape[1] // 2, w_up.shape[1])]

    def up_back(grad, part, by):
        return mm_back(grad, weight_down[part]) * by[:, part].astype(F32)

    up_lows = [plus(up_back(down_low, parts[0], slope), order).astype(BF16)]
    order = after(grid, up_lows[0], cls.held)
    cls.step(order)
    up_lows.append(plus(up_back(down_low, parts[1], slope), order).astype(BF16))
    order = after(grid, up_lows[1], cls.held)
    cls.step(order)
    cls.absorb()

    payload.absorb()
    all_cls = cls.value.reshape(-1, steps, width)
    payload = payload.value.reshape(-1, steps, width + LANES)
    all_queries = payload[:, :, :width]
    digits = payload[:, :, width : width + 2].astype(jnp.int32)
    all_positives = digits[:, :, 0] * 256 + digits[:, :, 1]
    first = (dp_index * grid.rep + rep_index) * count
    logits = jnp.einsum("qmd,pmd->mqp", all_queries, all_cls, preferred_element_type=F32)
    logits = logits * inv_width
    query_total = jax.nn.logsumexp(logits, axis=-1)
    passages_all = all_cls.shape[0]
    mine = lax.dynamic_slice_in_dim(logits, first, count, axis=1)
    mine_total = lax.dynamic_slice_in_dim(query_total, first, count, axis=1)
    onehot = (positives[:, :, None] == jnp.arange(passages_all)[None, None, :]).astype(F32)
    query_loss = mine_total - jnp.sum(mine * onehot, axis=-1)
    mine_grad = (jnp.exp(mine - mine_total[:, :, None]) - onehot) * inv_width
    queries_grad = jnp.einsum(
        "mqp,pmd->mqd", mine_grad.astype(BF16), all_cls, preferred_element_type=F32
    )
    column = lax.dynamic_slice_in_dim(logits, first, count, axis=2)
    hit = (all_positives.T[:, :, None] == (first + jnp.arange(count))[None, None, :]).astype(F32)
    column_grad = (jnp.exp(column - query_total[:, :, None]) - hit) * inv_width
    cls_grad = jnp.einsum(
        "mqp,qmd->mpd", column_grad.astype(BF16), all_queries, preferred_element_type=F32
    )

    grad_start = cls_grad.reshape(total, width)
    unit_start = starts(unit_two)
    grad_gain_two = grad_gain_two + jnp.sum(grad_start * unit_start, axis=0)
    grad_shift_two = grad_shift_two + jnp.sum(grad_start, axis=0)
    grad_start = grad_start + starts(out_grad.reshape(rows, width)).astype(F32)
    grad_start = norm_back(grad_start, unit_start, starts(scale_two), gain_two)
    down_start = grad_start.astype(BF16)
    up_starts = [up_back(down_start, part, starts(slope)).astype(BF16) for part in parts]
    grad_b_down = grad_b_down + row_total(down_start)
    grad_two = put_starts(grad_two, grad_start)
    down_low = put_starts(down_low, down_start)
    up_lows = [put_starts(u, start) for u, start in zip(up_lows, up_starts)]
    grad_b_up = jnp.concatenate([row_total(u) for u in up_lows])

    up_sum, first_sum, last_sum = [Scatter(grid, here) for _ in range(3)]
    grad_w_down = mm_left(gelu_low, down_low).astype(BF16)
    shard_w_down = lax.psum_scatter(grad_w_down, "dp", scatter_dimension=0, tiled=True)
    order = after(grid, grad_w_down)
    up_sum.start([plus(mm_left(hidden_low, u), order).astype(BF16) for u in up_lows])
    order = after(grid, up_sum.held)
    up_sum.step(order)
    grad_hidden = plus(grad_two + mm_back(up_lows[0], weight_up[:, parts[0]]), order)
    order = after(grid, up_sum.held, grad_hidden)
    up_sum.step(order)
    order = after(grid, up_sum.sent)
    grad_hidden = plus(grad_hidden + mm_back(up_lows[1], weight_up[:, parts[1]]), order)
    grad_gain_one = jnp.sum(grad_hidden * unit_one, axis=0)
    grad_shift_one = jnp.sum(grad_hidden, axis=0)
    grad_one = norm_back(grad_hidden, unit_one, scale_one, gain_one)
    attn_low = grad_one.astype(BF16)
    order = after(grid, up_sum.held, attn_low)
    up_sum.step(order)
    order = after(grid, up_sum.sent)
    grad_b_out = row_total(attn_low)
    grad_w_out = plus(mm_left(context, attn_low), order).astype(BF16)
    context_grad = plus(mm_back(attn_low, weight_out), order).astype(BF16)
    order = after(grid, context_grad, grad_w_out)
    q_low, k_low, v_low = attention_back(
        q, k, v, context_grad, log_total, spans, [jnp.full((8, LANES), order, F32)], length, H
    )
    order = after(grid, up_sum.held, q_low)
    up_sum.step(order)

    order = after(grid, up_sum.sent)

    def weight_grad(grad):
        return plus(mm_left(tokens, grad), order).astype(BF16)

    first_sum.start([grad_w_out, weight_grad(v_low)])
    order = after(grid, first_sum.held)
    first_sum.step(order)
    grad_b_query = row_total(q_low)
    grad_b_value = row_total(v_low)
    last_sum.start([weight_grad(q_low), weight_grad(k_low)])
    grads = (
        grad_b_query,
        grad_b_value,
        grad_b_out,
        grad_gain_one,
        grad_shift_one,
        grad_b_down,
        grad_gain_two,
        grad_shift_two,
    )
    grads = jnp.concatenate([jnp.stack(grads), grad_b_up.reshape(spread, width)])

    grads = Total(grid, grads)
    order = after(grid, up_sum.held, first_sum.held, last_sum.held)
    for group in (first_sum, last_sum, up_sum, grads):
        group.step(order)
    order = after(grid, first_sum.sent, up_sum.sent)
    input_grad = plus(grad_one + mm_back(q_low, weight_q), order)
    input_grad = input_grad + mm_back(k_low, weight_k) + mm_back(v_low, weight_v)
    shard_w_down = shard_w_down.astype(F32)
    if grid.fast:
        shard_w_down = shard_w_down + flip(shard_w_down.astype(BF16), "x").astype(F32)
    else:
        shard_w_down = lax.psum(shard_w_down, "rep")
    shard_w_up = jnp.concatenate(up_sum.finish(), axis=1)
    shard_w_out, shard_w_value = first_sum.finish()
    shard_w_query, shard_w_key = last_sum.finish()
    grads = grads.finish()
    low = lax.dynamic_slice_in_dim(grads[:8], dp_index * block, block, axis=1)
    s_b_up = lax.dynamic_slice_in_dim(
        grads[8:].reshape(-1), dp_index * spread * block, spread * block, axis=0
    )
    (s_b_q, s_b_v, s_b_out, s_gain1, s_shift1, s_b_down, s_gain2, s_shift2) = [
        low[i] for i in range(8)
    ]
    return (
        output,
        query_loss,
        input_grad.reshape(steps, count, length, width),
        queries_grad,
        cls_grad,
        shard_w_query,
        s_b_q,
        shard_w_key,
        shard_w_value,
        s_b_v,
        shard_w_out,
        s_b_out,
        s_gain1,
        s_shift1,
        shard_w_up,
        s_b_up,
        shard_w_down,
        s_b_down,
        s_gain2,
        s_shift2,
    )


def solution(mesh):
    both = ("dp", "rep")
    matrix, vector = P("dp", None), P("dp")
    weights = (
        matrix, vector, matrix, matrix, vector, matrix, vector, vector, vector,
        matrix, vector, matrix, vector, vector, vector,
    )
    grid = Grid(mesh.shape["dp"], mesh.shape["rep"], 768 // mesh.shape["dp"])
    wide = P(None, both, None, None)
    return jax.shard_map(
        functools.partial(per_device, grid),
        mesh=mesh,
        in_specs=(wide, P(None, both), P(None, both, None), P(None, both), wide) + weights,
        out_specs=(wide, P(None, both), wide, P(None, both, None), P(None, both, None)) + weights,
        check_vma=False,
    )
```

```python
import functools
import math

import jax
import jax.numpy as jnp
from jax import lax
from jax.experimental import pallas as pl
from jax.experimental.pallas import tpu as pltpu
from jax.sharding import PartitionSpec as P

H = 12
F32 = jnp.float32
BF16 = jnp.bfloat16
INV_SQRT2 = 1.0 / math.sqrt(2.0)
INV_SQRT_2PI = 1.0 / math.sqrt(2.0 * math.pi)


ANY = pl.BlockSpec(memory_space=pl.ANY)
SMEM = pl.BlockSpec(memory_space=pltpu.SMEM)
VMEM = pl.BlockSpec(memory_space=pltpu.VMEM)
MIB = 2**20
LANES = 128


class Grid:
    def __init__(self, dp, rep, rows):
        self.dp, self.rep = dp, rep
        self.fast = dp == 16 and rep == 2 and rows % 16 == 0
        self.bits = {"core": 1, "y": 2, "z1": 4, "z2": 8}

        place = [
            (((z * 2 + y) * 2 + c) * 2 + x, (z, y, c, x))
            for z in range(4)
            for y in range(2)
            for c in range(2)
            for x in range(2)
        ]
        lines, squares = {}, {}
        for i, (z, y, c, x) in place:
            lines.setdefault((y, c, x), []).append(i)
            squares.setdefault((z, c), []).append(i)
        self.groups = {"z": list(lines.values()), "xy": list(squares.values()), "all": None}

    def exchange(self, value, name):
        return lax.all_to_all(
            value, ("dp", "rep"), 0, 0, axis_index_groups=self.groups[name], tiled=True
        )

    def share(self, value, name, order=0.0):
        count = self.dp * self.rep if name == "all" else 4
        value = plus(jnp.broadcast_to(value[None], (count,) + value.shape), order)
        return self.exchange(value, name)

    def flip(self, value, name):
        if name == "x":
            return lax.ppermute(value, "rep", [(i, i ^ 1) for i in range(self.rep)])
        bit = self.bits[name]
        return lax.ppermute(value, "dp", [(i, i ^ bit) for i in range(self.dp)])


def run_copies(copies):
    for copy in copies:
        copy.start()
    for copy in copies:
        copy.wait()


def place_of(here_ref, key, rows):
    core, y, z, half = key[:4]
    if len(key) > 4:
        place = z * 4 + y * 2 + ((here_ref[0] & 1) ^ core)
        return pl.ds(pl.multiple_of(place * rows, 16), rows), half
    row = pl.multiple_of((here_ref[0] ^ (z * 4 + y * 2 + core)) * rows, 16)
    return pl.ds(row, rows), here_ref[1] ^ half


def square_keys(core):
    return [(core, y, z, x, True) for y in range(2) for x in range(2) for z in range(4)]


def join_kernel(here_ref, *refs, keys, widths, extra):
    count = len(keys)
    pieces, outs, sems = refs[:count], refs[count:-1], refs[-1]
    copies = []
    for piece, names in zip(pieces, keys):
        for i, key in enumerate(names):
            rows = piece.shape[1]
            where, half = place_of(here_ref, key, rows)
            at = 0
            for out, width in zip(outs, widths):
                column = half * width
                if len(key) == 4:
                    column = pl.multiple_of(column, LANES)
                column = pl.ds(column, width)
                copies.append((piece.at[i, :, pl.ds(at, width)], out.at[where, column]))
                at += width
            if extra and key[3] == 0:
                copies.append((piece.at[i, :, pl.ds(at, extra)], outs[-1].at[where, :]))
    run_copies([pltpu.make_async_copy(a, b, sems.at[i]) for i, (a, b) in enumerate(copies)])


def join(bag, widths, extra, here):
    arrays, keys = zip(*bag)
    rows = arrays[0].shape[1]
    shapes = [(16 * rows, 2 * width) for width in widths] + ([(16 * rows, extra)] if extra else [])
    copies = 32 * len(widths) + (16 if extra else 0)
    size = sum(a * b for a, b in shapes)
    return pl.pallas_call(
        functools.partial(join_kernel, keys=keys, widths=widths, extra=extra),
        out_shape=[jax.ShapeDtypeStruct(shape, arrays[0].dtype) for shape in shapes],
        in_specs=[SMEM] + [ANY] * len(arrays),
        out_specs=[VMEM] * len(shapes),
        scratch_shapes=[pltpu.SemaphoreType.DMA((copies,))],
        compiler_params=pltpu.CompilerParams(vmem_limit_bytes=2 * MIB),
        cost_estimate=pl.CostEstimate(flops=0, bytes_accessed=4 * size, transcendentals=0),
        name="join",
    )(here, *arrays)


def split_kernel(here_ref, *refs, keys, count):
    values, pieces, sems = refs[:count], refs[count:-1], refs[-1]
    copies = []
    for piece, names in zip(pieces, keys):
        rows = piece.shape[1]
        for i, key in enumerate(names):
            where, half = place_of(here_ref, key, rows)
            at = 0
            for value in values:
                width = value.shape[1] // 2
                column = half * width
                if len(key) == 4:
                    column = pl.multiple_of(column, LANES)
                column = pl.ds(column, width)
                copies.append((value.at[where, column], piece.at[i, :, pl.ds(at, width)]))
                at += width
    run_copies([pltpu.make_async_copy(a, b, sems.at[i]) for i, (a, b) in enumerate(copies)])


def split(values, keys, here):
    rows, width = values[0].shape[0] // 16, sum(v.shape[1] for v in values) // 2
    kind = values[0].dtype
    size = sum(v.size for v in values)
    return pl.pallas_call(
        functools.partial(split_kernel, keys=keys, count=len(values)),
        out_shape=[jax.ShapeDtypeStruct((len(names), rows, width), kind) for names in keys],
        in_specs=[SMEM] + [VMEM] * len(values),
        out_specs=[ANY] * len(keys),
        scratch_shapes=[pltpu.SemaphoreType.DMA((32 * len(values),))],
        compiler_params=pltpu.CompilerParams(vmem_limit_bytes=2 * MIB),
        cost_estimate=pl.CostEstimate(flops=0, bytes_accessed=4 * size, transcendentals=0),
        name="split",
    )(here, *values)


def order_kernel(*refs):
    refs[-1][0, 0] = 0.0


def after(grid, *trees):
    if not grid.fast:
        return 0.0
    leaves = jax.tree.leaves(trees)
    return pl.pallas_call(
        order_kernel,
        out_shape=jax.ShapeDtypeStruct((1, 1), F32),
        in_specs=[ANY] * len(leaves),
        out_specs=SMEM,
        compiler_params=pltpu.CompilerParams(vmem_limit_bytes=MIB // 4),
        name="order",
    )(*leaves).reshape(())


def halves_of(parts, extra, x):
    out = []
    for place in (x, 1 - x):
        row = [
            lax.dynamic_slice_in_dim(p, place * (p.shape[1] // 2), p.shape[1] // 2, axis=1)
            for p in parts
        ]
        out.append(jnp.concatenate(row + ([extra] if extra is not None else []), axis=1))
    return out


def core_keys(keys):
    return [(1,) + key[1:] for key in keys]


class Spread:
    def __init__(self, grid, value):
        self.grid, self.value = grid, value
        self.names = ["x", "core", "y", "z1", "z2"]
        self.other = None
        if not grid.fast:
            self.value = lax.all_gather(value, ("dp", "rep"), axis=0, tiled=True)
            self.names = []

    def absorb(self, order=0.0):
        if self.other is None:
            return
        name = self.names.pop(0)
        if name == "x":
            upper = lax.axis_index("rep") > 0
        else:
            upper = (lax.axis_index("dp") & self.grid.bits[name]) > 0
        low = jnp.where(upper, self.other, self.value)
        high = jnp.where(upper, self.value, self.other)
        self.value, self.other = jnp.concatenate([low, high], axis=0), None
        self.value = plus(self.value, order)

    def step(self, order=0.0):
        self.absorb(order)
        if self.names:
            self.other = self.grid.flip(self.value, self.names[0])
            self.held = [self.other]


class Total:
    def __init__(self, grid, value):
        self.grid, self.parts = grid, [value]
        self.names = ["x", "core", "y", "z1", "z2"]
        if not grid.fast:
            self.parts, self.names = [lax.psum(value, ("dp", "rep"))], []

    def step(self, order=0.0):
        value = sum(self.parts[1:], self.parts[0])
        self.parts = [plus(value, order)]
        if self.names:
            self.parts.append(self.grid.flip(self.parts[0], self.names.pop(0)))
        self.held = self.parts[1:]

    def finish(self):
        while self.names:
            self.step()
        return sum(self.parts[1:], self.parts[0])


def plus(value, order):
    return value if isinstance(order, float) else (value.astype(F32) + order).astype(value.dtype)


def sums_kernel(order_ref, *refs, plan, count):
    zero = order_ref[0, 0]
    for out_ref, terms in zip(refs[count:], plan):
        at = 0
        for size, parts in terms:
            for i in range(size):
                total = zero
                for source, first in parts:
                    total = total + refs[source][first + i].astype(F32)
                out_ref[at + i] = total.astype(out_ref.dtype)
            at += size


def sums(order, arrays, plan):
    shapes = [(sum(size for size, _ in terms),) + arrays[0].shape[1:] for terms in plan]
    size = sum(a * b * c for a, b, c in shapes)
    return pl.pallas_call(
        functools.partial(sums_kernel, plan=plan, count=len(arrays)),
        out_shape=[jax.ShapeDtypeStruct(shape, BF16) for shape in shapes],
        in_specs=[SMEM] + [VMEM] * len(arrays),
        out_specs=[VMEM] * len(shapes),
        compiler_params=pltpu.CompilerParams(vmem_limit_bytes=8 * MIB),
        cost_estimate=pl.CostEstimate(flops=2 * size, bytes_accessed=6 * size, transcendentals=0),
        name="sums",
    )(jnp.full((1, 1), order, F32), *arrays)


class Scatter:
    def __init__(self, grid, here):
        self.grid, self.here, self.stage, self.held, self.sent = grid, here, 0, [], []

    def start(self, grads):
        self.widths = [g.shape[1] for g in grads]
        if not self.grid.fast:
            parts = [
                lax.psum_scatter(g.astype(F32), "dp", scatter_dimension=0, tiled=True)
                for g in grads
            ]
            self.result = [lax.psum(p, "rep") for p in parts]
            return
        keys = [
            [(c, y, z, h) for y, h in ((1, 1), (0, 1), (1, 0), (0, 0)) for z in range(4)]
            for c in range(2)
        ]
        self.near, self.far = split(grads, keys, self.here)
        self.held = [self.far]

    def step(self, order=0.0):
        if not self.grid.fast:
            return
        flip = self.grid.flip
        self.stage += 1
        if self.stage == 1:
            self.held = [flip(self.far, "core")]
        elif self.stage == 2:
            plan = [[(n, [(0, at), (1, at)])] for n, at in ((2, 0), (2, 2), (4, 4), (4, 8), (4, 12))]
            low, high, self.x, self.y, self.own = sums(order, [self.near, *self.held], plan)
            self.sent, self.held = [low, high], [flip(low, "x"), flip(high, "y")]
        elif self.stage == 3:
            plan = [[(2, [(0, 0)]), (2, [(0, 2), (3, 0)])], [(2, [(1, 0), (2, 0)]), (2, [(1, 2)])]]
            to_x, to_y = sums(order, [self.x, self.y, *self.held], plan)
            self.sent, self.held = [to_x, to_y], [flip(to_x, "x"), flip(to_y, "y")]
        elif self.stage == 4:
            plan = [[(2, [(0, at), (1, at), (2, at)])] for at in (0, 2)]
            self.low, high = sums(order, [self.own, *self.held], plan)
            self.sent, self.held = [high], [flip(high, "z2")]
        elif self.stage == 5:
            plan = [[(1, [(0, at), (1, at)])] for at in (0, 1)]
            self.low, high = sums(order, [self.low, *self.held], plan)
            self.sent, self.held = [high], [flip(high, "z1")]
        elif self.stage == 6:
            (self.low,) = sums(order, [self.low, *self.held], [[(1, [(0, 0), (1, 0)])]])
            self.sent, self.held = [self.low], [flip(self.low, "x")]

    def finish(self):
        if not self.grid.fast:
            return self.result
        while self.stage < 6:
            self.step()
        value, other = self.low[0], self.held[0][0]
        first = self.here[1] == 0
        left, right = jnp.where(first, value, other), jnp.where(first, other, value)
        out, at = [], 0
        for width in self.widths:
            cut = slice(at, at + width // 2)
            out.append(jnp.concatenate([left[:, cut], right[:, cut]], axis=1).astype(F32))
            at += width // 2
        return out


class SquareScatter(Scatter):
    def start(self, grads):
        if not self.grid.fast:
            super().start(grads)
            return
        self.widths = [g.shape[1] for g in grads]
        self.near, self.far = split(grads, [square_keys(0), square_keys(1)], self.here)
        self.held = [self.far]

    def step(self, order=0.0):
        if not self.grid.fast:
            return
        self.stage += 1
        if self.stage == 1:
            self.held = [self.grid.flip(self.far, "core")]
            return
        if self.stage == 2:
            (value,) = sums(order, [self.near, *self.held], [[(16, [(0, 0), (1, 0)])]])
            self.held = [self.grid.exchange(value, "xy")]
        elif self.stage == 3:
            (value,) = sums(order, self.held, [[(4, [(0, 4 * i) for i in range(4)])]])
            self.held = [self.grid.exchange(value, "z")]
        elif self.stage == 4:
            (value,) = sums(order, self.held, [[(1, [(0, i) for i in range(4)])]])
            self.low, self.held = value, [self.grid.flip(value, "x")]
            self.stage = 6
        self.sent = [value]


def mm(left, right):
    return jnp.dot(left, right, preferred_element_type=F32)


def mm_left(left, right):
    return lax.dot_general(left, right, (((0,), (0,)), ((), ())), preferred_element_type=F32)


def mm_back(left, right):
    return lax.dot_general(left, right, (((1,), (1,)), ((), ())), preferred_element_type=F32)


def row_total(values):
    return mm(jnp.ones((8, values.shape[0]), BF16), values)[0]


def normal_parts(v):
    phi = 0.5 + 0.5 * lax.erf(v * INV_SQRT2)
    return phi, jnp.exp(-0.5 * v * v) * INV_SQRT_2PI


def norm_parts(v):
    mean_val = jnp.mean(v, axis=-1, keepdims=True)
    centred = v - mean_val
    variance = jnp.mean(centred * centred, axis=-1, keepdims=True)
    scale = lax.rsqrt(variance + 1e-05)
    return centred * scale, scale


def norm_back(grad, unit, scale, gain):
    inner = grad * gain
    mean_one = jnp.mean(inner, axis=-1, keepdims=True)
    mean_two = jnp.mean(inner * unit, axis=-1, keepdims=True)
    return (inner - mean_one - unit * mean_two) * scale


def two_heads(t, first):
    zero = jnp.zeros_like(t)
    return jnp.concatenate([jnp.where(first, t, zero), jnp.where(first, zero, t)], axis=0)

def attn_kernel(len_ref, q_ref, k_ref, v_ref, *refs, scale, n, pairs, many):
    c_ref, total_ref = refs[-2:]
    lane = lax.broadcasted_iota(jnp.int32, (1, 2 * n), 1) % n
    first = lax.broadcasted_iota(jnp.int32, (n, LANES), 1) < LANES // 2
    spot = lax.broadcasted_iota(jnp.int32, (n, LANES), 1)
    for i in range(many):
        rows = slice(i * n, (i + 1) * n)
        length = len_ref[pl.program_id(0) * many + i]
        totals = jnp.zeros((n, LANES), F32)
        for pair in range(pairs):
            at = slice(pair * LANES, (pair + 1) * LANES)
            q = q_ref[rows, at] * scale
            s = mm_back(q, two_heads(k_ref[rows, at], first))
            s = jnp.where(lane < length, s, -1000000000.0)
            parts = []
            for h in range(2):
                part = s[:, h * n : (h + 1) * n]
                top = jnp.max(part, axis=-1, keepdims=True)
                part = jnp.exp(part - top)
                total = jnp.sum(part, axis=-1, keepdims=True)
                parts.append((part * (1.0 / total)).astype(BF16))
                totals = jnp.where(spot == 2 * pair + h, top + jnp.log(total), totals)
            p = jnp.concatenate(parts, axis=1)
            c_ref[rows, at] = mm(p, two_heads(v_ref[rows, at], first)).astype(BF16)
        total_ref[i] = totals.T[: total_ref.shape[1]]

def attention(q, k, v, lengths, deps, n, heads):
    rows, width = q.shape
    count, many = rows // n, 2
    scale = 1.0 / math.sqrt(width // heads)
    block = pl.BlockSpec((n * many, width), lambda i: (i, 0))
    lines = 16
    return pl.pallas_call(
        functools.partial(attn_kernel, scale=scale, n=n, pairs=heads // 2, many=many),
        grid=(count // many,),
        in_specs=[SMEM, block, block, block] + [ANY] * len(deps),
        out_specs=[block, pl.BlockSpec((many, lines, n), lambda i: (i, 0, 0))],
        out_shape=[jax.ShapeDtypeStruct((rows, width), BF16), jax.ShapeDtypeStruct((count, lines, n), F32)],
        compiler_params=pltpu.CompilerParams(vmem_limit_bytes=16 * MIB),
        cost_estimate=pl.CostEstimate(flops=8 * rows * n * width, bytes_accessed=8 * rows * width, transcendentals=rows * n * heads),
        name="attention",
    )(lengths, q, k, v, *deps)

def attn_back_kernel(len_ref, total_ref, q_ref, k_ref, v_ref, d_ref, *refs, scale, n, pairs, many):
    dq_ref, dk_ref, dv_ref = refs[-3:]
    row = lax.broadcasted_iota(jnp.int32, (2 * n, n), 0) % n
    first = lax.broadcasted_iota(jnp.int32, (n, LANES), 1) < LANES // 2
    for i in range(many):
        rows = slice(i * n, (i + 1) * n)
        length = len_ref[pl.program_id(0) * many + i]
        valid = row < length
        for pair in range(pairs):
            at = slice(pair * LANES, (pair + 1) * LANES)
            q, k, v, d = q_ref[rows, at] * scale, k_ref[rows, at] * scale, v_ref[rows, at], d_ref[rows, at]
            kk = two_heads(k_ref[rows, at], first)
            s = jnp.where(valid, mm_back(kk, q), -1000000000.0)
            dp = mm_back(two_heads(v, first), d)
            ps, ds = [], []
            for h in range(2):
                part = slice(h * n, (h + 1) * n)
                p = jnp.exp(s[part] - total_ref[i, 2 * pair + h : 2 * pair + h + 1, :])
                t = p * dp[part]
                ds.append((t - p * jnp.sum(t, axis=0, keepdims=True)).astype(BF16))
                ps.append(p.astype(BF16))
            dv_ref[rows, at] = mm(jnp.concatenate(ps, axis=1), two_heads(d, first)).astype(BF16)
            dk_ref[rows, at] = mm(jnp.concatenate(ds, axis=1), two_heads(q, first)).astype(BF16)
            dq_ref[rows, at] = mm_left(jnp.concatenate(ds, axis=0), two_heads(k, first)).astype(BF16)

def attention_back(q, k, v, d, totals, lengths, deps, n, heads):
    rows, width = q.shape
    count, many = rows // n, 2
    scale = 1.0 / math.sqrt(width // heads)
    block = pl.BlockSpec((n * many, width), lambda i: (i, 0))
    shape = jax.ShapeDtypeStruct((rows, width), BF16)
    return pl.pallas_call(
        functools.partial(attn_back_kernel, scale=scale, n=n, pairs=heads // 2, many=many),
        grid=(count // many,),
        in_specs=[SMEM, pl.BlockSpec((many,) + totals.shape[1:], lambda i: (i, 0, 0))] + [block] * 4 + [ANY] * len(deps),
        out_specs=[block] * 3,
        out_shape=[shape] * 3,
        compiler_params=pltpu.CompilerParams(vmem_limit_bytes=16 * MIB),
        cost_estimate=pl.CostEstimate(flops=20 * rows * n * width, bytes_accessed=14 * rows * width, transcendentals=rows * n * heads),
        name="attention_back",
    )(lengths, totals, q, k, v, d, *deps)


def per_device(
    grid,
    passages,
    lengths,
    queries,
    positives,
    out_grad,
    w_query,
    b_query,
    w_key,
    w_value,
    b_value,
    w_out,
    b_out,
    norm1_gain,
    norm1_bias,
    w_up,
    b_up,
    w_down,
    b_down,
    norm2_gain,
    norm2_bias,
):
    steps, count, length, width = passages.shape
    total = steps * count
    rows = total * length
    inv_width = 1.0 / math.sqrt(width)
    dp = grid.dp
    dp_index, rep_index = lax.axis_index("dp"), lax.axis_index("rep")
    here = jnp.stack([dp_index, rep_index]).astype(jnp.int32)

    block = w_query.shape[0]
    vectors = (b_query, b_value, b_out, norm1_gain, norm1_bias, b_down, norm2_gain, norm2_bias)
    spread = b_up.shape[0] // block
    columns = [v[:, None] for v in vectors] + [b_up.reshape(spread, block).T]
    columns = jnp.concatenate(columns, axis=1)
    columns = jnp.pad(columns, ((0, 0), (0, LANES - columns.shape[1])))
    tokens = passages.reshape(rows, width)
    digits = jnp.stack([positives.T // 256, positives.T % 256], axis=-1).astype(BF16)
    payload = jnp.concatenate(
        [
            jnp.moveaxis(queries, 0, 1).reshape(total, width),
            jnp.pad(digits.reshape(total, 2), ((0, 0), (0, LANES - 2))),
        ],
        axis=-1,
    )
    spans = lengths.reshape(total)
    if grid.fast:
        flip = grid.flip
        mine, twin = halves_of((w_query, w_key, w_value), columns, here[1])
        own, mine = jnp.stack([mine, twin]), mine[None]
        second = halves_of((w_out, w_up), None, here[1])[0][None]
        third = halves_of((w_down,), None, here[1])[0]
        across, h1, h2 = flip(own, "y"), flip(mine, "z1"), flip(mine, "z2")
        s1 = flip(second, "z1")
        order = after(grid, across, h1, h2)
        line = plus(jnp.concatenate([h1, h2]), order)
        h3, line_y, line_x = flip(h1, "z2"), flip(line, "y"), flip(line, "x")
        second = plus(jnp.concatenate([second, s1]), order)
        second_far = flip(second, "z2")
        own_c, across_c = flip(own, "core"), flip(across, "core")
        order = after(grid, h3, line_y, line_x, second)
        back_y = flip(plus(jnp.concatenate([h3, line_x[:1]]), order), "y")
        back_x = flip(plus(jnp.concatenate([h3, line_y[1:]]), order), "x")
        cores = [flip(v, "core") for v in (line, h3, line_y, line_x)]
        order = after(grid, back_y, back_x)
        end = flip(plus(back_y[:1], order), "x")
        second = plus(second, order)
        second_y, second_x = flip(second, "y"), flip(second, "x")
        cores = [own_c, across_c] + cores + [flip(v, "core") for v in (back_y, back_x)]
        cores.append(flip(end, "core"))
        bag = [
            (own, [(0, 0, 0, 0), (0, 0, 0, 1)]),
            (across, [(0, 1, 0, 0), (0, 1, 0, 1)]),
            (line, [(0, 0, 1, 0), (0, 0, 2, 0)]),
            (h3, [(0, 0, 3, 0)]),
            (line_y, [(0, 1, 1, 0), (0, 1, 2, 0)]),
            (line_x, [(0, 0, 1, 1), (0, 0, 2, 1)]),
            (back_y, [(0, 1, 3, 0), (0, 1, 1, 1)]),
            (back_x, [(0, 0, 3, 1), (0, 1, 2, 1)]),
            (end, [(0, 1, 3, 1)]),
        ]
        bag += [(v, core_keys(keys)) for v, (_, keys) in zip(cores, bag)]
        weight_q, weight_k, weight_v, table = join(bag, [width // 2] * 3, LANES, here)
        order = after(grid, table)
        high = plus(second_far, order)
        high_y, high_x = flip(high, "y"), flip(high, "x")
        second_cross = flip(plus(second_y, order), "x")
        third = grid.share(third, "z", order)
        order = after(grid, high)
    else:
        weight_q, weight_k, weight_v, table, weight_out, weight_up, weight_down = [
            lax.all_gather(w, "dp", axis=0, tiled=True)
            for w in (w_query, w_key, w_value, columns, w_out, w_up, w_down)
        ]
        order = 0.0
    table = table[:, :16].T.astype(F32)
    (bias_q, bias_v, bias_out, gain_one, shift_one, bias_down, gain_two, shift_two) = [
        table[i] for i in range(8)
    ]
    bias_up = jnp.transpose(
        table[8 : 8 + spread].reshape(spread, dp, block), (1, 0, 2)
    ).reshape(-1)
    q = plus(mm(tokens, weight_q) + bias_q, order).astype(BF16)
    k = plus(mm(tokens, weight_k), order).astype(BF16)
    v = plus(mm(tokens, weight_v) + bias_v, order).astype(BF16)
    z_keys = [[(0, y, z, h) for z in range(4)] for y, h in ((0, 0), (1, 0), (0, 1), (1, 1))]

    def bag_of(blocks):
        cores = [flip(v, "core") for v, _ in blocks]
        return blocks + [(v, core_keys(keys)) for v, (_, keys) in zip(cores, blocks)]

    low_keys = [keys[:2] for keys in z_keys]
    high_keys = [keys[2:] for keys in z_keys]
    if grid.fast:
        order = after(grid, q, high_x, high_y)
        high_cross = flip(plus(high_x, order), "y")
        attention_order = [jnp.full((8, LANES), order, F32)]
    else:
        attention_order = []
    context, log_total = attention(q, k, v, spans, attention_order, length, H)
    if grid.fast:
        order = after(grid, context, high_cross, second_cross, third)
        third = grid.share(third, "xy", order)
        order = after(grid, context, high_cross)
        blocks = (second, second_y, second_x, second_cross)
        blocks = list(zip(blocks, low_keys)) + list(zip((high, high_y, high_x, high_cross), high_keys))
        weight_out, weight_up = join(bag_of(blocks), [width // 2, w_up.shape[1] // 2], 0, here)
        order = after(grid, weight_out)
    sum_one = tokens.astype(F32) + mm(context, weight_out) + bias_out
    unit_one, scale_one = norm_parts(sum_one)
    hidden = unit_one * gain_one + shift_one
    hidden_low = hidden.astype(BF16)
    pre = mm(hidden_low, weight_up) + bias_up
    phi, density = normal_parts(pre)
    gelu_low = (pre * phi).astype(BF16)
    slope = (phi + pre * density).astype(BF16)
    if grid.fast:
        order = after(grid, gelu_low, third)
        third = third.reshape((16,) + third.shape[2:])
        bag = [(third, square_keys(0)), (flip(third, "core"), square_keys(1))]
        (weight_down,) = join(bag, [width // 2], 0, here)
    sum_two = plus(hidden, order) + mm(gelu_low, weight_down) + bias_down
    unit_two, scale_two = norm_parts(sum_two)
    result = (unit_two * gain_two + shift_two).reshape(steps, count, length, width)
    output = result.astype(BF16)

    def starts(value):
        return value.reshape(total, length, -1)[:, 0]

    def put_starts(value, part):
        blocks = value.reshape(total, length, -1)
        return lax.dynamic_update_slice(blocks, part[:, None], (0, 0, 0)).reshape(value.shape)

    cls = jnp.moveaxis(output[:, :, 0, :], 0, 1).reshape(total, width)
    if grid.fast:
        cls = grid.share(jnp.concatenate([cls, payload], axis=1), "all")
    else:
        cls = jnp.concatenate([cls, payload], axis=1)
        cls = lax.all_gather(cls, ("dp", "rep"), axis=0, tiled=True)
    grad_out = out_grad.reshape(rows, width).astype(F32)
    grad_two = norm_back(grad_out, unit_two, scale_two, gain_two)
    down_low = grad_two.astype(BF16)
    later = (jnp.arange(rows) % length > 0)[:, None]
    grad_gain_two = jnp.sum(grad_out * unit_two, axis=0)
    grad_shift_two = jnp.sum(grad_out, axis=0)
    grad_b_down = jnp.sum(jnp.where(later, down_low.astype(F32), 0.0), axis=0)
    parts = [slice(0, w_up.shape[1] // 2), slice(w_up.shape[1] // 2, w_up.shape[1])]

    def up_back(grad, part, by):
        return mm_back(grad, weight_down[part]) * by[:, part].astype(F32)

    up_lows = [up_back(down_low, part, slope).astype(BF16) for part in parts]
    order = after(grid, cls, up_lows)

    cls = plus(cls.reshape(-1, steps, 2 * width + LANES), order)
    all_cls, all_queries = cls[:, :, :width], cls[:, :, width : 2 * width]
    digits = cls[:, :, 2 * width : 2 * width + 2].astype(jnp.int32)
    all_positives = digits[:, :, 0] * 256 + digits[:, :, 1]
    first = (dp_index * grid.rep + rep_index) * count
    logits = jnp.einsum("qmd,pmd->mqp", all_queries, all_cls, preferred_element_type=F32)
    logits = logits * inv_width
    query_total = jax.nn.logsumexp(logits, axis=-1)
    passages_all = all_cls.shape[0]
    mine = lax.dynamic_slice_in_dim(logits, first, count, axis=1)
    mine_total = lax.dynamic_slice_in_dim(query_total, first, count, axis=1)
    onehot = (positives[:, :, None] == jnp.arange(passages_all)[None, None, :]).astype(F32)
    query_loss = mine_total - jnp.sum(mine * onehot, axis=-1)
    mine_grad = (jnp.exp(mine - mine_total[:, :, None]) - onehot) * inv_width
    queries_grad = jnp.einsum(
        "mqp,pmd->mqd", mine_grad.astype(BF16), all_cls, preferred_element_type=F32
    )
    column = lax.dynamic_slice_in_dim(logits, first, count, axis=2)
    hit = (all_positives.T[:, :, None] == (first + jnp.arange(count))[None, None, :]).astype(F32)
    column_grad = (jnp.exp(column - query_total[:, :, None]) - hit) * inv_width
    cls_grad = jnp.einsum(
        "mqp,qmd->mpd", column_grad.astype(BF16), all_queries, preferred_element_type=F32
    )

    grad_start = cls_grad.reshape(total, width)
    unit_start = starts(unit_two)
    grad_gain_two = grad_gain_two + jnp.sum(grad_start * unit_start, axis=0)
    grad_shift_two = grad_shift_two + jnp.sum(grad_start, axis=0)
    grad_start = grad_start + starts(out_grad.reshape(rows, width)).astype(F32)
    grad_start = norm_back(grad_start, unit_start, starts(scale_two), gain_two)
    down_start = grad_start.astype(BF16)
    up_starts = [up_back(down_start, part, starts(slope)).astype(BF16) for part in parts]
    grad_b_down = grad_b_down + row_total(down_start)
    grad_two = put_starts(grad_two, grad_start)
    down_low = put_starts(down_low, down_start)
    up_lows = [put_starts(u, start) for u, start in zip(up_lows, up_starts)]
    grad_b_up = jnp.concatenate([row_total(u) for u in up_lows])

    down_sum, up_sum, first_sum, last_sum = [Scatter(grid, here) for _ in range(4)]
    down_sum.start([mm_left(gelu_low, down_low).astype(BF16)])
    order = after(grid, down_sum.held)
    down_sum.step(order)
    grads_up = [plus(mm_left(hidden_low, up_lows[0]), order).astype(BF16)]
    order = after(grid, down_sum.held, grads_up)
    down_sum.step(order)
    order = after(grid, down_sum.sent)
    grads_up.append(plus(mm_left(hidden_low, up_lows[1]), order).astype(BF16))
    up_sum.start(grads_up)
    order = after(grid, down_sum.held, up_sum.held)
    up_sum.step(order)
    down_sum.step(order)
    order = after(grid, down_sum.sent)
    grad_hidden = plus(grad_two + mm_back(up_lows[0], weight_up[:, parts[0]]), order)
    order = after(grid, up_sum.held, grad_hidden)
    up_sum.step(order)
    order = after(grid, up_sum.sent)
    grad_hidden = plus(grad_hidden + mm_back(up_lows[1], weight_up[:, parts[1]]), order)
    grad_gain_one = jnp.sum(grad_hidden * unit_one, axis=0)
    grad_shift_one = jnp.sum(grad_hidden, axis=0)
    grad_one = norm_back(grad_hidden, unit_one, scale_one, gain_one)
    attn_low = grad_one.astype(BF16)
    grad_b_out = row_total(attn_low)
    grad_w_out = mm_left(context, attn_low).astype(BF16)
    context_grad = mm_back(attn_low, weight_out).astype(BF16)
    order = after(grid, down_sum.held, up_sum.held, context_grad, grad_w_out)
    down_sum.step(order)
    up_sum.step(order)
    order = after(grid, down_sum.sent, up_sum.sent)
    q_low, k_low, v_low = attention_back(
        q, k, v, context_grad, log_total, spans, [jnp.full((8, LANES), order, F32)], length, H
    )
    order = after(grid, down_sum.held, up_sum.held, q_low)
    down_sum.step(order)
    up_sum.step(order)
    order = after(grid, down_sum.sent, up_sum.sent)

    def weight_grad(grad):
        return plus(mm_left(tokens, grad), order).astype(BF16)

    first_sum.start([grad_w_out, weight_grad(v_low)])
    order = after(grid, first_sum.held)
    first_sum.step(order)
    grad_b_query = row_total(q_low)
    grad_b_value = row_total(v_low)
    last_sum.start([weight_grad(q_low), weight_grad(k_low)])
    grads = (
        grad_b_query,
        grad_b_value,
        grad_b_out,
        grad_gain_one,
        grad_shift_one,
        grad_b_down,
        grad_gain_two,
        grad_shift_two,
    )
    grads = jnp.concatenate([jnp.stack(grads), grad_b_up.reshape(spread, width)])

    grads = Total(grid, grads)
    order = after(grid, up_sum.held, down_sum.held, first_sum.held, last_sum.held)
    for group in (first_sum, last_sum, up_sum, down_sum, grads):
        group.step(order)
    order = after(grid, first_sum.sent, up_sum.sent, down_sum.sent)
    input_grad = plus(grad_one + mm_back(q_low, weight_q), order)
    input_grad = input_grad + mm_back(k_low, weight_k) + mm_back(v_low, weight_v)
    (shard_w_down,) = down_sum.finish()
    shard_w_up = jnp.concatenate(up_sum.finish(), axis=1)
    shard_w_out, shard_w_value = first_sum.finish()
    shard_w_query, shard_w_key = last_sum.finish()
    grads = grads.finish()
    low = lax.dynamic_slice_in_dim(grads[:8], dp_index * block, block, axis=1)
    s_b_up = lax.dynamic_slice_in_dim(
        grads[8:].reshape(-1), dp_index * spread * block, spread * block, axis=0
    )
    (s_b_q, s_b_v, s_b_out, s_gain1, s_shift1, s_b_down, s_gain2, s_shift2) = [
        low[i] for i in range(8)
    ]
    return (
        output,
        query_loss,
        input_grad.reshape(steps, count, length, width),
        queries_grad,
        cls_grad,
        shard_w_query,
        s_b_q,
        shard_w_key,
        shard_w_value,
        s_b_v,
        shard_w_out,
        s_b_out,
        s_gain1,
        s_shift1,
        shard_w_up,
        s_b_up,
        shard_w_down,
        s_b_down,
        s_gain2,
        s_shift2,
    )


def solution(mesh):
    both = ("dp", "rep")
    matrix, vector = P("dp", None), P("dp")
    weights = (
        matrix, vector, matrix, matrix, vector, matrix, vector, vector, vector,
        matrix, vector, matrix, vector, vector, vector,
    )
    grid = Grid(mesh.shape["dp"], mesh.shape["rep"], 768 // mesh.shape["dp"])
    wide = P(None, both, None, None)
    return jax.shard_map(
        functools.partial(per_device, grid),
        mesh=mesh,
        in_specs=(wide, P(None, both), P(None, both, None), P(None, both), wide) + weights,
        out_specs=(wide, P(None, both), wide, P(None, both, None), P(None, both, None)) + weights,
        check_vma=False,
    )
```

```python
import functools
import math

import jax
import jax.numpy as jnp
from jax import lax
from jax.experimental import pallas as pl
from jax.experimental.pallas import tpu as pltpu
from jax.sharding import PartitionSpec as P

H = 12
F32 = jnp.float32
BF16 = jnp.bfloat16
INV_SQRT2 = 1.0 / math.sqrt(2.0)
INV_SQRT_2PI = 1.0 / math.sqrt(2.0 * math.pi)


ANY = pl.BlockSpec(memory_space=pl.ANY)
SMEM = pl.BlockSpec(memory_space=pltpu.SMEM)
VMEM = pl.BlockSpec(memory_space=pltpu.VMEM)
MIB = 2**20
LANES = 128


class Grid:
    def __init__(self, dp, rep, rows):
        self.dp, self.rep = dp, rep
        self.fast = dp == 16 and rep == 2 and rows % 16 == 0
        self.bits = {"core": 1, "y": 2, "z1": 4, "z2": 8, "z3": 12}

        place = [
            (((z * 2 + y) * 2 + c) * 2 + x, (z, y, c, x))
            for z in range(4)
            for y in range(2)
            for c in range(2)
            for x in range(2)
        ]
        lines, squares = {}, {}
        for i, (z, y, c, x) in place:
            lines.setdefault((y, c, x), []).append(i)
            squares.setdefault((z, c), []).append(i)
        self.groups = {"z": list(lines.values()), "xy": list(squares.values()), "all": None}

    def exchange(self, value, name):
        return lax.all_to_all(
            value, ("dp", "rep"), 0, 0, axis_index_groups=self.groups[name], tiled=True
        )

    def share(self, value, name, order=0.0):
        count = self.dp * self.rep if name == "all" else 4
        value = plus(jnp.broadcast_to(value[None], (count,) + value.shape), order)
        return self.exchange(value, name)

    def flip(self, value, name):
        if name == "x":
            return lax.ppermute(value, "rep", [(i, i ^ 1) for i in range(self.rep)])
        bit = self.bits[name]
        return lax.ppermute(value, "dp", [(i, i ^ bit) for i in range(self.dp)])


def run_copies(copies):
    for copy in copies:
        copy.start()
    for copy in copies:
        copy.wait()


def place_of(here_ref, key, rows):
    core, y, z, half = key[:4]
    if len(key) > 4:
        place = z * 4 + y * 2 + ((here_ref[0] & 1) ^ core)
        return pl.ds(pl.multiple_of(place * rows, 16), rows), half
    row = pl.multiple_of((here_ref[0] ^ (z * 4 + y * 2 + core)) * rows, 16)
    return pl.ds(row, rows), here_ref[1] ^ half


def square_keys(core):
    return [(core, y, z, x, True) for y in range(2) for x in range(2) for z in range(4)]


def join_kernel(here_ref, *refs, keys, widths, extra):
    count = len(keys)
    pieces, outs, sems = refs[:count], refs[count:-1], refs[-1]
    copies = []
    for piece, names in zip(pieces, keys):
        for i, key in enumerate(names):
            rows = piece.shape[1]
            where, half = place_of(here_ref, key, rows)
            at = 0
            for out, width in zip(outs, widths):
                column = half * width
                if len(key) == 4:
                    column = pl.multiple_of(column, LANES)
                column = pl.ds(column, width)
                copies.append((piece.at[i, :, pl.ds(at, width)], out.at[where, column]))
                at += width
            if extra and key[3] == 0:
                copies.append((piece.at[i, :, pl.ds(at, extra)], outs[-1].at[where, :]))
    run_copies([pltpu.make_async_copy(a, b, sems.at[i]) for i, (a, b) in enumerate(copies)])


def join(bag, widths, extra, here):
    arrays, keys = zip(*bag)
    rows = arrays[0].shape[1]
    shapes = [(16 * rows, 2 * width) for width in widths] + ([(16 * rows, extra)] if extra else [])
    copies = 32 * len(widths) + (16 if extra else 0)
    size = sum(a * b for a, b in shapes)
    return pl.pallas_call(
        functools.partial(join_kernel, keys=keys, widths=widths, extra=extra),
        out_shape=[jax.ShapeDtypeStruct(shape, arrays[0].dtype) for shape in shapes],
        in_specs=[SMEM] + [ANY] * len(arrays),
        out_specs=[VMEM] * len(shapes),
        scratch_shapes=[pltpu.SemaphoreType.DMA((copies,))],
        compiler_params=pltpu.CompilerParams(vmem_limit_bytes=2 * MIB),
        cost_estimate=pl.CostEstimate(flops=0, bytes_accessed=4 * size, transcendentals=0),
        name="join",
    )(here, *arrays)


def split_kernel(here_ref, *refs, keys, count):
    values, pieces, sems = refs[:count], refs[-1 - len(keys) : -1], refs[-1]
    copies = []
    for piece, names in zip(pieces, keys):
        rows = piece.shape[1]
        for i, key in enumerate(names):
            where, half = place_of(here_ref, key, rows)
            at = 0
            for value in values:
                width = value.shape[1] // 2
                column = half * width
                if len(key) == 4:
                    column = pl.multiple_of(column, LANES)
                column = pl.ds(column, width)
                copies.append((value.at[where, column], piece.at[i, :, pl.ds(at, width)]))
                at += width
    run_copies([pltpu.make_async_copy(a, b, sems.at[i]) for i, (a, b) in enumerate(copies)])


def split(values, keys, here, deps):
    rows, width = values[0].shape[0] // 16, sum(v.shape[1] for v in values) // 2
    kind = values[0].dtype
    size = sum(v.size for v in values)
    return pl.pallas_call(
        functools.partial(split_kernel, keys=keys, count=len(values)),
        out_shape=[jax.ShapeDtypeStruct((len(names), rows, width), kind) for names in keys],
        in_specs=[SMEM] + [VMEM] * len(values) + [ANY] * len(deps),
        out_specs=[ANY] * len(keys),
        scratch_shapes=[pltpu.SemaphoreType.DMA((32 * len(values),))],
        compiler_params=pltpu.CompilerParams(vmem_limit_bytes=2 * MIB),
        cost_estimate=pl.CostEstimate(flops=0, bytes_accessed=4 * size, transcendentals=0),
        name="split",
    )(here, *values, *deps)


def order_kernel(*refs):
    refs[-1][0, 0] = 0.0


def after(grid, *trees):
    if not grid.fast:
        return 0.0
    leaves = jax.tree.leaves(trees)
    return pl.pallas_call(
        order_kernel,
        out_shape=jax.ShapeDtypeStruct((1, 1), F32),
        in_specs=[ANY] * len(leaves),
        out_specs=SMEM,
        compiler_params=pltpu.CompilerParams(vmem_limit_bytes=MIB // 4),
        name="order",
    )(*leaves).reshape(())


def halves_of(parts, extra, x):
    out = []
    for place in (x, 1 - x):
        row = [
            lax.dynamic_slice_in_dim(p, place * (p.shape[1] // 2), p.shape[1] // 2, axis=1)
            for p in parts
        ]
        out.append(jnp.concatenate(row + ([extra] if extra is not None else []), axis=1))
    return out


def core_keys(keys):
    return [(1,) + key[1:] for key in keys]


class Spread:
    def __init__(self, grid, value):
        self.grid, self.value = grid, value
        self.names = ["x", "core", "y", "z1", "z2"]
        self.other = None
        if not grid.fast:
            self.value = lax.all_gather(value, ("dp", "rep"), axis=0, tiled=True)
            self.names = []

    def absorb(self, order=0.0):
        if self.other is None:
            return
        name = self.names.pop(0)
        if name == "x":
            upper = lax.axis_index("rep") > 0
        else:
            upper = (lax.axis_index("dp") & self.grid.bits[name]) > 0
        low = jnp.where(upper, self.other, self.value)
        high = jnp.where(upper, self.value, self.other)
        self.value, self.other = jnp.concatenate([low, high], axis=0), None
        self.value = plus(self.value, order)

    def step(self, order=0.0):
        self.absorb(order)
        if self.names:
            self.other = self.grid.flip(self.value, self.names[0])
            self.held = [self.other]


class Total:
    def __init__(self, grid, value):
        self.grid, self.parts = grid, [value]
        self.names = ["x", "core", "y", "z1", "z2"]
        if not grid.fast:
            self.parts, self.names = [lax.psum(value, ("dp", "rep"))], []

    def step(self, order=0.0):
        value = sum(self.parts[1:], self.parts[0])
        self.parts = [plus(value, order)]
        if self.names:
            self.parts.append(self.grid.flip(self.parts[0], self.names.pop(0)))
        self.held = self.parts[1:]

    def finish(self):
        while self.names:
            self.step()
        return sum(self.parts[1:], self.parts[0])


def plus(value, order):
    return value if isinstance(order, float) else (value.astype(F32) + order).astype(value.dtype)


def sums_kernel(order_ref, *refs, plan):
    zero = order_ref[0, 0]
    refs[-1][0, 0] = zero
    for out_ref, terms in zip(refs[-1 - len(plan) : -1], plan):
        at = 0
        for size, parts in terms:
            for i in range(size):
                total = zero
                for source, first in parts:
                    total = total + refs[source][first + i].astype(F32)
                out_ref[at + i] = total.astype(out_ref.dtype)
            at += size


def sums(order, arrays, plan, deps):
    deps = jax.tree.leaves(deps)
    shapes = [(sum(size for size, _ in terms),) + arrays[0].shape[1:] for terms in plan]
    size = sum(a * b * c for a, b, c in shapes)
    return pl.pallas_call(
        functools.partial(sums_kernel, plan=plan),
        out_shape=[jax.ShapeDtypeStruct(shape, BF16) for shape in shapes]
        + [jax.ShapeDtypeStruct((1, 1), F32)],
        in_specs=[SMEM] + [VMEM] * len(arrays) + [ANY] * len(deps),
        out_specs=[VMEM] * len(shapes) + [SMEM],
        compiler_params=pltpu.CompilerParams(vmem_limit_bytes=8 * MIB),
        cost_estimate=pl.CostEstimate(flops=2 * size, bytes_accessed=6 * size, transcendentals=0),
        name="sums",
    )(jnp.reshape(jnp.asarray(order, F32), (1, 1)), *arrays, *deps)


class Scatter:
    def __init__(self, grid, here):
        self.grid, self.here, self.stage, self.held, self.sent = grid, here, 0, [], []
        self.far, self.token = [], 0.0

    def start(self, grads, deps=()):
        self.widths = [g.shape[1] for g in grads]
        if not self.grid.fast:
            parts = [
                lax.psum_scatter(g.astype(F32), "dp", scatter_dimension=0, tiled=True)
                for g in grads
            ]
            self.result = [lax.psum(p, "rep") for p in parts]
            return
        keys = [
            [(c, y, z, h) for y, h in ((1, 1), (0, 1), (1, 0), (0, 0)) for z in range(4)]
            for c in range(2)
        ]
        self.token = 0.0
        self.near, self.far = split(grads, keys, self.here, deps)
        self.held = [self.far]

    def step(self, order=0.0, deps=()):
        if not self.grid.fast:
            return
        flip = self.grid.flip
        self.stage += 1
        if self.stage == 1:
            self.held = [flip(self.far, "core")]
            return
        if self.stage == 2:
            plan = [[(n, [(0, at), (1, at)])] for n, at in ((2, 0), (2, 2), (4, 4), (4, 8), (4, 12))]
            low, high, self.x, self.y, self.own, token = sums(
                order, [self.near, *self.held], plan, deps
            )
            self.sent, self.held = [low, high], [flip(low, "x"), flip(high, "y")]
        elif self.stage == 3:
            plan = [[(2, [(0, 0)]), (2, [(0, 2), (3, 0)])], [(2, [(1, 0), (2, 0)]), (2, [(1, 2)])]]
            to_x, to_y, token = sums(order, [self.x, self.y, *self.held], plan, deps)
            self.sent, self.held = [to_x, to_y], [flip(to_x, "x"), flip(to_y, "y")]
        elif self.stage == 4:
            plan = [[(2, [(0, at), (1, at), (2, at)])] for at in (0, 2)]
            self.low, high, token = sums(order, [self.own, *self.held], plan, deps)
            self.sent, self.held = [high], [flip(high, "z2")]
        elif self.stage == 5:
            plan = [[(1, [(0, at), (1, at)])] for at in (0, 1)]
            self.low, high, token = sums(order, [self.low, *self.held], plan, deps)
            self.sent, self.held = [high], [flip(high, "z1")]
        elif self.stage == 6:
            plan = [[(1, [(0, 0), (1, 0)])]]
            self.low, token = sums(order, [self.low, *self.held], plan, deps)
            self.sent, self.held = [self.low], [flip(self.low, "x")]
        self.token = token.reshape(())

    def finish(self):
        if not self.grid.fast:
            return self.result
        while self.stage < 6:
            self.step()
        value, other = self.low[0], self.held[0][0]
        first = self.here[1] == 0
        left, right = jnp.where(first, value, other), jnp.where(first, other, value)
        out, at = [], 0
        for width in self.widths:
            cut = slice(at, at + width // 2)
            out.append(jnp.concatenate([left[:, cut], right[:, cut]], axis=1).astype(F32))
            at += width // 2
        return out


def mm(left, right):
    return jnp.dot(left, right, preferred_element_type=F32)


def mm_left(left, right):
    return lax.dot_general(left, right, (((0,), (0,)), ((), ())), preferred_element_type=F32)


def mm_back(left, right):
    return lax.dot_general(left, right, (((1,), (1,)), ((), ())), preferred_element_type=F32)


def row_total(values, order=0.0):
    return mm(plus(jnp.ones((8, values.shape[0]), BF16), order), values)[0]


def normal_parts(v):
    phi = 0.5 + 0.5 * lax.erf(v * INV_SQRT2)
    return phi, jnp.exp(-0.5 * v * v) * INV_SQRT_2PI


def norm_parts(v):
    mean_val = jnp.mean(v, axis=-1, keepdims=True)
    centred = v - mean_val
    variance = jnp.mean(centred * centred, axis=-1, keepdims=True)
    scale = lax.rsqrt(variance + 1e-05)
    return centred * scale, scale


def norm_back(grad, unit, scale, gain):
    inner = grad * gain
    mean_one = jnp.mean(inner, axis=-1, keepdims=True)
    mean_two = jnp.mean(inner * unit, axis=-1, keepdims=True)
    return (inner - mean_one - unit * mean_two) * scale


def two_heads(t, first):
    zero = jnp.zeros_like(t)
    return jnp.concatenate([jnp.where(first, t, zero), jnp.where(first, zero, t)], axis=0)

def attn_kernel(len_ref, qkv_ref, *refs, scale, n, pairs, many):
    c_ref, total_ref = refs[-2:]
    width = pairs * LANES
    q_ref, k_ref, v_ref = [qkv_ref.at[:, pl.ds(i * width, width)] for i in range(3)]
    lane = lax.broadcasted_iota(jnp.int32, (1, 2 * n), 1) % n
    first = lax.broadcasted_iota(jnp.int32, (n, LANES), 1) < LANES // 2
    spot = lax.broadcasted_iota(jnp.int32, (n, LANES), 1)
    for i in range(many):
        rows = slice(i * n, (i + 1) * n)
        length = len_ref[pl.program_id(0) * many + i]
        totals = jnp.zeros((n, LANES), F32)
        for pair in range(pairs):
            at = slice(pair * LANES, (pair + 1) * LANES)
            q = q_ref[rows, at] * scale
            s = mm_back(q, two_heads(k_ref[rows, at], first))
            s = jnp.where(lane < length, s, -1000000000.0)
            parts = []
            for h in range(2):
                part = s[:, h * n : (h + 1) * n]
                top = jnp.max(part, axis=-1, keepdims=True)
                part = jnp.exp(part - top)
                total = jnp.sum(part, axis=-1, keepdims=True)
                parts.append((part * (1.0 / total)).astype(BF16))
                totals = jnp.where(spot == 2 * pair + h, top + jnp.log(total), totals)
            p = jnp.concatenate(parts, axis=1)
            c_ref[rows, at] = mm(p, two_heads(v_ref[rows, at], first)).astype(BF16)
        total_ref[i] = totals.T[: total_ref.shape[1]]

def attention(qkv, lengths, deps, n, heads):
    rows, width = qkv.shape[0], qkv.shape[1] // 3
    count, many = rows // n, 2
    scale = 1.0 / math.sqrt(width // heads)
    block = pl.BlockSpec((n * many, width), lambda i: (i, 0))
    lines = 16
    return pl.pallas_call(
        functools.partial(attn_kernel, scale=scale, n=n, pairs=heads // 2, many=many),
        grid=(count // many,),
        in_specs=[SMEM, pl.BlockSpec((n * many, 3 * width), lambda i: (i, 0))] + [ANY] * len(deps),
        out_specs=[block, pl.BlockSpec((many, lines, n), lambda i: (i, 0, 0))],
        out_shape=[jax.ShapeDtypeStruct((rows, width), BF16), jax.ShapeDtypeStruct((count, lines, n), F32)],
        compiler_params=pltpu.CompilerParams(vmem_limit_bytes=16 * MIB),
        cost_estimate=pl.CostEstimate(flops=8 * rows * n * width, bytes_accessed=8 * rows * width, transcendentals=rows * n * heads),
        name="attention",
    )(lengths, qkv, *deps)

def attn_back_kernel(len_ref, total_ref, qkv_ref, d_ref, *refs, scale, n, pairs, many):
    width = pairs * LANES
    q_ref, k_ref, v_ref = [qkv_ref.at[:, pl.ds(i * width, width)] for i in range(3)]
    dq_ref, dk_ref, dv_ref = [refs[-1].at[:, pl.ds(i * width, width)] for i in range(3)]
    row = lax.broadcasted_iota(jnp.int32, (2 * n, n), 0) % n
    first = lax.broadcasted_iota(jnp.int32, (n, LANES), 1) < LANES // 2
    for i in range(many):
        rows = slice(i * n, (i + 1) * n)
        length = len_ref[pl.program_id(0) * many + i]
        valid = row < length
        for pair in range(pairs):
            at = slice(pair * LANES, (pair + 1) * LANES)
            q, k, v, d = q_ref[rows, at] * scale, k_ref[rows, at] * scale, v_ref[rows, at], d_ref[rows, at]
            kk = two_heads(k_ref[rows, at], first)
            s = jnp.where(valid, mm_back(kk, q), -1000000000.0)
            dp = mm_back(two_heads(v, first), d)
            ps, ds = [], []
            for h in range(2):
                part = slice(h * n, (h + 1) * n)
                p = jnp.exp(s[part] - total_ref[i, 2 * pair + h : 2 * pair + h + 1, :])
                t = p * dp[part]
                ds.append((t - p * jnp.sum(t, axis=0, keepdims=True)).astype(BF16))
                ps.append(p.astype(BF16))
            dv_ref[rows, at] = mm(jnp.concatenate(ps, axis=1), two_heads(d, first)).astype(BF16)
            dk_ref[rows, at] = mm(jnp.concatenate(ds, axis=1), two_heads(q, first)).astype(BF16)
            dq_ref[rows, at] = mm_left(jnp.concatenate(ds, axis=0), two_heads(k, first)).astype(BF16)

def attention_back(qkv, d, totals, lengths, deps, n, heads):
    rows, width = d.shape
    count, many = rows // n, 2
    scale = 1.0 / math.sqrt(width // heads)
    block = pl.BlockSpec((n * many, width), lambda i: (i, 0))
    wide = pl.BlockSpec((n * many, 3 * width), lambda i: (i, 0))
    return pl.pallas_call(
        functools.partial(attn_back_kernel, scale=scale, n=n, pairs=heads // 2, many=many),
        grid=(count // many,),
        in_specs=[SMEM, pl.BlockSpec((many,) + totals.shape[1:], lambda i: (i, 0, 0)), wide, block]
        + [ANY] * len(deps),
        out_specs=wide,
        out_shape=jax.ShapeDtypeStruct((rows, 3 * width), BF16),
        compiler_params=pltpu.CompilerParams(vmem_limit_bytes=16 * MIB),
        cost_estimate=pl.CostEstimate(flops=20 * rows * n * width, bytes_accessed=14 * rows * width, transcendentals=rows * n * heads),
        name="attention_back",
    )(lengths, totals, qkv, d, *deps)


def per_device(
    grid,
    passages,
    lengths,
    queries,
    positives,
    out_grad,
    w_query,
    b_query,
    w_key,
    w_value,
    b_value,
    w_out,
    b_out,
    norm1_gain,
    norm1_bias,
    w_up,
    b_up,
    w_down,
    b_down,
    norm2_gain,
    norm2_bias,
):
    steps, count, length, width = passages.shape
    total = steps * count
    rows = total * length
    inv_width = 1.0 / math.sqrt(width)
    dp = grid.dp
    dp_index, rep_index = lax.axis_index("dp"), lax.axis_index("rep")
    here = jnp.stack([dp_index, rep_index]).astype(jnp.int32)

    block = w_query.shape[0]
    vectors = (b_query, b_value, b_out, norm1_gain, norm1_bias, b_down, norm2_gain, norm2_bias)
    spread = b_up.shape[0] // block
    columns = [v[:, None] for v in vectors] + [b_up.reshape(spread, block).T]
    columns = jnp.concatenate(columns, axis=1)
    columns = jnp.pad(columns, ((0, 0), (0, LANES - columns.shape[1])))
    tokens = passages.reshape(rows, width)
    w_qkv = jnp.concatenate([w_query, w_key, w_value], axis=1)
    digits = jnp.stack([positives.T // 256, positives.T % 256], axis=-1).astype(BF16)
    payload = jnp.concatenate(
        [
            jnp.moveaxis(queries, 0, 1).reshape(total, width),
            jnp.pad(digits.reshape(total, 2), ((0, 0), (0, LANES - 2))),
        ],
        axis=-1,
    )
    spans = lengths.reshape(total)
    if grid.fast:
        flip = grid.flip
        mine, twin = halves_of((w_qkv,), columns, here[1])
        own, mine = jnp.stack([mine, twin]), mine[None]
        second = halves_of((w_out, w_up), None, here[1])[0][None]
        third = halves_of((w_down,), None, here[1])[0]
        across, h1, h2, h3 = flip(own, "y"), flip(mine, "z1"), flip(mine, "z2"), flip(mine, "z3")
        s1 = flip(second, "z1")
        order = after(grid, across, h1, h2, h3)
        line = plus(jnp.concatenate([h1, h2, h3]), order)
        line_y, line_x = flip(line, "y"), flip(line, "x")
        second = plus(jnp.concatenate([second, s1]), order)
        second_far = flip(second, "z2")
        cores = [flip(own, "core"), flip(across, "core"), flip(line, "core")]
        order = after(grid, line_y, line_x, second)
        cross_x = flip(plus(line_y[:2], order), "x")
        cross_y = flip(plus(line_x[2:], order), "y")
        cores += [flip(line_y, "core"), flip(line_x, "core")]
        order = after(grid, cross_x, cross_y)
        second = plus(second, order)
        second_y, second_x = flip(second, "y"), flip(second, "x")
        cores += [flip(cross_x, "core"), flip(cross_y, "core")]
        bag = [
            (own, [(0, 0, 0, 0), (0, 0, 0, 1)]),
            (across, [(0, 1, 0, 0), (0, 1, 0, 1)]),
            (line, [(0, 0, z, 0) for z in (1, 2, 3)]),
            (line_y, [(0, 1, z, 0) for z in (1, 2, 3)]),
            (line_x, [(0, 0, z, 1) for z in (1, 2, 3)]),
            (cross_x, [(0, 1, z, 1) for z in (1, 2)]),
            (cross_y, [(0, 1, 3, 1)]),
        ]
        bag += [(v, core_keys(keys)) for v, (_, keys) in zip(cores, bag)]
        weight_qkv, table = join(bag, [3 * width // 2], LANES, here)
        order = after(grid, table)
        high = plus(second_far, order)
        high_y, high_x = flip(high, "y"), flip(high, "x")
        second_cross = flip(plus(second_y, order), "x")
        third = grid.share(third, "z", order)
        order = after(grid, high)
    else:
        weight_qkv, table, weight_out, weight_up, weight_down = [
            lax.all_gather(w, "dp", axis=0, tiled=True)
            for w in (w_qkv, columns, w_out, w_up, w_down)
        ]
        order = 0.0
    table = table[:, :16].T.astype(F32)
    (bias_q, bias_v, bias_out, gain_one, shift_one, bias_down, gain_two, shift_two) = [
        table[i] for i in range(8)
    ]
    bias_up = jnp.transpose(
        table[8 : 8 + spread].reshape(spread, dp, block), (1, 0, 2)
    ).reshape(-1)
    bias_qkv = jnp.concatenate([bias_q, jnp.zeros_like(bias_q), bias_v])
    qkv = plus(mm(tokens, weight_qkv) + bias_qkv, order).astype(BF16)
    z_keys = [[(0, y, z, h) for z in range(4)] for y, h in ((0, 0), (1, 0), (0, 1), (1, 1))]

    def bag_of(blocks):
        cores = [flip(v, "core") for v, _ in blocks]
        return blocks + [(v, core_keys(keys)) for v, (_, keys) in zip(cores, blocks)]

    low_keys = [keys[:2] for keys in z_keys]
    high_keys = [keys[2:] for keys in z_keys]
    if grid.fast:
        order = after(grid, qkv, high_x, high_y, second_x)
        high_cross = flip(plus(high_x, order), "y")
        attention_order = [jnp.full((8, LANES), order, F32)]
    else:
        attention_order = []
    context, log_total = attention(qkv, spans, attention_order, length, H)
    if grid.fast:
        order = after(grid, context, high_cross, second_cross, third)
        third = grid.share(third, "xy", order)
        order = after(grid, context, high_cross)
        blocks = (second, second_y, second_x, second_cross)
        blocks = list(zip(blocks, low_keys)) + list(zip((high, high_y, high_x, high_cross), high_keys))
        weight_out, weight_up = join(bag_of(blocks), [width // 2, w_up.shape[1] // 2], 0, here)
        order = after(grid, weight_out)
    sum_one = tokens.astype(F32) + mm(context, weight_out) + bias_out
    unit_one, scale_one = norm_parts(sum_one)
    hidden = unit_one * gain_one + shift_one
    hidden_low = hidden.astype(BF16)
    pre = mm(hidden_low, weight_up) + bias_up
    phi, density = normal_parts(pre)
    gelu_low = (pre * phi).astype(BF16)
    slope = (phi + pre * density).astype(BF16)
    if grid.fast:
        order = after(grid, gelu_low, third)
        third = third.reshape((16,) + third.shape[2:])
        bag = [(third, square_keys(0)), (flip(third, "core"), square_keys(1))]
        (weight_down,) = join(bag, [width // 2], 0, here)
    sum_two = plus(hidden, order) + mm(gelu_low, weight_down) + bias_down
    unit_two, scale_two = norm_parts(sum_two)
    result = (unit_two * gain_two + shift_two).reshape(steps, count, length, width)
    output = result.astype(BF16)

    def starts(value):
        return value.reshape(total, length, -1)[:, 0]

    def put_starts(value, part):
        blocks = value.reshape(total, length, -1)
        return lax.dynamic_update_slice(blocks, part[:, None], (0, 0, 0)).reshape(value.shape)

    cls = jnp.moveaxis(output[:, :, 0, :], 0, 1).reshape(total, width)
    if grid.fast:
        cls = grid.share(jnp.concatenate([cls, payload], axis=1), "all")
    else:
        cls = jnp.concatenate([cls, payload], axis=1)
        cls = lax.all_gather(cls, ("dp", "rep"), axis=0, tiled=True)
    grad_out = out_grad.reshape(rows, width).astype(F32)
    grad_two = norm_back(grad_out, unit_two, scale_two, gain_two)
    down_low = grad_two.astype(BF16)
    later = (jnp.arange(rows) % length > 0)[:, None]
    grad_gain_two = jnp.sum(grad_out * unit_two, axis=0)
    grad_shift_two = jnp.sum(grad_out, axis=0)
    grad_b_down = jnp.sum(jnp.where(later, down_low.astype(F32), 0.0), axis=0)
    parts = [slice(0, w_up.shape[1] // 2), slice(w_up.shape[1] // 2, w_up.shape[1])]

    def up_back(grad, part, by):
        return mm_back(grad, weight_down[part]) * by[:, part].astype(F32)

    up_lows = [up_back(down_low, part, slope).astype(BF16) for part in parts]
    order = after(grid, cls, up_lows)

    cls = plus(cls.reshape(-1, steps, 2 * width + LANES), order)
    all_cls, all_queries = cls[:, :, :width], cls[:, :, width : 2 * width]
    digits = cls[:, :, 2 * width : 2 * width + 2].astype(jnp.int32)
    all_positives = digits[:, :, 0] * 256 + digits[:, :, 1]
    first = (dp_index * grid.rep + rep_index) * count
    logits = jnp.einsum("qmd,pmd->mqp", all_queries, all_cls, preferred_element_type=F32)
    logits = logits * inv_width
    query_total = jax.nn.logsumexp(logits, axis=-1)
    passages_all = all_cls.shape[0]
    mine = lax.dynamic_slice_in_dim(logits, first, count, axis=1)
    mine_total = lax.dynamic_slice_in_dim(query_total, first, count, axis=1)
    onehot = (positives[:, :, None] == jnp.arange(passages_all)[None, None, :]).astype(F32)
    query_loss = mine_total - jnp.sum(mine * onehot, axis=-1)
    mine_grad = (jnp.exp(mine - mine_total[:, :, None]) - onehot) * inv_width
    queries_grad = jnp.einsum(
        "mqp,pmd->mqd", mine_grad.astype(BF16), all_cls, preferred_element_type=F32
    )
    column = lax.dynamic_slice_in_dim(logits, first, count, axis=2)
    hit = (all_positives.T[:, :, None] == (first + jnp.arange(count))[None, None, :]).astype(F32)
    column_grad = (jnp.exp(column - query_total[:, :, None]) - hit) * inv_width
    cls_grad = jnp.einsum(
        "mqp,qmd->mpd", column_grad.astype(BF16), all_queries, preferred_element_type=F32
    )

    grad_start = cls_grad.reshape(total, width)
    unit_start = starts(unit_two)
    grad_gain_two = grad_gain_two + jnp.sum(grad_start * unit_start, axis=0)
    grad_shift_two = grad_shift_two + jnp.sum(grad_start, axis=0)
    grad_start = grad_start + starts(out_grad.reshape(rows, width)).astype(F32)
    grad_start = norm_back(grad_start, unit_start, starts(scale_two), gain_two)
    down_start = grad_start.astype(BF16)
    up_starts = [up_back(down_start, part, starts(slope)).astype(BF16) for part in parts]
    grad_b_down = grad_b_down + row_total(down_start)
    grad_two = put_starts(grad_two, grad_start)
    down_low = put_starts(down_low, down_start)
    up_lows = [put_starts(u, start) for u, start in zip(up_lows, up_starts)]

    down_sum, up_sum, last_sum = [Scatter(grid, here) for _ in range(3)]
    down_sum.start([mm_left(gelu_low, down_low).astype(BF16)])
    order = after(grid, down_sum.held)
    down_sum.step(order)
    grads_up = [plus(mm_left(hidden_low, up_lows[0]), order).astype(BF16)]
    down_sum.step(deps=[grads_up])
    order = down_sum.token
    grads_up.append(plus(mm_left(hidden_low, up_lows[1]), order).astype(BF16))
    up_sum.start(grads_up, down_sum.held)
    up_sum.step()
    down_sum.step(deps=[up_sum.far])
    order = down_sum.token
    grad_hidden = plus(grad_two + mm_back(up_lows[0], weight_up[:, parts[0]]), order)
    up_sum.step(deps=[grad_hidden])
    order = up_sum.token
    grad_hidden = plus(grad_hidden + mm_back(up_lows[1], weight_up[:, parts[1]]), order)
    grad_gain_one = jnp.sum(grad_hidden * unit_one, axis=0)
    grad_shift_one = jnp.sum(grad_hidden, axis=0)
    grad_one = norm_back(grad_hidden, unit_one, scale_one, gain_one)
    attn_low = grad_one.astype(BF16)
    grad_w_out = mm_left(context, attn_low).astype(BF16)
    context_grad = mm_back(attn_low, weight_out).astype(BF16)
    down_sum.step(deps=[up_sum.held, attn_low])
    up_sum.step(down_sum.token)
    order = up_sum.token
    qkv_low = attention_back(
        qkv, context_grad, log_total, spans, [jnp.full((8, LANES), order, F32)], length, H
    )
    down_sum.step(deps=[up_sum.held, qkv_low])
    up_sum.step(down_sum.token)
    order = up_sum.token

    grad_w_qkv = plus(mm_left(tokens, qkv_low), order).astype(BF16)
    last_sum.start([grad_w_out, grad_w_qkv])
    last_sum.step()
    order = after(grid, last_sum.far)
    grad_b_qkv = row_total(qkv_low, order)
    grad_b_query, grad_b_value = grad_b_qkv[:width], grad_b_qkv[2 * width :]
    grad_b_out = row_total(attn_low, order)
    grad_b_up = jnp.concatenate([row_total(u, order) for u in up_lows])
    grads = (
        grad_b_query,
        grad_b_value,
        grad_b_out,
        grad_gain_one,
        grad_shift_one,
        grad_b_down,
        grad_gain_two,
        grad_shift_two,
    )
    grads = jnp.concatenate([jnp.stack(grads), grad_b_up.reshape(spread, width)])

    grads = Total(grid, grads)
    up_sum.step(order)
    last_sum.step(deps=[grads.parts])
    order = last_sum.token
    grads.step(order)
    last_sum.step(deps=[grads.held])
    order = last_sum.token
    grads.step(order)
    input_grad = plus(grad_one + mm_back(qkv_low, weight_qkv), order)
    last_sum.step(deps=[input_grad, grads.held])
    order = last_sum.token
    grads.step(order)
    last_sum.step(deps=[input_grad, up_sum.held, grads.held])
    order = last_sum.token
    up_sum.step(order)
    down_sum.step(order)
    grads.step(order)
    (shard_w_down,) = down_sum.finish()
    shard_w_up = jnp.concatenate(up_sum.finish(), axis=1)
    shard_w_out, shard_w_qkv = last_sum.finish()
    shard_w_query, shard_w_key, shard_w_value = jnp.split(shard_w_qkv, 3, axis=1)
    grads = grads.finish()
    low = lax.dynamic_slice_in_dim(grads[:8], dp_index * block, block, axis=1)
    s_b_up = lax.dynamic_slice_in_dim(
        grads[8:].reshape(-1), dp_index * spread * block, spread * block, axis=0
    )
    (s_b_q, s_b_v, s_b_out, s_gain1, s_shift1, s_b_down, s_gain2, s_shift2) = [
        low[i] for i in range(8)
    ]
    return (
        output,
        query_loss,
        input_grad.reshape(steps, count, length, width),
        queries_grad,
        cls_grad,
        shard_w_query,
        s_b_q,
        shard_w_key,
        shard_w_value,
        s_b_v,
        shard_w_out,
        s_b_out,
        s_gain1,
        s_shift1,
        shard_w_up,
        s_b_up,
        shard_w_down,
        s_b_down,
        s_gain2,
        s_shift2,
    )


def solution(mesh):
    both = ("dp", "rep")
    matrix, vector = P("dp", None), P("dp")
    weights = (
        matrix, vector, matrix, matrix, vector, matrix, vector, vector, vector,
        matrix, vector, matrix, vector, vector, vector,
    )
    grid = Grid(mesh.shape["dp"], mesh.shape["rep"], 768 // mesh.shape["dp"])
    wide = P(None, both, None, None)
    return jax.shard_map(
        functools.partial(per_device, grid),
        mesh=mesh,
        in_specs=(wide, P(None, both), P(None, both, None), P(None, both), wide) + weights,
        out_specs=(wide, P(None, both), wide, P(None, both, None), P(None, both, None)) + weights,
        check_vma=False,
    )
```

```python
import functools
import math

import jax
import jax.numpy as jnp
from jax import lax
from jax.experimental import pallas as pl
from jax.experimental.pallas import tpu as pltpu
from jax.sharding import PartitionSpec as P

H = 12
F32 = jnp.float32
BF16 = jnp.bfloat16
INV_SQRT2 = 1.0 / math.sqrt(2.0)
INV_SQRT_2PI = 1.0 / math.sqrt(2.0 * math.pi)


ANY = pl.BlockSpec(memory_space=pl.ANY)
SMEM = pl.BlockSpec(memory_space=pltpu.SMEM)
VMEM = pl.BlockSpec(memory_space=pltpu.VMEM)
MIB = 2**20
LANES = 128


class Grid:
    def __init__(self, dp, rep, rows):
        self.dp, self.rep = dp, rep
        self.fast = dp == 16 and rep == 2 and rows % 16 == 0
        self.bits = {"core": 1, "y": 2, "z1": 4, "z2": 8, "z3": 12}

        place = [
            (((z * 2 + y) * 2 + c) * 2 + x, (z, y, c, x))
            for z in range(4)
            for y in range(2)
            for c in range(2)
            for x in range(2)
        ]
        lines, squares = {}, {}
        for i, (z, y, c, x) in place:
            lines.setdefault((y, c, x), []).append(i)
            squares.setdefault((z, c), []).append(i)
        self.groups = {"z": list(lines.values()), "xy": list(squares.values()), "all": None}

    def exchange(self, value, name):
        return lax.all_to_all(
            value, ("dp", "rep"), 0, 0, axis_index_groups=self.groups[name], tiled=True
        )

    def share(self, value, name, order=0.0):
        count = self.dp * self.rep if name == "all" else 4
        value = plus(jnp.broadcast_to(value[None], (count,) + value.shape), order)
        return self.exchange(value, name)

    def flip(self, value, name):
        if name == "x":
            return lax.ppermute(value, "rep", [(i, i ^ 1) for i in range(self.rep)])
        bit = self.bits[name]
        return lax.ppermute(value, "dp", [(i, i ^ bit) for i in range(self.dp)])


def run_copies(copies):
    for copy in copies:
        copy.start()
    for copy in copies:
        copy.wait()


def place_of(here_ref, key, rows):
    core, y, z, half = key[:4]
    if len(key) > 4:
        place = z * 4 + y * 2 + ((here_ref[0] & 1) ^ core)
        return pl.ds(pl.multiple_of(place * rows, 16), rows), half
    row = pl.multiple_of((here_ref[0] ^ (z * 4 + y * 2 + core)) * rows, 16)
    return pl.ds(row, rows), here_ref[1] ^ half


def square_keys(core):
    return [(core, y, z, x, True) for y in range(2) for x in range(2) for z in range(4)]


def join_kernel(here_ref, *refs, keys, widths, extra):
    count = len(keys)
    pieces, outs, sems = refs[:count], refs[count:-1], refs[-1]
    copies = []
    for piece, names in zip(pieces, keys):
        for i, key in enumerate(names):
            rows = piece.shape[1]
            where, half = place_of(here_ref, key, rows)
            at = 0
            for out, width in zip(outs, widths):
                column = half * width
                if len(key) == 4:
                    column = pl.multiple_of(column, LANES)
                column = pl.ds(column, width)
                copies.append((piece.at[i, :, pl.ds(at, width)], out.at[where, column]))
                at += width
            if extra and key[3] == 0:
                copies.append((piece.at[i, :, pl.ds(at, extra)], outs[-1].at[where, :]))
    run_copies([pltpu.make_async_copy(a, b, sems.at[i]) for i, (a, b) in enumerate(copies)])


def join(bag, widths, extra, here):
    arrays, keys = zip(*bag)
    rows = arrays[0].shape[1]
    shapes = [(16 * rows, 2 * width) for width in widths] + ([(16 * rows, extra)] if extra else [])
    copies = 32 * len(widths) + (16 if extra else 0)
    size = sum(a * b for a, b in shapes)
    return pl.pallas_call(
        functools.partial(join_kernel, keys=keys, widths=widths, extra=extra),
        out_shape=[jax.ShapeDtypeStruct(shape, arrays[0].dtype) for shape in shapes],
        in_specs=[SMEM] + [ANY] * len(arrays),
        out_specs=[VMEM] * len(shapes),
        scratch_shapes=[pltpu.SemaphoreType.DMA((copies,))],
        compiler_params=pltpu.CompilerParams(vmem_limit_bytes=2 * MIB),
        cost_estimate=pl.CostEstimate(flops=0, bytes_accessed=4 * size, transcendentals=0),
        name="join",
    )(here, *arrays)


def split_kernel(here_ref, *refs, keys, count):
    values, pieces, sems = refs[:count], refs[-1 - len(keys) : -1], refs[-1]
    copies = []
    for piece, names in zip(pieces, keys):
        rows = piece.shape[1]
        for i, key in enumerate(names):
            where, half = place_of(here_ref, key, rows)
            at = 0
            for value in values:
                width = value.shape[1] // 2
                column = half * width
                if len(key) == 4:
                    column = pl.multiple_of(column, LANES)
                column = pl.ds(column, width)
                copies.append((value.at[where, column], piece.at[i, :, pl.ds(at, width)]))
                at += width
    run_copies([pltpu.make_async_copy(a, b, sems.at[i]) for i, (a, b) in enumerate(copies)])


def split(values, keys, here, deps):
    rows, width = values[0].shape[0] // 16, sum(v.shape[1] for v in values) // 2
    kind = values[0].dtype
    size = sum(v.size for v in values)
    return pl.pallas_call(
        functools.partial(split_kernel, keys=keys, count=len(values)),
        out_shape=[jax.ShapeDtypeStruct((len(names), rows, width), kind) for names in keys],
        in_specs=[SMEM] + [VMEM] * len(values) + [ANY] * len(deps),
        out_specs=[ANY] * len(keys),
        scratch_shapes=[pltpu.SemaphoreType.DMA((32 * len(values),))],
        compiler_params=pltpu.CompilerParams(vmem_limit_bytes=2 * MIB),
        cost_estimate=pl.CostEstimate(flops=0, bytes_accessed=4 * size, transcendentals=0),
        name="split",
    )(here, *values, *deps)


def order_kernel(*refs):
    refs[-1][0, 0] = 0.0


def after(grid, *trees):
    if not grid.fast:
        return 0.0
    leaves = jax.tree.leaves(trees)
    return pl.pallas_call(
        order_kernel,
        out_shape=jax.ShapeDtypeStruct((1, 1), F32),
        in_specs=[ANY] * len(leaves),
        out_specs=SMEM,
        compiler_params=pltpu.CompilerParams(vmem_limit_bytes=MIB // 4),
        name="order",
    )(*leaves).reshape(())


def halves_of(parts, extra, x):
    out = []
    for place in (x, 1 - x):
        row = [
            lax.dynamic_slice_in_dim(p, place * (p.shape[1] // 2), p.shape[1] // 2, axis=1)
            for p in parts
        ]
        out.append(jnp.concatenate(row + ([extra] if extra is not None else []), axis=1))
    return out


def core_keys(keys):
    return [(1,) + key[1:] for key in keys]


class Spread:
    def __init__(self, grid, value):
        self.grid, self.value = grid, value
        self.names = ["x", "core", "y", "z1", "z2"]
        self.other = None
        if not grid.fast:
            self.value = lax.all_gather(value, ("dp", "rep"), axis=0, tiled=True)
            self.names = []

    def absorb(self, order=0.0):
        if self.other is None:
            return
        name = self.names.pop(0)
        if name == "x":
            upper = lax.axis_index("rep") > 0
        else:
            upper = (lax.axis_index("dp") & self.grid.bits[name]) > 0
        low = jnp.where(upper, self.other, self.value)
        high = jnp.where(upper, self.value, self.other)
        self.value, self.other = jnp.concatenate([low, high], axis=0), None
        self.value = plus(self.value, order)

    def step(self, order=0.0):
        self.absorb(order)
        if self.names:
            self.other = self.grid.flip(self.value, self.names[0])
            self.held = [self.other]


class Total:
    def __init__(self, grid, value):
        self.grid, self.parts = grid, [value]
        self.names = ["x", "core", "y", "z1", "z2"]
        if not grid.fast:
            self.parts, self.names = [lax.psum(value, ("dp", "rep"))], []

    def step(self, order=0.0):
        value = sum(self.parts[1:], self.parts[0])
        self.parts = [plus(value, order)]
        if self.names:
            self.parts.append(self.grid.flip(self.parts[0], self.names.pop(0)))
        self.held = self.parts[1:]

    def finish(self):
        while self.names:
            self.step()
        return sum(self.parts[1:], self.parts[0])


def plus(value, order):
    return value if isinstance(order, float) else (value.astype(F32) + order).astype(value.dtype)


def sums_kernel(order_ref, *refs, plan):
    zero = order_ref[0, 0]
    refs[-1][0, 0] = zero
    for out_ref, terms in zip(refs[-1 - len(plan) : -1], plan):
        at = 0
        for size, parts in terms:
            for i in range(size):
                total = zero
                for source, first in parts:
                    total = total + refs[source][first + i].astype(F32)
                out_ref[at + i] = total.astype(out_ref.dtype)
            at += size


def sums(order, arrays, plan, deps):
    deps = jax.tree.leaves(deps)
    shapes = [(sum(size for size, _ in terms),) + arrays[0].shape[1:] for terms in plan]
    size = sum(a * b * c for a, b, c in shapes)
    return pl.pallas_call(
        functools.partial(sums_kernel, plan=plan),
        out_shape=[jax.ShapeDtypeStruct(shape, BF16) for shape in shapes]
        + [jax.ShapeDtypeStruct((1, 1), F32)],
        in_specs=[SMEM] + [VMEM] * len(arrays) + [ANY] * len(deps),
        out_specs=[VMEM] * len(shapes) + [SMEM],
        compiler_params=pltpu.CompilerParams(vmem_limit_bytes=8 * MIB),
        cost_estimate=pl.CostEstimate(flops=2 * size, bytes_accessed=6 * size, transcendentals=0),
        name="sums",
    )(jnp.reshape(jnp.asarray(order, F32), (1, 1)), *arrays, *deps)


class Scatter:
    def __init__(self, grid, here):
        self.grid, self.here, self.stage, self.held, self.sent = grid, here, 0, [], []
        self.far, self.token = [], 0.0

    def start(self, grads, deps=()):
        self.widths = [g.shape[1] for g in grads]
        if not self.grid.fast:
            parts = [
                lax.psum_scatter(g.astype(F32), "dp", scatter_dimension=0, tiled=True)
                for g in grads
            ]
            self.result = [lax.psum(p, "rep") for p in parts]
            return
        keys = [
            [(c, y, z, h) for y, h in ((1, 1), (0, 1), (1, 0), (0, 0)) for z in range(4)]
            for c in range(2)
        ]
        self.token = 0.0
        self.near, self.far = split(grads, keys, self.here, deps)
        self.held = [self.far]

    def step(self, order=0.0, deps=()):
        if not self.grid.fast:
            return
        flip = self.grid.flip
        self.stage += 1
        if self.stage == 1:
            self.held = [flip(self.far, "core")]
            return
        if self.stage == 2:
            plan = [[(n, [(0, at), (1, at)])] for n, at in ((2, 0), (2, 2), (4, 4), (4, 8), (4, 12))]
            low, high, self.x, self.y, self.own, token = sums(
                order, [self.near, *self.held], plan, deps
            )
            self.sent, self.held = [low, high], [flip(low, "x"), flip(high, "y")]
        elif self.stage == 3:
            plan = [[(2, [(0, 0)]), (2, [(0, 2), (3, 0)])], [(2, [(1, 0), (2, 0)]), (2, [(1, 2)])]]
            to_x, to_y, token = sums(order, [self.x, self.y, *self.held], plan, deps)
            self.sent, self.held = [to_x, to_y], [flip(to_x, "x"), flip(to_y, "y")]
        elif self.stage == 4:
            plan = [[(2, [(0, at), (1, at), (2, at)])] for at in (0, 2)]
            self.low, high, token = sums(order, [self.own, *self.held], plan, deps)
            self.sent, self.held = [high], [flip(high, "z2")]
        elif self.stage == 5:
            plan = [[(1, [(0, at), (1, at)])] for at in (0, 1)]
            self.low, high, token = sums(order, [self.low, *self.held], plan, deps)
            self.sent, self.held = [high], [flip(high, "z1")]
        elif self.stage == 6:
            plan = [[(1, [(0, 0), (1, 0)])]]
            self.low, token = sums(order, [self.low, *self.held], plan, deps)
            self.sent, self.held = [self.low], [flip(self.low, "x")]
        self.token = token.reshape(())

    def finish(self):
        if not self.grid.fast:
            return self.result
        while self.stage < 6:
            self.step()
        value, other = self.low[0], self.held[0][0]
        first = self.here[1] == 0
        left, right = jnp.where(first, value, other), jnp.where(first, other, value)
        out, at = [], 0
        for width in self.widths:
            cut = slice(at, at + width // 2)
            out.append(jnp.concatenate([left[:, cut], right[:, cut]], axis=1).astype(F32))
            at += width // 2
        return out


def mm(left, right):
    return jnp.dot(left, right, preferred_element_type=F32)


def mm_left(left, right):
    return lax.dot_general(left, right, (((0,), (0,)), ((), ())), preferred_element_type=F32)


def mm_back(left, right):
    return lax.dot_general(left, right, (((1,), (1,)), ((), ())), preferred_element_type=F32)


def row_total(values, order=0.0):
    return mm(plus(jnp.ones((8, values.shape[0]), BF16), order), values)[0]


def normal_parts(v):
    phi = 0.5 + 0.5 * lax.erf(v * INV_SQRT2)
    return phi, jnp.exp(-0.5 * v * v) * INV_SQRT_2PI


def norm_parts(v):
    mean_val = jnp.mean(v, axis=-1, keepdims=True)
    centred = v - mean_val
    variance = jnp.mean(centred * centred, axis=-1, keepdims=True)
    scale = lax.rsqrt(variance + 1e-05)
    return centred * scale, scale


def norm_back(grad, unit, scale, gain):
    inner = grad * gain
    mean_one = jnp.mean(inner, axis=-1, keepdims=True)
    mean_two = jnp.mean(inner * unit, axis=-1, keepdims=True)
    return (inner - mean_one - unit * mean_two) * scale


def two_heads(t, first):
    zero = jnp.zeros_like(t)
    return jnp.concatenate([jnp.where(first, t, zero), jnp.where(first, zero, t)], axis=0)

def attn_kernel(len_ref, qkv_ref, *refs, scale, n, pairs, many):
    c_ref, total_ref = refs[-2:]
    width = pairs * LANES
    q_ref, k_ref, v_ref = [qkv_ref.at[:, pl.ds(i * width, width)] for i in range(3)]
    lane = lax.broadcasted_iota(jnp.int32, (1, 2 * n), 1) % n
    first = lax.broadcasted_iota(jnp.int32, (n, LANES), 1) < LANES // 2
    spot = lax.broadcasted_iota(jnp.int32, (n, LANES), 1)
    for i in range(many):
        rows = slice(i * n, (i + 1) * n)
        length = len_ref[pl.program_id(0) * many + i]
        totals = jnp.zeros((n, LANES), F32)
        for pair in range(pairs):
            at = slice(pair * LANES, (pair + 1) * LANES)
            q = q_ref[rows, at] * scale
            s = mm_back(q, two_heads(k_ref[rows, at], first))
            s = jnp.where(lane < length, s, -1000000000.0)
            parts = []
            for h in range(2):
                part = s[:, h * n : (h + 1) * n]
                top = jnp.max(part, axis=-1, keepdims=True)
                part = jnp.exp(part - top)
                total = jnp.sum(part, axis=-1, keepdims=True)
                parts.append((part * (1.0 / total)).astype(BF16))
                totals = jnp.where(spot == 2 * pair + h, top + jnp.log(total), totals)
            p = jnp.concatenate(parts, axis=1)
            c_ref[rows, at] = mm(p, two_heads(v_ref[rows, at], first)).astype(BF16)
        total_ref[i] = totals.T[: total_ref.shape[1]]

def attention(qkv, lengths, deps, n, heads):
    rows, width = qkv.shape[0], qkv.shape[1] // 3
    count, many = rows // n, 2
    scale = 1.0 / math.sqrt(width // heads)
    block = pl.BlockSpec((n * many, width), lambda i: (i, 0))
    lines = 16
    return pl.pallas_call(
        functools.partial(attn_kernel, scale=scale, n=n, pairs=heads // 2, many=many),
        grid=(count // many,),
        in_specs=[SMEM, pl.BlockSpec((n * many, 3 * width), lambda i: (i, 0))] + [ANY] * len(deps),
        out_specs=[block, pl.BlockSpec((many, lines, n), lambda i: (i, 0, 0))],
        out_shape=[jax.ShapeDtypeStruct((rows, width), BF16), jax.ShapeDtypeStruct((count, lines, n), F32)],
        compiler_params=pltpu.CompilerParams(vmem_limit_bytes=16 * MIB),
        cost_estimate=pl.CostEstimate(flops=8 * rows * n * width, bytes_accessed=8 * rows * width, transcendentals=rows * n * heads),
        name="attention",
    )(lengths, qkv, *deps)

def attn_back_kernel(len_ref, total_ref, qkv_ref, d_ref, *refs, scale, n, pairs, many):
    width = pairs * LANES
    q_ref, k_ref, v_ref = [qkv_ref.at[:, pl.ds(i * width, width)] for i in range(3)]
    out_ref, total_out_ref = refs[-2:]
    dq_ref, dk_ref, dv_ref = [out_ref.at[:, pl.ds(i * width, width)] for i in range(3)]
    row = lax.broadcasted_iota(jnp.int32, (2 * n, n), 0) % n
    first = lax.broadcasted_iota(jnp.int32, (n, LANES), 1) < LANES // 2
    for i in range(many):
        rows = slice(i * n, (i + 1) * n)
        length = len_ref[pl.program_id(0) * many + i]
        valid = row < length
        for pair in range(pairs):
            at = slice(pair * LANES, (pair + 1) * LANES)
            q, k, v, d = q_ref[rows, at] * scale, k_ref[rows, at] * scale, v_ref[rows, at], d_ref[rows, at]
            kk = two_heads(k_ref[rows, at], first)
            s = jnp.where(valid, mm_back(kk, q), -1000000000.0)
            dp = mm_back(two_heads(v, first), d)
            ps, ds = [], []
            for h in range(2):
                part = slice(h * n, (h + 1) * n)
                p = jnp.exp(s[part] - total_ref[i, 2 * pair + h : 2 * pair + h + 1, :])
                t = p * dp[part]
                ds.append((t - p * jnp.sum(t, axis=0, keepdims=True)).astype(BF16))
                ps.append(p.astype(BF16))
            dv_ref[rows, at] = mm(jnp.concatenate(ps, axis=1), two_heads(d, first)).astype(BF16)
            dk_ref[rows, at] = mm(jnp.concatenate(ds, axis=1), two_heads(q, first)).astype(BF16)
            dq_ref[rows, at] = mm_left(jnp.concatenate(ds, axis=0), two_heads(k, first)).astype(BF16)
    term = jnp.sum(out_ref[...].astype(F32), axis=0, keepdims=True)

    @pl.when(pl.program_id(0) == 0)
    def _():
        total_out_ref[...] = term

    @pl.when(pl.program_id(0) > 0)
    def _():
        total_out_ref[...] += term


def attention_back(qkv, d, totals, lengths, deps, n, heads):
    rows, width = d.shape
    count, many = rows // n, 2
    scale = 1.0 / math.sqrt(width // heads)
    block = pl.BlockSpec((n * many, width), lambda i: (i, 0))
    wide = pl.BlockSpec((n * many, 3 * width), lambda i: (i, 0))
    return pl.pallas_call(
        functools.partial(attn_back_kernel, scale=scale, n=n, pairs=heads // 2, many=many),
        grid=(count // many,),
        in_specs=[SMEM, pl.BlockSpec((many,) + totals.shape[1:], lambda i: (i, 0, 0)), wide, block]
        + [ANY] * len(deps),
        out_specs=[wide, pl.BlockSpec((1, 3 * width), lambda i: (0, 0))],
        out_shape=[
            jax.ShapeDtypeStruct((rows, 3 * width), BF16),
            jax.ShapeDtypeStruct((1, 3 * width), F32),
        ],
        compiler_params=pltpu.CompilerParams(vmem_limit_bytes=16 * MIB),
        cost_estimate=pl.CostEstimate(flops=20 * rows * n * width, bytes_accessed=14 * rows * width, transcendentals=rows * n * heads),
        name="attention_back",
    )(lengths, totals, qkv, d, *deps)


def per_device(
    grid,
    passages,
    lengths,
    queries,
    positives,
    out_grad,
    w_query,
    b_query,
    w_key,
    w_value,
    b_value,
    w_out,
    b_out,
    norm1_gain,
    norm1_bias,
    w_up,
    b_up,
    w_down,
    b_down,
    norm2_gain,
    norm2_bias,
):
    steps, count, length, width = passages.shape
    total = steps * count
    rows = total * length
    inv_width = 1.0 / math.sqrt(width)
    dp = grid.dp
    dp_index, rep_index = lax.axis_index("dp"), lax.axis_index("rep")
    here = jnp.stack([dp_index, rep_index]).astype(jnp.int32)

    block = w_query.shape[0]
    vectors = (b_query, b_value, b_out, norm1_gain, norm1_bias, b_down, norm2_gain, norm2_bias)
    spread = b_up.shape[0] // block
    columns = [v[:, None] for v in vectors] + [b_up.reshape(spread, block).T]
    columns = jnp.concatenate(columns, axis=1)
    columns = jnp.pad(columns, ((0, 0), (0, LANES - columns.shape[1])))
    tokens = passages.reshape(rows, width)
    w_qkv = jnp.concatenate([w_query, w_key, w_value], axis=1)
    digits = jnp.stack([positives.T // 256, positives.T % 256], axis=-1).astype(BF16)
    payload = jnp.concatenate(
        [
            jnp.moveaxis(queries, 0, 1).reshape(total, width),
            jnp.pad(digits.reshape(total, 2), ((0, 0), (0, LANES - 2))),
        ],
        axis=-1,
    )
    spans = lengths.reshape(total)
    if grid.fast:
        flip = grid.flip
        mine, twin = halves_of((w_qkv,), columns, here[1])
        own, mine = jnp.stack([mine, twin]), mine[None]
        second = halves_of((w_out, w_up), None, here[1])[0][None]
        third = halves_of((w_down,), None, here[1])[0]
        across, h1, h2, h3 = flip(own, "y"), flip(mine, "z1"), flip(mine, "z2"), flip(mine, "z3")
        s1 = flip(second, "z1")
        order = after(grid, across, h1, h2, h3)
        line = plus(jnp.concatenate([h1, h2, h3]), order)
        line_y, line_x = flip(line, "y"), flip(line, "x")
        second = plus(jnp.concatenate([second, s1]), order)
        second_far = flip(second, "z2")
        cores = [flip(own, "core"), flip(across, "core"), flip(line, "core")]
        order = after(grid, line_y, line_x, second)
        cross_x = flip(plus(line_y[:2], order), "x")
        cross_y = flip(plus(line_x[2:], order), "y")
        cores += [flip(line_y, "core"), flip(line_x, "core")]
        order = after(grid, cross_x, cross_y)
        second = plus(second, order)
        second_y, second_x = flip(second, "y"), flip(second, "x")
        cores += [flip(cross_x, "core"), flip(cross_y, "core")]
        bag = [
            (own, [(0, 0, 0, 0), (0, 0, 0, 1)]),
            (across, [(0, 1, 0, 0), (0, 1, 0, 1)]),
            (line, [(0, 0, z, 0) for z in (1, 2, 3)]),
            (line_y, [(0, 1, z, 0) for z in (1, 2, 3)]),
            (line_x, [(0, 0, z, 1) for z in (1, 2, 3)]),
            (cross_x, [(0, 1, z, 1) for z in (1, 2)]),
            (cross_y, [(0, 1, 3, 1)]),
        ]
        bag += [(v, core_keys(keys)) for v, (_, keys) in zip(cores, bag)]
        weight_qkv, table = join(bag, [3 * width // 2], LANES, here)
        order = after(grid, table)
        high = plus(second_far, order)
        high_y, high_x = flip(high, "y"), flip(high, "x")
        second_cross = flip(plus(second_y, order), "x")
        third = grid.share(third, "z", order)
        order = after(grid, high)
    else:
        weight_qkv, table, weight_out, weight_up, weight_down = [
            lax.all_gather(w, "dp", axis=0, tiled=True)
            for w in (w_qkv, columns, w_out, w_up, w_down)
        ]
        order = 0.0
    table = table[:, :16].T.astype(F32)
    (bias_q, bias_v, bias_out, gain_one, shift_one, bias_down, gain_two, shift_two) = [
        table[i] for i in range(8)
    ]
    bias_up = jnp.transpose(
        table[8 : 8 + spread].reshape(spread, dp, block), (1, 0, 2)
    ).reshape(-1)
    bias_qkv = jnp.concatenate([bias_q, jnp.zeros_like(bias_q), bias_v])
    qkv = plus(mm(tokens, weight_qkv) + bias_qkv, order).astype(BF16)
    z_keys = [[(0, y, z, h) for z in range(4)] for y, h in ((0, 0), (1, 0), (0, 1), (1, 1))]

    def bag_of(blocks):
        cores = [flip(v, "core") for v, _ in blocks]
        return blocks + [(v, core_keys(keys)) for v, (_, keys) in zip(cores, blocks)]

    low_keys = [keys[:2] for keys in z_keys]
    high_keys = [keys[2:] for keys in z_keys]
    if grid.fast:
        order = after(grid, qkv, high_x, high_y, second_x)
        high_cross = flip(plus(high_x, order), "y")
        attention_order = [jnp.full((8, LANES), order, F32)]
    else:
        attention_order = []
    context, log_total = attention(qkv, spans, attention_order, length, H)
    if grid.fast:
        order = after(grid, context, high_cross, second_cross, third)
        third = grid.share(third, "xy", order)
        order = after(grid, context, high_cross)
        blocks = (second, second_y, second_x, second_cross)
        blocks = list(zip(blocks, low_keys)) + list(zip((high, high_y, high_x, high_cross), high_keys))
        weight_out, weight_up = join(bag_of(blocks), [width // 2, w_up.shape[1] // 2], 0, here)
        order = after(grid, weight_out)
    sum_one = tokens.astype(F32) + mm(context, weight_out) + bias_out
    unit_one, scale_one = norm_parts(sum_one)
    hidden = unit_one * gain_one + shift_one
    hidden_low = hidden.astype(BF16)
    pre = mm(hidden_low, weight_up) + bias_up
    phi, density = normal_parts(pre)
    gelu_low = (pre * phi).astype(BF16)
    slope = (phi + pre * density).astype(BF16)
    if grid.fast:
        order = after(grid, gelu_low, third)
        third = third.reshape((16,) + third.shape[2:])
        bag = [(third, square_keys(0)), (flip(third, "core"), square_keys(1))]
        (weight_down,) = join(bag, [width // 2], 0, here)
    sum_two = plus(hidden, order) + mm(gelu_low, weight_down) + bias_down
    unit_two, scale_two = norm_parts(sum_two)
    result = (unit_two * gain_two + shift_two).reshape(steps, count, length, width)
    output = result.astype(BF16)

    def starts(value):
        return value.reshape(total, length, -1)[:, 0]

    def put_starts(value, part):
        blocks = value.reshape(total, length, -1)
        return lax.dynamic_update_slice(blocks, part[:, None], (0, 0, 0)).reshape(value.shape)

    cls = jnp.moveaxis(output[:, :, 0, :], 0, 1).reshape(total, width)
    if grid.fast:
        cls = grid.share(jnp.concatenate([cls, payload], axis=1), "all")
    else:
        cls = jnp.concatenate([cls, payload], axis=1)
        cls = lax.all_gather(cls, ("dp", "rep"), axis=0, tiled=True)
    grad_out = out_grad.reshape(rows, width).astype(F32)
    grad_two = norm_back(grad_out, unit_two, scale_two, gain_two)
    down_low = grad_two.astype(BF16)
    later = (jnp.arange(rows) % length > 0)[:, None]
    grad_gain_two = jnp.sum(grad_out * unit_two, axis=0)
    grad_shift_two = jnp.sum(grad_out, axis=0)
    grad_b_down = jnp.sum(jnp.where(later, down_low.astype(F32), 0.0), axis=0)

    def up_back(grad, by):
        return (mm_back(grad, weight_down) * by.astype(F32)).astype(BF16)

    up_low = up_back(down_low, slope)
    order = after(grid, cls, up_low)

    cls = plus(cls.reshape(-1, steps, 2 * width + LANES), order)
    all_cls, all_queries = cls[:, :, :width], cls[:, :, width : 2 * width]
    digits = cls[:, :, 2 * width : 2 * width + 2].astype(jnp.int32)
    all_positives = digits[:, :, 0] * 256 + digits[:, :, 1]
    first = (dp_index * grid.rep + rep_index) * count
    logits = jnp.einsum("qmd,pmd->mqp", all_queries, all_cls, preferred_element_type=F32)
    logits = logits * inv_width
    query_total = jax.nn.logsumexp(logits, axis=-1)
    passages_all = all_cls.shape[0]
    mine = lax.dynamic_slice_in_dim(logits, first, count, axis=1)
    mine_total = lax.dynamic_slice_in_dim(query_total, first, count, axis=1)
    onehot = (positives[:, :, None] == jnp.arange(passages_all)[None, None, :]).astype(F32)
    query_loss = mine_total - jnp.sum(mine * onehot, axis=-1)
    mine_grad = (jnp.exp(mine - mine_total[:, :, None]) - onehot) * inv_width
    queries_grad = jnp.einsum(
        "mqp,pmd->mqd", mine_grad.astype(BF16), all_cls, preferred_element_type=F32
    )
    column = lax.dynamic_slice_in_dim(logits, first, count, axis=2)
    hit = (all_positives.T[:, :, None] == (first + jnp.arange(count))[None, None, :]).astype(F32)
    column_grad = (jnp.exp(column - query_total[:, :, None]) - hit) * inv_width
    cls_grad = jnp.einsum(
        "mqp,qmd->mpd", column_grad.astype(BF16), all_queries, preferred_element_type=F32
    )

    grad_start = cls_grad.reshape(total, width)
    unit_start = starts(unit_two)
    grad_gain_two = grad_gain_two + jnp.sum(grad_start * unit_start, axis=0)
    grad_shift_two = grad_shift_two + jnp.sum(grad_start, axis=0)
    grad_start = grad_start + starts(out_grad.reshape(rows, width)).astype(F32)
    grad_start = norm_back(grad_start, unit_start, starts(scale_two), gain_two)
    down_start = grad_start.astype(BF16)
    up_start = up_back(down_start, starts(slope))
    grad_b_down = grad_b_down + row_total(down_start)
    grad_two = put_starts(grad_two, grad_start)
    down_low = put_starts(down_low, down_start)
    up_low = put_starts(up_low, up_start)

    down_sum, up_sum, last_sum = [Scatter(grid, here) for _ in range(3)]
    down_sum.start([mm_left(gelu_low, down_low).astype(BF16)])
    order = after(grid, down_sum.held)
    down_sum.step(order)
    down_sum.step(deps=[up_low])
    order = down_sum.token
    grad_w_up = plus(mm_left(hidden_low, up_low), order).astype(BF16)
    up_sum.start([grad_w_up], down_sum.held)
    up_sum.step()
    down_sum.step(deps=[up_sum.far])
    order = down_sum.token
    half = w_up.shape[1] // 2
    grad_hidden = plus(grad_two + mm_back(up_low[:, :half], weight_up[:, :half]), order)
    up_sum.step(deps=[grad_hidden])
    order = up_sum.token
    grad_hidden = plus(grad_hidden + mm_back(up_low[:, half:], weight_up[:, half:]), order)
    grad_gain_one = jnp.sum(grad_hidden * unit_one, axis=0)
    grad_shift_one = jnp.sum(grad_hidden, axis=0)
    grad_one = norm_back(grad_hidden, unit_one, scale_one, gain_one)
    attn_low = grad_one.astype(BF16)
    grad_w_out = mm_left(context, attn_low).astype(BF16)
    context_grad = mm_back(attn_low, weight_out).astype(BF16)
    down_sum.step(deps=[up_sum.held, attn_low])
    up_sum.step(down_sum.token)
    order = up_sum.token
    qkv_low, grad_b_qkv = attention_back(
        qkv, context_grad, log_total, spans, [jnp.full((8, LANES), order, F32)], length, H
    )
    down_sum.step(deps=[up_sum.held, qkv_low])
    up_sum.step(down_sum.token)
    order = up_sum.token

    grad_w_qkv = plus(mm_left(tokens, qkv_low), order).astype(BF16)
    last_sum.start([grad_w_out, grad_w_qkv])
    last_sum.step()
    order = after(grid, last_sum.far)
    grad_b_query, grad_b_value = grad_b_qkv[0, :width], grad_b_qkv[0, 2 * width :]
    grad_b_out = row_total(attn_low, order)
    grad_b_up = row_total(up_low, order)
    grads = (
        grad_b_query,
        grad_b_value,
        grad_b_out,
        grad_gain_one,
        grad_shift_one,
        grad_b_down,
        grad_gain_two,
        grad_shift_two,
    )
    grads = jnp.concatenate([jnp.stack(grads), grad_b_up.reshape(spread, width)])

    grads = Total(grid, grads)
    up_sum.step(order)
    last_sum.step(deps=[grads.parts])
    order = last_sum.token
    grads.step(order)
    last_sum.step(deps=[grads.held])
    order = last_sum.token
    grads.step(order)
    input_grad = plus(grad_one + mm_back(qkv_low, weight_qkv), order)
    last_sum.step(deps=[input_grad, grads.held])
    order = last_sum.token
    grads.step(order)
    last_sum.step(deps=[input_grad, up_sum.held, grads.held])
    order = last_sum.token
    up_sum.step(order)
    down_sum.step(order)
    grads.step(order)
    (shard_w_down,) = down_sum.finish()
    (shard_w_up,) = up_sum.finish()
    shard_w_out, shard_w_qkv = last_sum.finish()
    shard_w_query, shard_w_key, shard_w_value = jnp.split(shard_w_qkv, 3, axis=1)
    grads = grads.finish()
    low = lax.dynamic_slice_in_dim(grads[:8], dp_index * block, block, axis=1)
    s_b_up = lax.dynamic_slice_in_dim(
        grads[8:].reshape(-1), dp_index * spread * block, spread * block, axis=0
    )
    (s_b_q, s_b_v, s_b_out, s_gain1, s_shift1, s_b_down, s_gain2, s_shift2) = [
        low[i] for i in range(8)
    ]
    return (
        output,
        query_loss,
        input_grad.reshape(steps, count, length, width),
        queries_grad,
        cls_grad,
        shard_w_query,
        s_b_q,
        shard_w_key,
        shard_w_value,
        s_b_v,
        shard_w_out,
        s_b_out,
        s_gain1,
        s_shift1,
        shard_w_up,
        s_b_up,
        shard_w_down,
        s_b_down,
        s_gain2,
        s_shift2,
    )


def solution(mesh):
    both = ("dp", "rep")
    matrix, vector = P("dp", None), P("dp")
    weights = (
        matrix, vector, matrix, matrix, vector, matrix, vector, vector, vector,
        matrix, vector, matrix, vector, vector, vector,
    )
    grid = Grid(mesh.shape["dp"], mesh.shape["rep"], 768 // mesh.shape["dp"])
    wide = P(None, both, None, None)
    return jax.shard_map(
        functools.partial(per_device, grid),
        mesh=mesh,
        in_specs=(wide, P(None, both), P(None, both, None), P(None, both), wide) + weights,
        out_specs=(wide, P(None, both), wide, P(None, both, None), P(None, both, None)) + weights,
        check_vma=False,
    )
```

```python
import functools
import math

import jax
import jax.numpy as jnp
from jax import lax
from jax.experimental import pallas as pl
from jax.experimental.pallas import tpu as pltpu
from jax.sharding import PartitionSpec as P

H = 12
F32 = jnp.float32
BF16 = jnp.bfloat16
INV_SQRT2 = 1.0 / math.sqrt(2.0)
INV_SQRT_2PI = 1.0 / math.sqrt(2.0 * math.pi)


ANY = pl.BlockSpec(memory_space=pl.ANY)
SMEM = pl.BlockSpec(memory_space=pltpu.SMEM)
VMEM = pl.BlockSpec(memory_space=pltpu.VMEM)
MIB = 2**20
LANES = 128


class Grid:
    def __init__(self, dp, rep, rows):
        self.dp, self.rep = dp, rep
        self.fast = dp == 16 and rep == 2 and rows % 16 == 0
        self.bits = {"core": 1, "y": 2, "z1": 4, "z2": 8, "z3": 12}

        place = [
            (((z * 2 + y) * 2 + c) * 2 + x, (z, y, c, x))
            for z in range(4)
            for y in range(2)
            for c in range(2)
            for x in range(2)
        ]
        lines, squares = {}, {}
        for i, (z, y, c, x) in place:
            lines.setdefault((y, c, x), []).append(i)
            squares.setdefault((z, c), []).append(i)
        self.groups = {"z": list(lines.values()), "xy": list(squares.values()), "all": None}

    def exchange(self, value, name):
        return lax.all_to_all(
            value, ("dp", "rep"), 0, 0, axis_index_groups=self.groups[name], tiled=True
        )

    def share(self, value, name, order=0.0):
        count = self.dp * self.rep if name == "all" else 4
        value = plus(jnp.broadcast_to(value[None], (count,) + value.shape), order)
        return self.exchange(value, name)

    def flip(self, value, name):
        if name == "x":
            return lax.ppermute(value, "rep", [(i, i ^ 1) for i in range(self.rep)])
        bit = self.bits[name]
        return lax.ppermute(value, "dp", [(i, i ^ bit) for i in range(self.dp)])


def run_copies(copies):
    for copy in copies:
        copy.start()
    for copy in copies:
        copy.wait()


def place_of(here_ref, key, rows):
    core, y, z, half = key[:4]
    if len(key) > 4:
        place = z * 4 + y * 2 + ((here_ref[0] & 1) ^ core)
        return pl.ds(pl.multiple_of(place * rows, 16), rows), half
    row = pl.multiple_of((here_ref[0] ^ (z * 4 + y * 2 + core)) * rows, 16)
    return pl.ds(row, rows), here_ref[1] ^ half


def square_keys(core):
    return [(core, y, z, x, True) for y in range(2) for x in range(2) for z in range(4)]


def join_kernel(here_ref, *refs, keys, widths, extra, rows):
    count = len(keys)
    pieces, outs, sems = refs[:count], refs[count:-1], refs[-1]
    copies = []
    for piece, names in zip(pieces, keys):
        for i, key in enumerate(names):
            where, half = place_of(here_ref, key, rows)
            at = 0
            for out, width in zip(outs, widths):
                column = half * width
                if len(key) == 4:
                    column = pl.multiple_of(column, LANES)
                column = pl.ds(column, width)
                source = piece.at[i, pl.ds(0, rows), pl.ds(at, width)]
                copies.append((source, out.at[where, column]))
                at += width
            if extra and key[3] == 0:
                copies.append((piece.at[i, :, pl.ds(at, extra)], outs[-1].at[where, :]))
    run_copies([pltpu.make_async_copy(a, b, sems.at[i]) for i, (a, b) in enumerate(copies)])


def join(bag, widths, extra, here, rows=None):
    arrays, keys = zip(*bag)
    rows = rows or arrays[0].shape[1]
    shapes = [(16 * rows, 2 * width) for width in widths] + ([(16 * rows, extra)] if extra else [])
    copies = 32 * len(widths) + (16 if extra else 0)
    size = sum(a * b for a, b in shapes)
    return pl.pallas_call(
        functools.partial(join_kernel, keys=keys, widths=widths, extra=extra, rows=rows),
        out_shape=[jax.ShapeDtypeStruct(shape, arrays[0].dtype) for shape in shapes],
        in_specs=[SMEM] + [ANY] * len(arrays),
        out_specs=[VMEM] * len(shapes),
        scratch_shapes=[pltpu.SemaphoreType.DMA((copies,))],
        compiler_params=pltpu.CompilerParams(vmem_limit_bytes=2 * MIB),
        cost_estimate=pl.CostEstimate(flops=0, bytes_accessed=4 * size, transcendentals=0),
        name="join",
    )(here, *arrays)


def split_kernel(here_ref, *refs, keys, count):
    values, pieces, sems = refs[:count], refs[-1 - len(keys) : -1], refs[-1]
    copies = []
    for piece, names in zip(pieces, keys):
        rows = piece.shape[1]
        for i, key in enumerate(names):
            where, half = place_of(here_ref, key, rows)
            at = 0
            for value in values:
                width = value.shape[1] // 2
                column = half * width
                if len(key) == 4:
                    column = pl.multiple_of(column, LANES)
                column = pl.ds(column, width)
                copies.append((value.at[where, column], piece.at[i, :, pl.ds(at, width)]))
                at += width
    run_copies([pltpu.make_async_copy(a, b, sems.at[i]) for i, (a, b) in enumerate(copies)])


def split(values, keys, here, deps):
    rows, width = values[0].shape[0] // 16, sum(v.shape[1] for v in values) // 2
    kind = values[0].dtype
    size = sum(v.size for v in values)
    return pl.pallas_call(
        functools.partial(split_kernel, keys=keys, count=len(values)),
        out_shape=[jax.ShapeDtypeStruct((len(names), rows, width), kind) for names in keys],
        in_specs=[SMEM] + [VMEM] * len(values) + [ANY] * len(deps),
        out_specs=[ANY] * len(keys),
        scratch_shapes=[pltpu.SemaphoreType.DMA((32 * len(values),))],
        compiler_params=pltpu.CompilerParams(vmem_limit_bytes=2 * MIB),
        cost_estimate=pl.CostEstimate(flops=0, bytes_accessed=4 * size, transcendentals=0),
        name="split",
    )(here, *values, *deps)


def order_kernel(*refs):
    refs[-1][0, 0] = 0.0


def after(grid, *trees):
    if not grid.fast:
        return 0.0
    leaves = jax.tree.leaves(trees)
    return pl.pallas_call(
        order_kernel,
        out_shape=jax.ShapeDtypeStruct((1, 1), F32),
        in_specs=[ANY] * len(leaves),
        out_specs=SMEM,
        compiler_params=pltpu.CompilerParams(vmem_limit_bytes=MIB // 4),
        name="order",
    )(*leaves).reshape(())


def halves_of(parts, extra, x):
    out = []
    for place in (x, 1 - x):
        row = [
            lax.dynamic_slice_in_dim(p, place * (p.shape[1] // 2), p.shape[1] // 2, axis=1)
            for p in parts
        ]
        out.append(jnp.concatenate(row + ([extra] if extra is not None else []), axis=1))
    return out


def core_keys(keys):
    return [(1,) + key[1:] for key in keys]


class Spread:
    def __init__(self, grid, value):
        self.grid, self.value = grid, value
        self.names = ["x", "core", "y", "z1", "z2"]
        self.other = None
        if not grid.fast:
            self.value = lax.all_gather(value, ("dp", "rep"), axis=0, tiled=True)
            self.names = []

    def absorb(self, order=0.0):
        if self.other is None:
            return
        name = self.names.pop(0)
        if name == "x":
            upper = lax.axis_index("rep") > 0
        else:
            upper = (lax.axis_index("dp") & self.grid.bits[name]) > 0
        low = jnp.where(upper, self.other, self.value)
        high = jnp.where(upper, self.value, self.other)
        self.value, self.other = jnp.concatenate([low, high], axis=0), None
        self.value = plus(self.value, order)

    def step(self, order=0.0):
        self.absorb(order)
        if self.names:
            self.other = self.grid.flip(self.value, self.names[0])
            self.held = [self.other]


class Total:
    def __init__(self, grid, value):
        self.grid, self.parts = grid, [value]
        self.names = ["x", "core", "y", "z1", "z2"]
        if not grid.fast:
            self.parts, self.names = [lax.psum(value, ("dp", "rep"))], []

    def step(self, order=0.0):
        value = sum(self.parts[1:], self.parts[0])
        self.parts = [plus(value, order)]
        if self.names:
            self.parts.append(self.grid.flip(self.parts[0], self.names.pop(0)))
        self.held = self.parts[1:]

    def finish(self):
        while self.names:
            self.step()
        return sum(self.parts[1:], self.parts[0])


def plus(value, order):
    return value if isinstance(order, float) else (value.astype(F32) + order).astype(value.dtype)


def sums_kernel(order_ref, *refs, plan):
    zero = order_ref[0, 0]
    refs[-1][0, 0] = zero
    for out_ref, terms in zip(refs[-1 - len(plan) : -1], plan):
        at = 0
        for size, parts in terms:
            for i in range(size):
                total = zero
                for source, first in parts:
                    total = total + refs[source][first + i].astype(F32)
                out_ref[at + i] = total.astype(out_ref.dtype)
            at += size


def sums(order, arrays, plan, deps):
    deps = jax.tree.leaves(deps)
    shapes = [(sum(size for size, _ in terms),) + arrays[0].shape[1:] for terms in plan]
    size = sum(a * b * c for a, b, c in shapes)
    return pl.pallas_call(
        functools.partial(sums_kernel, plan=plan),
        out_shape=[jax.ShapeDtypeStruct(shape, BF16) for shape in shapes]
        + [jax.ShapeDtypeStruct((1, 1), F32)],
        in_specs=[SMEM] + [VMEM] * len(arrays) + [ANY] * len(deps),
        out_specs=[VMEM] * len(shapes) + [SMEM],
        compiler_params=pltpu.CompilerParams(vmem_limit_bytes=8 * MIB),
        cost_estimate=pl.CostEstimate(flops=2 * size, bytes_accessed=6 * size, transcendentals=0),
        name="sums",
    )(jnp.reshape(jnp.asarray(order, F32), (1, 1)), *arrays, *deps)


class Scatter:
    def __init__(self, grid, here):
        self.grid, self.here, self.stage, self.held, self.sent = grid, here, 0, [], []
        self.far, self.token = [], 0.0

    def start(self, grads, deps=()):
        self.widths = [g.shape[1] for g in grads]
        if not self.grid.fast:
            parts = [
                lax.psum_scatter(g.astype(F32), "dp", scatter_dimension=0, tiled=True)
                for g in grads
            ]
            self.result = [lax.psum(p, "rep") for p in parts]
            return
        keys = [
            [(c, y, z, h) for y, h in ((1, 1), (0, 1), (1, 0), (0, 0)) for z in range(4)]
            for c in range(2)
        ]
        self.token = 0.0
        self.near, self.far = split(grads, keys, self.here, deps)
        self.held = [self.far]

    def step(self, order=0.0, deps=()):
        if not self.grid.fast:
            return
        flip = self.grid.flip
        self.stage += 1
        if self.stage == 1:
            self.held = [flip(self.far, "core")]
            return
        if self.stage == 2:
            plan = [[(n, [(0, at), (1, at)])] for n, at in ((2, 0), (2, 2), (4, 4), (4, 8), (4, 12))]
            low, high, self.x, self.y, self.own, token = sums(
                order, [self.near, *self.held], plan, deps
            )
            self.sent, self.held = [low, high], [flip(low, "x"), flip(high, "y")]
        elif self.stage == 3:
            plan = [[(2, [(0, 0)]), (2, [(0, 2), (3, 0)])], [(2, [(1, 0), (2, 0)]), (2, [(1, 2)])]]
            to_x, to_y, token = sums(order, [self.x, self.y, *self.held], plan, deps)
            self.sent, self.held = [to_x, to_y], [flip(to_x, "x"), flip(to_y, "y")]
        elif self.stage == 4:
            plan = [[(2, [(0, at), (1, at), (2, at)])] for at in (0, 2)]
            self.low, high, token = sums(order, [self.own, *self.held], plan, deps)
            self.sent, self.held = [high], [flip(high, "z2")]
        elif self.stage == 5:
            plan = [[(1, [(0, at), (1, at)])] for at in (0, 1)]
            self.low, high, token = sums(order, [self.low, *self.held], plan, deps)
            self.sent, self.held = [high], [flip(high, "z1")]
        elif self.stage == 6:
            plan = [[(1, [(0, 0), (1, 0)])]]
            self.low, token = sums(order, [self.low, *self.held], plan, deps)
            self.sent, self.held = [self.low], [flip(self.low, "x")]
        self.token = token.reshape(())

    def finish(self):
        if not self.grid.fast:
            return self.result
        while self.stage < 6:
            self.step()
        value, other = self.low[0], self.held[0][0]
        first = self.here[1] == 0
        left, right = jnp.where(first, value, other), jnp.where(first, other, value)
        out, at = [], 0
        for width in self.widths:
            cut = slice(at, at + width // 2)
            out.append(jnp.concatenate([left[:, cut], right[:, cut]], axis=1).astype(F32))
            at += width // 2
        return out


def mm(left, right):
    return jnp.dot(left, right, preferred_element_type=F32)


def mm_left(left, right):
    return lax.dot_general(left, right, (((0,), (0,)), ((), ())), preferred_element_type=F32)


def mm_back(left, right):
    return lax.dot_general(left, right, (((1,), (1,)), ((), ())), preferred_element_type=F32)


def row_total(values, order=0.0):
    return mm(plus(jnp.ones((8, values.shape[0]), BF16), order), values)[0]


def normal_parts(v):
    phi = 0.5 + 0.5 * lax.erf(v * INV_SQRT2)
    return phi, jnp.exp(-0.5 * v * v) * INV_SQRT_2PI


def norm_parts(v):
    mean_val = jnp.mean(v, axis=-1, keepdims=True)
    centred = v - mean_val
    variance = jnp.mean(centred * centred, axis=-1, keepdims=True)
    scale = lax.rsqrt(variance + 1e-05)
    return centred * scale, scale


def norm_back(grad, unit, scale, gain):
    inner = grad * gain
    mean_one = jnp.mean(inner, axis=-1, keepdims=True)
    mean_two = jnp.mean(inner * unit, axis=-1, keepdims=True)
    return (inner - mean_one - unit * mean_two) * scale


def two_heads(t, first):
    zero = jnp.zeros_like(t)
    return jnp.concatenate([jnp.where(first, t, zero), jnp.where(first, zero, t)], axis=0)

def attn_kernel(len_ref, qkv_ref, *refs, scale, n, pairs, many):
    c_ref, total_ref = refs[-2:]
    width = pairs * LANES
    q_ref, k_ref, v_ref = [qkv_ref.at[:, pl.ds(i * width, width)] for i in range(3)]
    lane = lax.broadcasted_iota(jnp.int32, (1, 2 * n), 1) % n
    first = lax.broadcasted_iota(jnp.int32, (n, LANES), 1) < LANES // 2
    spot = lax.broadcasted_iota(jnp.int32, (n, LANES), 1)
    for i in range(many):
        rows = slice(i * n, (i + 1) * n)
        length = len_ref[pl.program_id(0) * many + i]
        totals = jnp.zeros((n, LANES), F32)
        for pair in range(pairs):
            at = slice(pair * LANES, (pair + 1) * LANES)
            q = q_ref[rows, at] * scale
            s = mm_back(q, two_heads(k_ref[rows, at], first))
            s = jnp.where(lane < length, s, -1000000000.0)
            parts = []
            for h in range(2):
                part = s[:, h * n : (h + 1) * n]
                top = jnp.max(part, axis=-1, keepdims=True)
                part = jnp.exp(part - top)
                total = jnp.sum(part, axis=-1, keepdims=True)
                parts.append((part * (1.0 / total)).astype(BF16))
                totals = jnp.where(spot == 2 * pair + h, top + jnp.log(total), totals)
            p = jnp.concatenate(parts, axis=1)
            c_ref[rows, at] = mm(p, two_heads(v_ref[rows, at], first)).astype(BF16)
        total_ref[i] = totals.T[: total_ref.shape[1]]

def attention(qkv, lengths, deps, n, heads):
    rows, width = qkv.shape[0], qkv.shape[1] // 3
    count, many = rows // n, 2
    scale = 1.0 / math.sqrt(width // heads)
    block = pl.BlockSpec((n * many, width), lambda i: (i, 0))
    lines = 16
    return pl.pallas_call(
        functools.partial(attn_kernel, scale=scale, n=n, pairs=heads // 2, many=many),
        grid=(count // many,),
        in_specs=[SMEM, pl.BlockSpec((n * many, 3 * width), lambda i: (i, 0))] + [ANY] * len(deps),
        out_specs=[block, pl.BlockSpec((many, lines, n), lambda i: (i, 0, 0))],
        out_shape=[jax.ShapeDtypeStruct((rows, width), BF16), jax.ShapeDtypeStruct((count, lines, n), F32)],
        compiler_params=pltpu.CompilerParams(vmem_limit_bytes=16 * MIB),
        cost_estimate=pl.CostEstimate(flops=8 * rows * n * width, bytes_accessed=8 * rows * width, transcendentals=rows * n * heads),
        name="attention",
    )(lengths, qkv, *deps)

def attn_back_kernel(len_ref, total_ref, qkv_ref, d_ref, *refs, scale, n, pairs, many):
    width = pairs * LANES
    q_ref, k_ref, v_ref = [qkv_ref.at[:, pl.ds(i * width, width)] for i in range(3)]
    out_ref, total_out_ref = refs[-2:]
    dq_ref, dk_ref, dv_ref = [out_ref.at[:, pl.ds(i * width, width)] for i in range(3)]
    row = lax.broadcasted_iota(jnp.int32, (2 * n, n), 0) % n
    first = lax.broadcasted_iota(jnp.int32, (n, LANES), 1) < LANES // 2
    for i in range(many):
        rows = slice(i * n, (i + 1) * n)
        length = len_ref[pl.program_id(0) * many + i]
        valid = row < length
        for pair in range(pairs):
            at = slice(pair * LANES, (pair + 1) * LANES)
            q, k, v, d = q_ref[rows, at] * scale, k_ref[rows, at] * scale, v_ref[rows, at], d_ref[rows, at]
            kk = two_heads(k_ref[rows, at], first)
            s = jnp.where(valid, mm_back(kk, q), -1000000000.0)
            dp = mm_back(two_heads(v, first), d)
            ps, ds = [], []
            for h in range(2):
                part = slice(h * n, (h + 1) * n)
                p = jnp.exp(s[part] - total_ref[i, 2 * pair + h : 2 * pair + h + 1, :])
                t = p * dp[part]
                ds.append((t - p * jnp.sum(t, axis=0, keepdims=True)).astype(BF16))
                ps.append(p.astype(BF16))
            dv_ref[rows, at] = mm(jnp.concatenate(ps, axis=1), two_heads(d, first)).astype(BF16)
            dk_ref[rows, at] = mm(jnp.concatenate(ds, axis=1), two_heads(q, first)).astype(BF16)
            dq_ref[rows, at] = mm_left(jnp.concatenate(ds, axis=0), two_heads(k, first)).astype(BF16)
    term = jnp.sum(out_ref[...].astype(F32), axis=0, keepdims=True)

    @pl.when(pl.program_id(0) == 0)
    def _():
        total_out_ref[...] = term

    @pl.when(pl.program_id(0) > 0)
    def _():
        total_out_ref[...] += term


def attention_back(qkv, d, totals, lengths, deps, n, heads):
    rows, width = d.shape
    count, many = rows // n, 2
    scale = 1.0 / math.sqrt(width // heads)
    block = pl.BlockSpec((n * many, width), lambda i: (i, 0))
    wide = pl.BlockSpec((n * many, 3 * width), lambda i: (i, 0))
    return pl.pallas_call(
        functools.partial(attn_back_kernel, scale=scale, n=n, pairs=heads // 2, many=many),
        grid=(count // many,),
        in_specs=[SMEM, pl.BlockSpec((many,) + totals.shape[1:], lambda i: (i, 0, 0)), wide, block]
        + [ANY] * len(deps),
        out_specs=[wide, pl.BlockSpec((1, 3 * width), lambda i: (0, 0))],
        out_shape=[
            jax.ShapeDtypeStruct((rows, 3 * width), BF16),
            jax.ShapeDtypeStruct((1, 3 * width), F32),
        ],
        compiler_params=pltpu.CompilerParams(vmem_limit_bytes=16 * MIB),
        cost_estimate=pl.CostEstimate(flops=20 * rows * n * width, bytes_accessed=14 * rows * width, transcendentals=rows * n * heads),
        name="attention_back",
    )(lengths, totals, qkv, d, *deps)


def per_device(
    grid,
    passages,
    lengths,
    queries,
    positives,
    out_grad,
    w_query,
    b_query,
    w_key,
    w_value,
    b_value,
    w_out,
    b_out,
    norm1_gain,
    norm1_bias,
    w_up,
    b_up,
    w_down,
    b_down,
    norm2_gain,
    norm2_bias,
):
    steps, count, length, width = passages.shape
    total = steps * count
    rows = total * length
    inv_width = 1.0 / math.sqrt(width)
    dp = grid.dp
    dp_index, rep_index = lax.axis_index("dp"), lax.axis_index("rep")
    here = jnp.stack([dp_index, rep_index]).astype(jnp.int32)

    block = w_query.shape[0]
    vectors = (b_query, b_value, b_out, norm1_gain, norm1_bias, b_down, norm2_gain, norm2_bias)
    spread = b_up.shape[0] // block
    columns = [v[:, None] for v in vectors] + [b_up.reshape(spread, block).T]
    columns = jnp.concatenate(columns, axis=1)
    columns = jnp.pad(columns, ((0, 0), (0, LANES - columns.shape[1])))
    tokens = passages.reshape(rows, width)
    w_qkv = jnp.concatenate([w_query, w_key, w_value], axis=1)
    digits = jnp.stack([positives.T // 256, positives.T % 256], axis=-1).astype(BF16)
    query_rows = jnp.moveaxis(queries, 0, 1).reshape(total, width)
    digits = jnp.pad(digits.reshape(total, 2), ((0, 0), (0, LANES - 2)))
    spans = lengths.reshape(total)
    if grid.fast:
        flip = grid.flip
        mine, twin = halves_of((w_qkv,), columns, here[1])
        own, mine = jnp.stack([mine, twin]), mine[None]
        second = halves_of((w_out, w_up), None, here[1])[0][None]
        third = halves_of((w_down,), None, here[1])[0]
        third = jnp.concatenate([third, query_rows[:, : width // 2], query_rows[:, width // 2 :]])
        across, h1, h2, h3 = flip(own, "y"), flip(mine, "z1"), flip(mine, "z2"), flip(mine, "z3")
        s1 = flip(second, "z1")
        order = after(grid, across, h1, h2, h3)
        line = plus(jnp.concatenate([h1, h2, h3]), order)
        line_y, line_x = flip(line, "y"), flip(line, "x")
        second = plus(jnp.concatenate([second, s1]), order)
        second_far = flip(second, "z2")
        cores = [flip(own, "core"), flip(across, "core"), flip(line, "core")]
        order = after(grid, line_y, line_x, second)
        cross_x = flip(plus(line_y[:2], order), "x")
        cross_y = flip(plus(line_x[2:], order), "y")
        cores += [flip(line_y, "core"), flip(line_x, "core")]
        order = after(grid, cross_x, cross_y)
        second = plus(second, order)
        second_y, second_x = flip(second, "y"), flip(second, "x")
        cores += [flip(cross_x, "core"), flip(cross_y, "core")]
        bag = [
            (own, [(0, 0, 0, 0), (0, 0, 0, 1)]),
            (across, [(0, 1, 0, 0), (0, 1, 0, 1)]),
            (line, [(0, 0, z, 0) for z in (1, 2, 3)]),
            (line_y, [(0, 1, z, 0) for z in (1, 2, 3)]),
            (line_x, [(0, 0, z, 1) for z in (1, 2, 3)]),
            (cross_x, [(0, 1, z, 1) for z in (1, 2)]),
            (cross_y, [(0, 1, 3, 1)]),
        ]
        bag += [(v, core_keys(keys)) for v, (_, keys) in zip(cores, bag)]
        weight_qkv, table = join(bag, [3 * width // 2], LANES, here)
        order = after(grid, table)
        high = plus(second_far, order)
        high_y, high_x = flip(high, "y"), flip(high, "x")
        second_cross = flip(plus(second_y, order), "x")
        third = grid.share(third, "z", order)
        order = after(grid, high)
    else:
        weight_qkv, table, weight_out, weight_up, weight_down = [
            lax.all_gather(w, "dp", axis=0, tiled=True)
            for w in (w_qkv, columns, w_out, w_up, w_down)
        ]
        order = 0.0
    table = table[:, :16].T.astype(F32)
    (bias_q, bias_v, bias_out, gain_one, shift_one, bias_down, gain_two, shift_two) = [
        table[i] for i in range(8)
    ]
    bias_up = jnp.transpose(
        table[8 : 8 + spread].reshape(spread, dp, block), (1, 0, 2)
    ).reshape(-1)
    bias_qkv = jnp.concatenate([bias_q, jnp.zeros_like(bias_q), bias_v])
    qkv = plus(mm(tokens, weight_qkv) + bias_qkv, order).astype(BF16)
    z_keys = [[(0, y, z, h) for z in range(4)] for y, h in ((0, 0), (1, 0), (0, 1), (1, 1))]

    def bag_of(blocks):
        cores = [flip(v, "core") for v, _ in blocks]
        return blocks + [(v, core_keys(keys)) for v, (_, keys) in zip(cores, blocks)]

    low_keys = [keys[:2] for keys in z_keys]
    high_keys = [keys[2:] for keys in z_keys]
    if grid.fast:
        order = after(grid, qkv, high_x, high_y, second_x)
        high_cross = flip(plus(high_x, order), "y")
        attention_order = [jnp.full((8, LANES), order, F32)]
    else:
        attention_order = []
    context, log_total = attention(qkv, spans, attention_order, length, H)
    if grid.fast:
        order = after(grid, context, high_cross, second_cross, third)
        third = grid.share(third, "xy", order)
        order = after(grid, context, high_cross)
        blocks = (second, second_y, second_x, second_cross)
        blocks = list(zip(blocks, low_keys)) + list(zip((high, high_y, high_x, high_cross), high_keys))
        weight_out, weight_up = join(bag_of(blocks), [width // 2, w_up.shape[1] // 2], 0, here)
        order = after(grid, weight_out)
    sum_one = tokens.astype(F32) + mm(context, weight_out) + bias_out
    unit_one, scale_one = norm_parts(sum_one)
    hidden = unit_one * gain_one + shift_one
    hidden_low = hidden.astype(BF16)
    pre = mm(hidden_low, weight_up) + bias_up
    phi, density = normal_parts(pre)
    gelu_low = (pre * phi).astype(BF16)
    slope = (phi + pre * density).astype(BF16)
    if grid.fast:
        order = after(grid, gelu_low, third)
        third = third.reshape((16,) + third.shape[2:])
        third_core = flip(third, "core")
        bag = [(third, square_keys(0)), (third_core, square_keys(1))]
        (weight_down,) = join(bag, [width // 2], 0, here, w_down.shape[0])
    sum_two = plus(hidden, order) + mm(gelu_low, weight_down) + bias_down
    unit_two, scale_two = norm_parts(sum_two)
    result = (unit_two * gain_two + shift_two).reshape(steps, count, length, width)
    output = result.astype(BF16)

    def starts(value):
        return value.reshape(total, length, -1)[:, 0]

    def put_starts(value, part):
        blocks = value.reshape(total, length, -1)
        return lax.dynamic_update_slice(blocks, part[:, None], (0, 0, 0)).reshape(value.shape)

    cls = jnp.moveaxis(output[:, :, 0, :], 0, 1).reshape(total, width)
    cls = jnp.concatenate([cls, digits], axis=1)
    if grid.fast:
        cls = grid.share(cls, "all")
        order = after(grid, output)
        left, right = [
            [v[:, at : at + total] for v in (third, third_core)]
            for at in (w_down.shape[0], w_down.shape[0] + total)
        ]
        near, far = [plus(jnp.concatenate(v, axis=2), order) for v in zip(left, right)]
        odd = dp_index % 2 == 1
        all_queries = jnp.stack([jnp.where(odd, far, near), jnp.where(odd, near, far)])
        all_queries = all_queries.reshape(2, 2, 2, 4, total, width)
        all_queries = jnp.transpose(all_queries, (3, 1, 0, 2, 4, 5))
    else:
        cls = lax.all_gather(cls, ("dp", "rep"), axis=0, tiled=True)
        all_queries = lax.all_gather(query_rows, ("dp", "rep"), axis=0, tiled=True)
    grad_out = out_grad.reshape(rows, width).astype(F32)
    grad_two = norm_back(grad_out, unit_two, scale_two, gain_two)
    down_low = grad_two.astype(BF16)
    later = (jnp.arange(rows) % length > 0)[:, None]
    grad_gain_two = jnp.sum(grad_out * unit_two, axis=0)
    grad_shift_two = jnp.sum(grad_out, axis=0)
    grad_b_down = jnp.sum(jnp.where(later, down_low.astype(F32), 0.0), axis=0)

    def up_back(grad, by):
        return (mm_back(grad, weight_down) * by.astype(F32)).astype(BF16)

    up_low = up_back(down_low, slope)
    order = after(grid, cls, up_low)

    cls = plus(cls.reshape(-1, steps, width + LANES), order)
    all_cls = cls[:, :, :width]
    all_queries = all_queries.reshape(-1, steps, width)
    digits = cls[:, :, width : width + 2].astype(jnp.int32)
    all_positives = digits[:, :, 0] * 256 + digits[:, :, 1]
    first = (dp_index * grid.rep + rep_index) * count
    logits = jnp.einsum("qmd,pmd->mqp", all_queries, all_cls, preferred_element_type=F32)
    logits = logits * inv_width
    query_total = jax.nn.logsumexp(logits, axis=-1)
    passages_all = all_cls.shape[0]
    mine = lax.dynamic_slice_in_dim(logits, first, count, axis=1)
    mine_total = lax.dynamic_slice_in_dim(query_total, first, count, axis=1)
    onehot = (positives[:, :, None] == jnp.arange(passages_all)[None, None, :]).astype(F32)
    query_loss = mine_total - jnp.sum(mine * onehot, axis=-1)
    mine_grad = (jnp.exp(mine - mine_total[:, :, None]) - onehot) * inv_width
    queries_grad = jnp.einsum(
        "mqp,pmd->mqd", mine_grad.astype(BF16), all_cls, preferred_element_type=F32
    )
    column = lax.dynamic_slice_in_dim(logits, first, count, axis=2)
    hit = (all_positives.T[:, :, None] == (first + jnp.arange(count))[None, None, :]).astype(F32)
    column_grad = (jnp.exp(column - query_total[:, :, None]) - hit) * inv_width
    cls_grad = jnp.einsum(
        "mqp,qmd->mpd", column_grad.astype(BF16), all_queries, preferred_element_type=F32
    )

    grad_start = cls_grad.reshape(total, width)
    unit_start = starts(unit_two)
    grad_gain_two = grad_gain_two + jnp.sum(grad_start * unit_start, axis=0)
    grad_shift_two = grad_shift_two + jnp.sum(grad_start, axis=0)
    grad_start = grad_start + starts(out_grad.reshape(rows, width)).astype(F32)
    grad_start = norm_back(grad_start, unit_start, starts(scale_two), gain_two)
    down_start = grad_start.astype(BF16)
    up_start = up_back(down_start, starts(slope))
    grad_b_down = grad_b_down + row_total(down_start)
    grad_two = put_starts(grad_two, grad_start)
    down_low = put_starts(down_low, down_start)
    up_low = put_starts(up_low, up_start)

    down_sum, up_sum, last_sum = [Scatter(grid, here) for _ in range(3)]
    down_sum.start([mm_left(gelu_low, down_low).astype(BF16)])
    order = after(grid, down_sum.held)
    down_sum.step(order)
    down_sum.step(deps=[up_low])
    order = down_sum.token
    grad_w_up = plus(mm_left(hidden_low, up_low), order).astype(BF16)
    up_sum.start([grad_w_up], down_sum.held)
    up_sum.step()
    down_sum.step(deps=[up_sum.far])
    order = down_sum.token
    half = w_up.shape[1] // 2
    grad_hidden = plus(grad_two + mm_back(up_low[:, :half], weight_up[:, :half]), order)
    up_sum.step(deps=[grad_hidden])
    order = up_sum.token
    grad_hidden = plus(grad_hidden + mm_back(up_low[:, half:], weight_up[:, half:]), order)
    grad_gain_one = jnp.sum(grad_hidden * unit_one, axis=0)
    grad_shift_one = jnp.sum(grad_hidden, axis=0)
    grad_one = norm_back(grad_hidden, unit_one, scale_one, gain_one)
    attn_low = grad_one.astype(BF16)
    grad_w_out = mm_left(context, attn_low).astype(BF16)
    context_grad = mm_back(attn_low, weight_out).astype(BF16)
    down_sum.step(deps=[up_sum.held, attn_low])
    up_sum.step(down_sum.token)
    order = up_sum.token
    qkv_low, grad_b_qkv = attention_back(
        qkv, context_grad, log_total, spans, [jnp.full((8, LANES), order, F32)], length, H
    )
    down_sum.step(deps=[up_sum.held, qkv_low])
    up_sum.step(down_sum.token)
    order = up_sum.token

    grad_w_qkv = plus(mm_left(tokens, qkv_low), order).astype(BF16)
    last_sum.start([grad_w_out, grad_w_qkv])
    last_sum.step()
    order = after(grid, last_sum.far)
    grad_b_query, grad_b_value = grad_b_qkv[0, :width], grad_b_qkv[0, 2 * width :]
    grad_b_out = row_total(attn_low, order)
    grad_b_up = row_total(up_low, order)
    grads = (
        grad_b_query,
        grad_b_value,
        grad_b_out,
        grad_gain_one,
        grad_shift_one,
        grad_b_down,
        grad_gain_two,
        grad_shift_two,
    )
    grads = jnp.concatenate([jnp.stack(grads), grad_b_up.reshape(spread, width)])

    grads = Total(grid, grads)
    up_sum.step(order)
    last_sum.step(deps=[grads.parts])
    order = last_sum.token
    grads.step(order)
    last_sum.step(deps=[grads.held])
    order = last_sum.token
    grads.step(order)
    input_grad = plus(grad_one + mm_back(qkv_low, weight_qkv), order)
    last_sum.step(deps=[input_grad, grads.held])
    order = last_sum.token
    grads.step(order)
    last_sum.step(deps=[input_grad, up_sum.held, grads.held])
    order = last_sum.token
    up_sum.step(order)
    down_sum.step(order)
    grads.step(order)
    (shard_w_down,) = down_sum.finish()
    (shard_w_up,) = up_sum.finish()
    shard_w_out, shard_w_qkv = last_sum.finish()
    shard_w_query, shard_w_key, shard_w_value = jnp.split(shard_w_qkv, 3, axis=1)
    grads = grads.finish()
    low = lax.dynamic_slice_in_dim(grads[:8], dp_index * block, block, axis=1)
    s_b_up = lax.dynamic_slice_in_dim(
        grads[8:].reshape(-1), dp_index * spread * block, spread * block, axis=0
    )
    (s_b_q, s_b_v, s_b_out, s_gain1, s_shift1, s_b_down, s_gain2, s_shift2) = [
        low[i] for i in range(8)
    ]
    return (
        output,
        query_loss,
        input_grad.reshape(steps, count, length, width),
        queries_grad,
        cls_grad,
        shard_w_query,
        s_b_q,
        shard_w_key,
        shard_w_value,
        s_b_v,
        shard_w_out,
        s_b_out,
        s_gain1,
        s_shift1,
        shard_w_up,
        s_b_up,
        shard_w_down,
        s_b_down,
        s_gain2,
        s_shift2,
    )


def solution(mesh):
    both = ("dp", "rep")
    matrix, vector = P("dp", None), P("dp")
    weights = (
        matrix, vector, matrix, matrix, vector, matrix, vector, vector, vector,
        matrix, vector, matrix, vector, vector, vector,
    )
    grid = Grid(mesh.shape["dp"], mesh.shape["rep"], 768 // mesh.shape["dp"])
    wide = P(None, both, None, None)
    return jax.shard_map(
        functools.partial(per_device, grid),
        mesh=mesh,
        in_specs=(wide, P(None, both), P(None, both, None), P(None, both), wide) + weights,
        out_specs=(wide, P(None, both), wide, P(None, both, None), P(None, both, None)) + weights,
        check_vma=False,
    )
```

```python
import functools
import math

import jax
import jax.numpy as jnp
from jax import lax
from jax.experimental import pallas as pl
from jax.experimental.pallas import tpu as pltpu
from jax.sharding import PartitionSpec as P

H = 12
F32 = jnp.float32
BF16 = jnp.bfloat16
INV_SQRT2 = 1.0 / math.sqrt(2.0)
INV_SQRT_2PI = 1.0 / math.sqrt(2.0 * math.pi)


ANY = pl.BlockSpec(memory_space=pl.ANY)
SMEM = pl.BlockSpec(memory_space=pltpu.SMEM)
VMEM = pl.BlockSpec(memory_space=pltpu.VMEM)
MIB = 2**20
LANES = 128


class Grid:
    def __init__(self, dp, rep, rows):
        self.dp, self.rep = dp, rep
        self.fast = dp == 16 and rep == 2 and rows % 16 == 0
        self.bits = {"core": 1, "y": 2, "z1": 4, "z2": 8, "z3": 12}

        place = [
            (((z * 2 + y) * 2 + c) * 2 + x, (z, y, c, x))
            for z in range(4)
            for y in range(2)
            for c in range(2)
            for x in range(2)
        ]
        lines, squares = {}, {}
        for i, (z, y, c, x) in place:
            lines.setdefault((y, c, x), []).append(i)
            squares.setdefault((z, c), []).append(i)
        self.groups = {"z": list(lines.values()), "xy": list(squares.values()), "all": None}

    def exchange(self, value, name):
        return lax.all_to_all(
            value, ("dp", "rep"), 0, 0, axis_index_groups=self.groups[name], tiled=True
        )

    def share(self, value, name, order=0.0):
        count = self.dp * self.rep if name == "all" else 4
        value = plus(jnp.broadcast_to(value[None], (count,) + value.shape), order)
        return self.exchange(value, name)

    def flip(self, value, name):
        if name == "x":
            return lax.ppermute(value, "rep", [(i, i ^ 1) for i in range(self.rep)])
        bit = self.bits[name]
        return lax.ppermute(value, "dp", [(i, i ^ bit) for i in range(self.dp)])


def run_copies(copies):
    for copy in copies:
        copy.start()
    for copy in copies:
        copy.wait()


def place_of(here_ref, key, rows):
    core, y, z, half = key[:4]
    if len(key) > 4:
        place = z * 4 + y * 2 + ((here_ref[0] & 1) ^ core)
        return pl.ds(pl.multiple_of(place * rows, 16), rows), half
    row = pl.multiple_of((here_ref[0] ^ (z * 4 + y * 2 + core)) * rows, 16)
    return pl.ds(row, rows), here_ref[1] ^ half


def square_keys(core):
    return [(core, y, z, x, True) for y in range(2) for x in range(2) for z in range(4)]


def join_kernel(here_ref, *refs, keys, widths, extra, rows):
    count = len(keys)
    pieces, outs, sems = refs[:count], refs[count:-1], refs[-1]
    copies = []
    for piece, names in zip(pieces, keys):
        for i, key in enumerate(names):
            where, half = place_of(here_ref, key, rows)
            at = 0
            for out, width in zip(outs, widths):
                column = half * width
                if len(key) == 4:
                    column = pl.multiple_of(column, LANES)
                column = pl.ds(column, width)
                source = piece.at[i, pl.ds(0, rows), pl.ds(at, width)]
                copies.append((source, out.at[where, column]))
                at += width
            if extra and key[3] == 0:
                copies.append((piece.at[i, :, pl.ds(at, extra)], outs[-1].at[where, :]))
    run_copies([pltpu.make_async_copy(a, b, sems.at[i]) for i, (a, b) in enumerate(copies)])


def join(bag, widths, extra, here, rows=None):
    arrays, keys = zip(*bag)
    rows = rows or arrays[0].shape[1]
    shapes = [(16 * rows, 2 * width) for width in widths] + ([(16 * rows, extra)] if extra else [])
    copies = 32 * len(widths) + (16 if extra else 0)
    size = sum(a * b for a, b in shapes)
    return pl.pallas_call(
        functools.partial(join_kernel, keys=keys, widths=widths, extra=extra, rows=rows),
        out_shape=[jax.ShapeDtypeStruct(shape, arrays[0].dtype) for shape in shapes],
        in_specs=[SMEM] + [ANY] * len(arrays),
        out_specs=[VMEM] * len(shapes),
        scratch_shapes=[pltpu.SemaphoreType.DMA((copies,))],
        compiler_params=pltpu.CompilerParams(vmem_limit_bytes=2 * MIB),
        cost_estimate=pl.CostEstimate(flops=0, bytes_accessed=4 * size, transcendentals=0),
        name="join",
    )(here, *arrays)


def split_kernel(here_ref, *refs, keys, count):
    values, pieces, sems = refs[:count], refs[-1 - len(keys) : -1], refs[-1]
    copies = []
    for piece, names in zip(pieces, keys):
        rows = piece.shape[1]
        for i, key in enumerate(names):
            where, half = place_of(here_ref, key, rows)
            at = 0
            for value in values:
                width = value.shape[1] // 2
                column = half * width
                if len(key) == 4:
                    column = pl.multiple_of(column, LANES)
                column = pl.ds(column, width)
                copies.append((value.at[where, column], piece.at[i, :, pl.ds(at, width)]))
                at += width
    run_copies([pltpu.make_async_copy(a, b, sems.at[i]) for i, (a, b) in enumerate(copies)])


def split(values, keys, here, deps):
    rows, width = values[0].shape[0] // 16, sum(v.shape[1] for v in values) // 2
    kind = values[0].dtype
    size = sum(v.size for v in values)
    return pl.pallas_call(
        functools.partial(split_kernel, keys=keys, count=len(values)),
        out_shape=[jax.ShapeDtypeStruct((len(names), rows, width), kind) for names in keys],
        in_specs=[SMEM] + [VMEM] * len(values) + [ANY] * len(deps),
        out_specs=[ANY] * len(keys),
        scratch_shapes=[pltpu.SemaphoreType.DMA((32 * len(values),))],
        compiler_params=pltpu.CompilerParams(vmem_limit_bytes=2 * MIB),
        cost_estimate=pl.CostEstimate(flops=0, bytes_accessed=4 * size, transcendentals=0),
        name="split",
    )(here, *values, *deps)


def order_kernel(*refs):
    refs[-1][0, 0] = 0.0


def after(grid, *trees):
    if not grid.fast:
        return 0.0
    leaves = jax.tree.leaves(trees)
    return pl.pallas_call(
        order_kernel,
        out_shape=jax.ShapeDtypeStruct((1, 1), F32),
        in_specs=[ANY] * len(leaves),
        out_specs=SMEM,
        compiler_params=pltpu.CompilerParams(vmem_limit_bytes=MIB // 4),
        name="order",
    )(*leaves).reshape(())


def halves_of(parts, extra, x):
    out = []
    for place in (x, 1 - x):
        row = [
            lax.dynamic_slice_in_dim(p, place * (p.shape[1] // 2), p.shape[1] // 2, axis=1)
            for p in parts
        ]
        out.append(jnp.concatenate(row + ([extra] if extra is not None else []), axis=1))
    return out


def core_keys(keys):
    return [(1,) + key[1:] for key in keys]


class Spread:
    def __init__(self, grid, value):
        self.grid, self.value = grid, value
        self.names = ["x", "core", "y", "z1", "z2"]
        self.other = None
        if not grid.fast:
            self.value = lax.all_gather(value, ("dp", "rep"), axis=0, tiled=True)
            self.names = []

    def absorb(self, order=0.0):
        if self.other is None:
            return
        name = self.names.pop(0)
        if name == "x":
            upper = lax.axis_index("rep") > 0
        else:
            upper = (lax.axis_index("dp") & self.grid.bits[name]) > 0
        low = jnp.where(upper, self.other, self.value)
        high = jnp.where(upper, self.value, self.other)
        self.value, self.other = jnp.concatenate([low, high], axis=0), None
        self.value = plus(self.value, order)

    def step(self, order=0.0):
        self.absorb(order)
        if self.names:
            self.other = self.grid.flip(self.value, self.names[0])
            self.held = [self.other]


class Total:
    def __init__(self, grid, value):
        self.grid, self.parts = grid, [value]
        self.names = ["x", "core", "y", "z1", "z2"]
        if not grid.fast:
            self.parts, self.names = [lax.psum(value, ("dp", "rep"))], []

    def step(self, order=0.0):
        value = sum(self.parts[1:], self.parts[0])
        self.parts = [plus(value, order)]
        if self.names:
            self.parts.append(self.grid.flip(self.parts[0], self.names.pop(0)))
        self.held = self.parts[1:]

    def finish(self):
        while self.names:
            self.step()
        return sum(self.parts[1:], self.parts[0])


def plus(value, order):
    return value if isinstance(order, float) else (value.astype(F32) + order).astype(value.dtype)


def sums_kernel(order_ref, *refs, plan):
    zero = order_ref[0, 0]
    refs[-1][0, 0] = zero
    for out_ref, terms in zip(refs[-1 - len(plan) : -1], plan):
        at = 0
        for size, parts in terms:
            for i in range(size):
                total = zero
                for source, first in parts:
                    total = total + refs[source][first + i].astype(F32)
                out_ref[at + i] = total.astype(out_ref.dtype)
            at += size


def sums(order, arrays, plan, deps):
    deps = jax.tree.leaves(deps)
    shapes = [(sum(size for size, _ in terms),) + arrays[0].shape[1:] for terms in plan]
    size = sum(a * b * c for a, b, c in shapes)
    return pl.pallas_call(
        functools.partial(sums_kernel, plan=plan),
        out_shape=[jax.ShapeDtypeStruct(shape, BF16) for shape in shapes]
        + [jax.ShapeDtypeStruct((1, 1), F32)],
        in_specs=[SMEM] + [VMEM] * len(arrays) + [ANY] * len(deps),
        out_specs=[VMEM] * len(shapes) + [SMEM],
        compiler_params=pltpu.CompilerParams(vmem_limit_bytes=8 * MIB),
        cost_estimate=pl.CostEstimate(flops=2 * size, bytes_accessed=6 * size, transcendentals=0),
        name="sums",
    )(jnp.reshape(jnp.asarray(order, F32), (1, 1)), *arrays, *deps)


class Scatter:
    def __init__(self, grid, here):
        self.grid, self.here, self.stage, self.held, self.sent = grid, here, 0, [], []
        self.far, self.token = [], 0.0

    def start(self, grads, deps=()):
        self.widths = [g.shape[1] for g in grads]
        if not self.grid.fast:
            parts = [
                lax.psum_scatter(g.astype(F32), "dp", scatter_dimension=0, tiled=True)
                for g in grads
            ]
            self.result = [lax.psum(p, "rep") for p in parts]
            return
        keys = [
            [(c, y, z, h) for y, h in ((1, 1), (0, 1), (1, 0), (0, 0)) for z in range(4)]
            for c in range(2)
        ]
        self.token = 0.0
        self.near, self.far = split(grads, keys, self.here, deps)
        self.held = [self.far]

    def step(self, order=0.0, deps=()):
        if not self.grid.fast:
            return
        flip = self.grid.flip
        self.stage += 1
        if self.stage == 1:
            self.held = [flip(self.far, "core")]
            return
        if self.stage == 2:
            plan = [[(n, [(0, at), (1, at)])] for n, at in ((2, 0), (2, 2), (4, 4), (4, 8), (4, 12))]
            low, high, self.x, self.y, self.own, token = sums(
                order, [self.near, *self.held], plan, deps
            )
            self.sent, self.held = [low, high], [flip(low, "x"), flip(high, "y")]
        elif self.stage == 3:
            plan = [[(2, [(0, 0)]), (2, [(0, 2), (3, 0)])], [(2, [(1, 0), (2, 0)]), (2, [(1, 2)])]]
            to_x, to_y, token = sums(order, [self.x, self.y, *self.held], plan, deps)
            self.sent, self.held = [to_x, to_y], [flip(to_x, "x"), flip(to_y, "y")]
        elif self.stage == 4:
            plan = [[(2, [(0, at), (1, at), (2, at)])] for at in (0, 2)]
            self.low, high, token = sums(order, [self.own, *self.held], plan, deps)
            self.sent, self.held = [high], [flip(high, "z2")]
        elif self.stage == 5:
            plan = [[(1, [(0, at), (1, at)])] for at in (0, 1)]
            self.low, high, token = sums(order, [self.low, *self.held], plan, deps)
            self.sent, self.held = [high], [flip(high, "z1")]
        elif self.stage == 6:
            plan = [[(1, [(0, 0), (1, 0)])]]
            self.low, token = sums(order, [self.low, *self.held], plan, deps)
            self.sent, self.held = [self.low], [flip(self.low, "x")]
        self.token = token.reshape(())

    def finish(self):
        if not self.grid.fast:
            return self.result
        while self.stage < 6:
            self.step()
        value, other = self.low[0], self.held[0][0]
        first = self.here[1] == 0
        left, right = jnp.where(first, value, other), jnp.where(first, other, value)
        out, at = [], 0
        for width in self.widths:
            cut = slice(at, at + width // 2)
            out.append(jnp.concatenate([left[:, cut], right[:, cut]], axis=1).astype(F32))
            at += width // 2
        return out


def mm(left, right):
    return jnp.dot(left, right, preferred_element_type=F32)


def mm_left(left, right):
    return lax.dot_general(left, right, (((0,), (0,)), ((), ())), preferred_element_type=F32)


def mm_back(left, right):
    return lax.dot_general(left, right, (((1,), (1,)), ((), ())), preferred_element_type=F32)


def row_total(values, order=0.0):
    return mm(plus(jnp.ones((8, values.shape[0]), BF16), order), values)[0]


def normal_parts(v):
    phi = 0.5 + 0.5 * lax.erf(v * INV_SQRT2)
    return phi, jnp.exp(-0.5 * v * v) * INV_SQRT_2PI


def norm_parts(v):
    mean_val = jnp.mean(v, axis=-1, keepdims=True)
    centred = v - mean_val
    variance = jnp.mean(centred * centred, axis=-1, keepdims=True)
    scale = lax.rsqrt(variance + 1e-05)
    return centred * scale, scale


def norm_back(grad, unit, scale, gain):
    inner = grad * gain
    mean_one = jnp.mean(inner, axis=-1, keepdims=True)
    mean_two = jnp.mean(inner * unit, axis=-1, keepdims=True)
    return (inner - mean_one - unit * mean_two) * scale


def two_heads(t, first):
    zero = jnp.zeros_like(t)
    return jnp.concatenate([jnp.where(first, t, zero), jnp.where(first, zero, t)], axis=0)

def attn_kernel(len_ref, qkv_ref, *refs, scale, n, pairs, many):
    c_ref, total_ref = refs[-2:]
    width = pairs * LANES
    q_ref, k_ref, v_ref = [qkv_ref.at[:, pl.ds(i * width, width)] for i in range(3)]
    lane = lax.broadcasted_iota(jnp.int32, (1, 2 * n), 1) % n
    first = lax.broadcasted_iota(jnp.int32, (n, LANES), 1) < LANES // 2
    spot = lax.broadcasted_iota(jnp.int32, (n, LANES), 1)
    for i in range(many):
        rows = slice(i * n, (i + 1) * n)
        length = len_ref[pl.program_id(0) * many + i]
        totals = jnp.zeros((n, LANES), F32)
        for pair in range(pairs):
            at = slice(pair * LANES, (pair + 1) * LANES)
            q = q_ref[rows, at] * scale
            s = mm_back(q, two_heads(k_ref[rows, at], first))
            s = jnp.where(lane < length, s, -1000000000.0)
            parts = []
            for h in range(2):
                part = s[:, h * n : (h + 1) * n]
                top = jnp.max(part, axis=-1, keepdims=True)
                part = jnp.exp(part - top)
                total = jnp.sum(part, axis=-1, keepdims=True)
                parts.append((part * (1.0 / total)).astype(BF16))
                totals = jnp.where(spot == 2 * pair + h, top + jnp.log(total), totals)
            p = jnp.concatenate(parts, axis=1)
            c_ref[rows, at] = mm(p, two_heads(v_ref[rows, at], first)).astype(BF16)
        total_ref[i] = totals.T[: total_ref.shape[1]]

def attention(qkv, lengths, deps, n, heads):
    rows, width = qkv.shape[0], qkv.shape[1] // 3
    count, many = rows // n, 2
    scale = 1.0 / math.sqrt(width // heads)
    block = pl.BlockSpec((n * many, width), lambda i: (i, 0))
    lines = 16
    return pl.pallas_call(
        functools.partial(attn_kernel, scale=scale, n=n, pairs=heads // 2, many=many),
        grid=(count // many,),
        in_specs=[SMEM, pl.BlockSpec((n * many, 3 * width), lambda i: (i, 0))] + [ANY] * len(deps),
        out_specs=[block, pl.BlockSpec((many, lines, n), lambda i: (i, 0, 0))],
        out_shape=[jax.ShapeDtypeStruct((rows, width), BF16), jax.ShapeDtypeStruct((count, lines, n), F32)],
        compiler_params=pltpu.CompilerParams(vmem_limit_bytes=16 * MIB),
        cost_estimate=pl.CostEstimate(flops=8 * rows * n * width, bytes_accessed=8 * rows * width, transcendentals=rows * n * heads),
        name="attention",
    )(lengths, qkv, *deps)

def attn_back_kernel(len_ref, total_ref, qkv_ref, d_ref, *refs, scale, n, pairs, many):
    width = pairs * LANES
    q_ref, k_ref, v_ref = [qkv_ref.at[:, pl.ds(i * width, width)] for i in range(3)]
    out_ref, total_out_ref = refs[-2:]
    dq_ref, dk_ref, dv_ref = [out_ref.at[:, pl.ds(i * width, width)] for i in range(3)]
    row = lax.broadcasted_iota(jnp.int32, (2 * n, n), 0) % n
    first = lax.broadcasted_iota(jnp.int32, (n, LANES), 1) < LANES // 2
    for i in range(many):
        rows = slice(i * n, (i + 1) * n)
        length = len_ref[pl.program_id(0) * many + i]
        valid = row < length
        for pair in range(pairs):
            at = slice(pair * LANES, (pair + 1) * LANES)
            q, k, v, d = q_ref[rows, at] * scale, k_ref[rows, at] * scale, v_ref[rows, at], d_ref[rows, at]
            kk = two_heads(k_ref[rows, at], first)
            s = jnp.where(valid, mm_back(kk, q), -1000000000.0)
            dp = mm_back(two_heads(v, first), d)
            ps, ds = [], []
            for h in range(2):
                part = slice(h * n, (h + 1) * n)
                p = jnp.exp(s[part] - total_ref[i, 2 * pair + h : 2 * pair + h + 1, :])
                t = p * dp[part]
                ds.append((t - p * jnp.sum(t, axis=0, keepdims=True)).astype(BF16))
                ps.append(p.astype(BF16))
            dv_ref[rows, at] = mm(jnp.concatenate(ps, axis=1), two_heads(d, first)).astype(BF16)
            dk_ref[rows, at] = mm(jnp.concatenate(ds, axis=1), two_heads(q, first)).astype(BF16)
            dq_ref[rows, at] = mm_left(jnp.concatenate(ds, axis=0), two_heads(k, first)).astype(BF16)
    term = jnp.sum(out_ref[...].astype(F32), axis=0, keepdims=True)

    @pl.when(pl.program_id(0) == 0)
    def _():
        total_out_ref[...] = term

    @pl.when(pl.program_id(0) > 0)
    def _():
        total_out_ref[...] += term


def attention_back(qkv, d, totals, lengths, deps, n, heads):
    rows, width = d.shape
    count, many = rows // n, 2
    scale = 1.0 / math.sqrt(width // heads)
    block = pl.BlockSpec((n * many, width), lambda i: (i, 0))
    wide = pl.BlockSpec((n * many, 3 * width), lambda i: (i, 0))
    return pl.pallas_call(
        functools.partial(attn_back_kernel, scale=scale, n=n, pairs=heads // 2, many=many),
        grid=(count // many,),
        in_specs=[SMEM, pl.BlockSpec((many,) + totals.shape[1:], lambda i: (i, 0, 0)), wide, block]
        + [ANY] * len(deps),
        out_specs=[wide, pl.BlockSpec((1, 3 * width), lambda i: (0, 0))],
        out_shape=[
            jax.ShapeDtypeStruct((rows, 3 * width), BF16),
            jax.ShapeDtypeStruct((1, 3 * width), F32),
        ],
        compiler_params=pltpu.CompilerParams(vmem_limit_bytes=16 * MIB),
        cost_estimate=pl.CostEstimate(flops=20 * rows * n * width, bytes_accessed=14 * rows * width, transcendentals=rows * n * heads),
        name="attention_back",
    )(lengths, totals, qkv, d, *deps)


def per_device(
    grid,
    passages,
    lengths,
    queries,
    positives,
    out_grad,
    w_query,
    b_query,
    w_key,
    w_value,
    b_value,
    w_out,
    b_out,
    norm1_gain,
    norm1_bias,
    w_up,
    b_up,
    w_down,
    b_down,
    norm2_gain,
    norm2_bias,
):
    steps, count, length, width = passages.shape
    total = steps * count
    rows = total * length
    inv_width = 1.0 / math.sqrt(width)
    dp = grid.dp
    dp_index, rep_index = lax.axis_index("dp"), lax.axis_index("rep")
    here = jnp.stack([dp_index, rep_index]).astype(jnp.int32)

    block = w_query.shape[0]
    vectors = (b_query, b_value, b_out, norm1_gain, norm1_bias, b_down, norm2_gain, norm2_bias)
    spread = b_up.shape[0] // block
    columns = [v[:, None] for v in vectors] + [b_up.reshape(spread, block).T]
    columns = jnp.concatenate(columns, axis=1)
    columns = jnp.pad(columns, ((0, 0), (0, LANES - columns.shape[1])))
    tokens = passages.reshape(rows, width)
    w_qkv = jnp.concatenate([w_query, w_key, w_value], axis=1)
    digits = jnp.stack([positives.T // 256, positives.T % 256], axis=-1).astype(BF16)
    query_rows = jnp.moveaxis(queries, 0, 1).reshape(total, width)
    digits = jnp.pad(digits.reshape(total, 2), ((0, 0), (0, LANES - 2)))
    spans = lengths.reshape(total)
    if grid.fast:
        flip = grid.flip
        mine, twin = halves_of((w_qkv,), columns, here[1])
        own, mine = jnp.stack([mine, twin]), mine[None]
        second = halves_of((w_out, w_up), None, here[1])[0][None]
        third = halves_of((w_down,), None, here[1])[0]
        third = jnp.concatenate([third, query_rows[:, : width // 2], query_rows[:, width // 2 :]])
        across, h1, h2, h3 = flip(own, "y"), flip(mine, "z1"), flip(mine, "z2"), flip(mine, "z3")
        s1 = flip(second, "z1")
        order = after(grid, across, h1, h2, h3)
        line = plus(jnp.concatenate([h1, h2, h3]), order)
        line_y, line_x = flip(line, "y"), flip(line, "x")
        second = plus(jnp.concatenate([second, s1]), order)
        second_far = flip(second, "z2")
        cores = [flip(own, "core"), flip(across, "core"), flip(line, "core")]
        order = after(grid, line_y, line_x, second)
        cross_x = flip(plus(line_y[:2], order), "x")
        cross_y = flip(plus(line_x[2:], order), "y")
        cores += [flip(line_y, "core"), flip(line_x, "core")]
        order = after(grid, cross_x, cross_y)
        second = plus(second, order)
        second_y, second_x = flip(second, "y"), flip(second, "x")
        cores += [flip(cross_x, "core"), flip(cross_y, "core")]
        bag = [
            (own, [(0, 0, 0, 0), (0, 0, 0, 1)]),
            (across, [(0, 1, 0, 0), (0, 1, 0, 1)]),
            (line, [(0, 0, z, 0) for z in (1, 2, 3)]),
            (line_y, [(0, 1, z, 0) for z in (1, 2, 3)]),
            (line_x, [(0, 0, z, 1) for z in (1, 2, 3)]),
            (cross_x, [(0, 1, z, 1) for z in (1, 2)]),
            (cross_y, [(0, 1, 3, 1)]),
        ]
        bag += [(v, core_keys(keys)) for v, (_, keys) in zip(cores, bag)]
        weight_qkv, table = join(bag, [3 * width // 2], LANES, here)
        order = after(grid, table)
        high = plus(second_far, order)
        high_y, high_x = flip(high, "y"), flip(high, "x")
        second_cross = flip(plus(second_y, order), "x")
        third = grid.share(third, "z", order)
    else:
        weight_qkv, table, weight_out, weight_up, weight_down = [
            lax.all_gather(w, "dp", axis=0, tiled=True)
            for w in (w_qkv, columns, w_out, w_up, w_down)
        ]
        order = 0.0
    table = table[:, :16].T.astype(F32)
    (bias_q, bias_v, bias_out, gain_one, shift_one, bias_down, gain_two, shift_two) = [
        table[i] for i in range(8)
    ]
    bias_up = jnp.transpose(
        table[8 : 8 + spread].reshape(spread, dp, block), (1, 0, 2)
    ).reshape(-1)
    bias_qkv = jnp.concatenate([bias_q, jnp.zeros_like(bias_q), bias_v])
    qkv = plus(mm(tokens, weight_qkv) + bias_qkv, order).astype(BF16)
    z_keys = [[(0, y, z, h) for z in range(4)] for y, h in ((0, 0), (1, 0), (0, 1), (1, 1))]

    def bag_of(blocks):
        cores = [flip(v, "core") for v, _ in blocks]
        return blocks + [(v, core_keys(keys)) for v, (_, keys) in zip(cores, blocks)]

    low_keys = [keys[:2] for keys in z_keys]
    high_keys = [keys[2:] for keys in z_keys]
    if grid.fast:
        order = after(grid, qkv, high_x, high_y, second_x)
        high_cross = flip(plus(high_x, order), "y")
        attention_order = [jnp.full((8, LANES), order, F32)]
    else:
        attention_order = []
    context, log_total = attention(qkv, spans, attention_order, length, H)
    if grid.fast:
        order = after(grid, context, high_cross, second_cross, third)
        third = grid.share(third, "xy", order)
        order = after(grid, context, high_cross)
        blocks = (second, second_y, second_x, second_cross)
        blocks = list(zip(blocks, low_keys)) + list(zip((high, high_y, high_x, high_cross), high_keys))
        weight_out, weight_up = join(bag_of(blocks), [width // 2, w_up.shape[1] // 2], 0, here)
        order = after(grid, weight_out)
    sum_one = tokens.astype(F32) + mm(context, weight_out) + bias_out
    unit_one, scale_one = norm_parts(sum_one)
    hidden = unit_one * gain_one + shift_one
    hidden_low = hidden.astype(BF16)
    pre = mm(hidden_low, weight_up) + bias_up
    phi, density = normal_parts(pre)
    gelu_low = (pre * phi).astype(BF16)
    slope = (phi + pre * density).astype(BF16)
    if grid.fast:
        order = after(grid, gelu_low, third)
        third = third.reshape((16,) + third.shape[2:])
        third_core = flip(third, "core")
        bag = [(third, square_keys(0)), (third_core, square_keys(1))]
        (weight_down,) = join(bag, [width // 2], 0, here, w_down.shape[0])
    sum_two = plus(hidden, order) + mm(gelu_low, weight_down) + bias_down
    unit_two, scale_two = norm_parts(sum_two)
    result = (unit_two * gain_two + shift_two).reshape(steps, count, length, width)
    output = result.astype(BF16)

    def starts(value):
        return value.reshape(total, length, -1)[:, 0]

    def put_starts(value, part):
        blocks = value.reshape(total, length, -1)
        return lax.dynamic_update_slice(blocks, part[:, None], (0, 0, 0)).reshape(value.shape)

    cls = jnp.moveaxis(output[:, :, 0, :], 0, 1).reshape(total, width)
    cls = jnp.concatenate([cls, digits], axis=1)
    if grid.fast:
        cls = grid.share(cls, "all")
        order = after(grid, output)
        left, right = [
            [v[:, at : at + total] for v in (third, third_core)]
            for at in (w_down.shape[0], w_down.shape[0] + total)
        ]
        near, far = [plus(jnp.concatenate(v, axis=2), order) for v in zip(left, right)]
        odd = dp_index % 2 == 1
        all_queries = jnp.stack([jnp.where(odd, far, near), jnp.where(odd, near, far)])
        all_queries = all_queries.reshape(2, 2, 2, 4, total, width)
        all_queries = jnp.transpose(all_queries, (3, 1, 0, 2, 4, 5))
    else:
        cls = lax.all_gather(cls, ("dp", "rep"), axis=0, tiled=True)
        all_queries = lax.all_gather(query_rows, ("dp", "rep"), axis=0, tiled=True)
    grad_out = plus(out_grad.reshape(rows, width).astype(F32), after(grid, output))
    grad_two = norm_back(grad_out, unit_two, scale_two, gain_two)
    down_low = grad_two.astype(BF16)
    later = (jnp.arange(rows) % length > 0)[:, None]
    grad_gain_two = jnp.sum(grad_out * unit_two, axis=0)
    grad_shift_two = jnp.sum(grad_out, axis=0)
    grad_b_down = jnp.sum(jnp.where(later, down_low.astype(F32), 0.0), axis=0)

    def up_back(grad, by):
        return (mm_back(grad, weight_down) * by.astype(F32)).astype(BF16)

    up_low = up_back(down_low, slope)
    order = after(grid, cls, up_low)

    cls = plus(cls.reshape(-1, steps, width + LANES), order)
    all_cls = cls[:, :, :width]
    all_queries = all_queries.reshape(-1, steps, width)
    digits = cls[:, :, width : width + 2].astype(jnp.int32)
    all_positives = digits[:, :, 0] * 256 + digits[:, :, 1]
    first = (dp_index * grid.rep + rep_index) * count
    logits = jnp.einsum("qmd,pmd->mqp", all_queries, all_cls, preferred_element_type=F32)
    logits = logits * inv_width
    query_total = jax.nn.logsumexp(logits, axis=-1)
    passages_all = all_cls.shape[0]
    mine = lax.dynamic_slice_in_dim(logits, first, count, axis=1)
    mine_total = lax.dynamic_slice_in_dim(query_total, first, count, axis=1)
    onehot = (positives[:, :, None] == jnp.arange(passages_all)[None, None, :]).astype(F32)
    query_loss = mine_total - jnp.sum(mine * onehot, axis=-1)
    mine_grad = (jnp.exp(mine - mine_total[:, :, None]) - onehot) * inv_width
    queries_grad = jnp.einsum(
        "mqp,pmd->mqd", mine_grad.astype(BF16), all_cls, preferred_element_type=F32
    )
    column = lax.dynamic_slice_in_dim(logits, first, count, axis=2)
    hit = (all_positives.T[:, :, None] == (first + jnp.arange(count))[None, None, :]).astype(F32)
    column_grad = (jnp.exp(column - query_total[:, :, None]) - hit) * inv_width
    cls_grad = jnp.einsum(
        "mqp,qmd->mpd", column_grad.astype(BF16), all_queries, preferred_element_type=F32
    )

    grad_start = cls_grad.reshape(total, width)
    unit_start = starts(unit_two)
    grad_gain_two = grad_gain_two + jnp.sum(grad_start * unit_start, axis=0)
    grad_shift_two = grad_shift_two + jnp.sum(grad_start, axis=0)
    grad_start = grad_start + starts(out_grad.reshape(rows, width)).astype(F32)
    grad_start = norm_back(grad_start, unit_start, starts(scale_two), gain_two)
    down_start = grad_start.astype(BF16)
    up_start = up_back(down_start, starts(slope))
    grad_b_down = grad_b_down + row_total(down_start)
    grad_two = put_starts(grad_two, grad_start)
    down_low = put_starts(down_low, down_start)
    up_low = put_starts(up_low, up_start)

    down_sum, up_sum, last_sum = [Scatter(grid, here) for _ in range(3)]
    down_sum.start([mm_left(gelu_low, down_low).astype(BF16)])
    order = after(grid, down_sum.held)
    down_sum.step(order)
    down_sum.step(deps=[up_low])
    order = down_sum.token
    grad_w_up = plus(mm_left(hidden_low, up_low), order).astype(BF16)
    up_sum.start([grad_w_up], down_sum.held)
    up_sum.step()
    down_sum.step(deps=[up_sum.far])
    order = down_sum.token
    half = w_up.shape[1] // 2
    grad_hidden = plus(grad_two + mm_back(up_low[:, :half], weight_up[:, :half]), order)
    up_sum.step(deps=[grad_hidden])
    order = up_sum.token
    grad_hidden = plus(grad_hidden + mm_back(up_low[:, half:], weight_up[:, half:]), order)
    grad_gain_one = jnp.sum(grad_hidden * unit_one, axis=0)
    grad_shift_one = jnp.sum(grad_hidden, axis=0)
    grad_one = norm_back(grad_hidden, unit_one, scale_one, gain_one)
    attn_low = grad_one.astype(BF16)
    grad_w_out = mm_left(context, attn_low).astype(BF16)
    context_grad = mm_back(attn_low, weight_out).astype(BF16)
    down_sum.step(deps=[up_sum.held, attn_low])
    up_sum.step(down_sum.token)
    order = up_sum.token
    qkv_low, grad_b_qkv = attention_back(
        qkv, context_grad, log_total, spans, [jnp.full((8, LANES), order, F32)], length, H
    )
    down_sum.step(deps=[up_sum.held, qkv_low])
    up_sum.step(down_sum.token)
    order = up_sum.token

    grad_w_qkv = plus(mm_left(tokens, qkv_low), order).astype(BF16)
    last_sum.start([grad_w_out, grad_w_qkv])
    last_sum.step()
    order = after(grid, last_sum.far)
    grad_b_query, grad_b_value = grad_b_qkv[0, :width], grad_b_qkv[0, 2 * width :]
    grad_b_out = row_total(attn_low, order)
    grad_b_up = row_total(up_low, order)
    grads = (
        grad_b_query,
        grad_b_value,
        grad_b_out,
        grad_gain_one,
        grad_shift_one,
        grad_b_down,
        grad_gain_two,
        grad_shift_two,
    )
    grads = jnp.concatenate([jnp.stack(grads), grad_b_up.reshape(spread, width)])

    grads = Total(grid, grads)
    up_sum.step(order)
    last_sum.step(deps=[grads.parts])
    order = last_sum.token
    grads.step(order)
    last_sum.step(deps=[grads.held])
    order = last_sum.token
    grads.step(order)
    input_grad = plus(grad_one + mm_back(qkv_low, weight_qkv), order)
    last_sum.step(deps=[input_grad, grads.held])
    order = last_sum.token
    grads.step(order)
    last_sum.step(deps=[input_grad, up_sum.held, grads.held])
    order = last_sum.token
    up_sum.step(order)
    down_sum.step(order)
    grads.step(order)
    (shard_w_down,) = down_sum.finish()
    (shard_w_up,) = up_sum.finish()
    shard_w_out, shard_w_qkv = last_sum.finish()
    shard_w_query, shard_w_key, shard_w_value = jnp.split(shard_w_qkv, 3, axis=1)
    grads = grads.finish()
    low = lax.dynamic_slice_in_dim(grads[:8], dp_index * block, block, axis=1)
    s_b_up = lax.dynamic_slice_in_dim(
        grads[8:].reshape(-1), dp_index * spread * block, spread * block, axis=0
    )
    (s_b_q, s_b_v, s_b_out, s_gain1, s_shift1, s_b_down, s_gain2, s_shift2) = [
        low[i] for i in range(8)
    ]
    return (
        output,
        query_loss,
        input_grad.reshape(steps, count, length, width),
        queries_grad,
        cls_grad,
        shard_w_query,
        s_b_q,
        shard_w_key,
        shard_w_value,
        s_b_v,
        shard_w_out,
        s_b_out,
        s_gain1,
        s_shift1,
        shard_w_up,
        s_b_up,
        shard_w_down,
        s_b_down,
        s_gain2,
        s_shift2,
    )


def solution(mesh):
    both = ("dp", "rep")
    matrix, vector = P("dp", None), P("dp")
    weights = (
        matrix, vector, matrix, matrix, vector, matrix, vector, vector, vector,
        matrix, vector, matrix, vector, vector, vector,
    )
    grid = Grid(mesh.shape["dp"], mesh.shape["rep"], 768 // mesh.shape["dp"])
    wide = P(None, both, None, None)
    return jax.shard_map(
        functools.partial(per_device, grid),
        mesh=mesh,
        in_specs=(wide, P(None, both), P(None, both, None), P(None, both), wide) + weights,
        out_specs=(wide, P(None, both), wide, P(None, both, None), P(None, both, None)) + weights,
        check_vma=False,
    )
```
